32 devices in a mesh: grp: 2 (over x), vel: 16 (over z, y, core).
Axes of the slice: x: 2, y: 2, z: 4, core: 2. Of those that a mesh axis runs over, the one named last changes fastest.
Arguments:
- discrete_lattice_vectors: float32 [3, 2048], P(None, 'vel'), may hold values from -7.5 to 7.5, as said below
- initial_compactness: float32 [16384], P('grp'), parts along dimension 0, may hold values from 0.5 to 2
- initial_flow_vector: float32 [3, 16384], P(None, 'grp'), parts along dimension 1, may hold values from -3 to 3
- initial_thermal_level: float32 [16384], P('grp'), parts along dimension 0, may hold values from 0.6 to 1.5
- initial_deviation: float32 [2048, 16384], P('vel', 'grp'), parts along dimension 1, may hold values from -0.5 to 0.5
Outputs:
- distribution: float32 [2048, 16384], P('vel', 'grp'), parts along dimension 1
- macro_profile: float32 [8, 16384], P(None, 'grp'), parts along dimension 1
The draws below stay inside these ranges and needn't reach their ends.
There are 2 independent parts, one for each index of `grp`. The reference program is written for one: setup_inputs(seed, part) draws one part's arguments, and reference() takes and returns one part's arrays. A program takes and returns all parts, laid end to end along the dimension named above; an argument that names none is the same for every part. Nothing has to cross between parts.
Inputs may be any that keep to these rules, and one draw needn't show every extreme that they name: `discrete_lattice_vectors`: velocity components, drawn independently with a spread of about 1.5.
All inputs are finite; a program needn't handle non-finite values.
Results may differ from the reference program's by a relative error of at most 0.0003.
Values sent between devices are 32-bit elements; how exact they have to be, the bound alone decides.
No kernel may reach another device: no remote copies, remote signals or barrier semaphores. Data moves between devices by JAX's collectives and lax.ppermute only.
A program may use at most 128 MiB of HBM per device.

```python
import math
import jax
import jax.numpy as jnp
from jax import lax

MESH_LENGTH = 8192
ITERS = 2
VELOCITIES = 2048


def draw_discrete_lattice_vectors(key, part):
    key = jax.random.fold_in(key, 11)
    values = jax.random.normal(key, (3, VELOCITIES), jnp.float32) * 1.5
    return jnp.clip(values, -7.5, 7.5)


def block_scale(stream_key, dims, cuts, least, high):
    factor_of = 1.0
    for position, parts in cuts:
        steps = jax.random.uniform(jax.random.fold_in(jax.random.fold_in(stream_key, 6), position), (parts,), jnp.float32, least / len(cuts), high / len(cuts))
        factor_of = factor_of * jnp.repeat(jnp.exp(steps), dims[position] // parts).reshape((-1,) + (1,) * (len(dims) - 1 - position))
    return factor_of


def scatter_about(stream_key, dims, width, most, kind=jnp.bfloat16):
    return jnp.clip(width * jax.random.normal(stream_key, dims, jnp.float32), -most, most).astype(kind)


def setup_inputs(seed: int = 0, part: int = 0) -> dict:
    splits = jax.random.split(jax.random.key(seed), 6)
    own_keys = jax.random.split(jax.random.fold_in(splits[5], part), 6)
    discrete_lattice_vectors = draw_discrete_lattice_vectors(jax.random.fold_in(splits[5], 71), part)
    initial_compactness = jnp.clip(jax.random.uniform(own_keys[1], (MESH_LENGTH,), jnp.float32, 0.5, 2.0), 0.5, 2.0)
    initial_flow_vector = scatter_about(own_keys[2], (3, MESH_LENGTH), 0.3, 3.0, jnp.float32)
    initial_thermal_level = jnp.clip(jax.random.uniform(own_keys[3], (MESH_LENGTH,), jnp.float32, 0.6, 1.5), 0.6, 1.5)
    initial_deviation = jnp.clip(jax.random.uniform(own_keys[4], (VELOCITIES, MESH_LENGTH), jnp.float32, -0.5, 0.5) * block_scale(own_keys[4], (VELOCITIES, MESH_LENGTH), ((0, 16),), -0.4, 0.0), -0.5, 0.5)
    return {"discrete_lattice_vectors": discrete_lattice_vectors, "initial_compactness": initial_compactness, "initial_flow_vector": initial_flow_vector, "initial_thermal_level": initial_thermal_level, "initial_deviation": initial_deviation}


ADIABATIC_INDEX = 5.0 / 3.0
CONDUCTIVE_SHARE = 2.0 / 3.0
SHEAR_EXPONENT = 0.81
SHEAR_REFERENCE = 0.05
KINETIC_STEP = 0.05
COURANT = 0.4
SPREAD_SCALE = 1.5

def quad_weights(discrete_lattice_vectors, total_count):
    magnitude_sq = lax.optimization_barrier(jnp.sum(discrete_lattice_vectors * discrete_lattice_vectors, axis=0))
    return SPREAD_SCALE ** 3 * jnp.exp(magnitude_sq / (2.0 * SPREAD_SCALE ** 2)) / total_count

def moment_basis(discrete_lattice_vectors):
    along_x, along_y, along_z = (discrete_lattice_vectors[0], discrete_lattice_vectors[1], discrete_lattice_vectors[2])
    magnitude_sq = along_x * along_x + along_y * along_y + along_z * along_z
    return jnp.stack([jnp.ones_like(along_x), along_x, along_y, along_z, magnitude_sq, along_x * along_x, along_x * along_y, along_x * along_z, along_y * along_y, along_y * along_z, along_x * magnitude_sq, along_y * magnitude_sq, along_z * magnitude_sq])

def equilibrium(discrete_lattice_vectors, macro_profile):
    inertial_amount = macro_profile[0]
    mean_flow_vector = macro_profile[1:4]
    thermal_level = macro_profile[4]
    boltzmann_thermal_current = macro_profile[5:8]
    peculiar = discrete_lattice_vectors[:, :, None] - mean_flow_vector[:, None, :]
    magnitude_sq = lax.optimization_barrier(jnp.sum(peculiar * peculiar, axis=0))
    gaussian_equilibrium = inertial_amount * thermal_level ** (-1.5) * jnp.exp(-magnitude_sq / (2.0 * thermal_level))
    thermal_current_factor = lax.optimization_barrier(jnp.sum(peculiar * boltzmann_thermal_current[:, None, :], axis=0))
    fluid_stress_scalar = inertial_amount * thermal_level
    return gaussian_equilibrium * (1.0 + (1.0 - CONDUCTIVE_SHARE) * thermal_current_factor * (magnitude_sq / thermal_level - 5.0) / (5.0 * fluid_stress_scalar * thermal_level))

def kinetic_update(distribution, discrete_lattice_vectors, macro_profile):
    target = equilibrium(discrete_lattice_vectors, macro_profile)
    inertial_amount = macro_profile[0]
    thermal_level = macro_profile[4]
    collision_interval = SHEAR_REFERENCE * thermal_level ** SHEAR_EXPONENT / (inertial_amount * thermal_level)
    relax_ratio = KINETIC_STEP / collision_interval
    left_diff = distribution - jnp.roll(distribution, 1, axis=1)
    right_diff = jnp.roll(distribution, -1, axis=1) - distribution
    slope = jnp.where(left_diff * right_diff > 0, jnp.sign(left_diff) * jnp.minimum(jnp.abs(left_diff), jnp.abs(right_diff)), 0.0)
    upwind_plus = distribution + 0.5 * slope
    upwind_minus = jnp.roll(distribution - 0.5 * slope, -1, axis=1)
    stream = discrete_lattice_vectors[0][:, None]
    face_flux = stream * jnp.where(stream > 0, upwind_plus, upwind_minus)
    divergence = face_flux - jnp.roll(face_flux, 1, axis=1)
    return (distribution - KINETIC_STEP * divergence + relax_ratio * target) / (1.0 + relax_ratio)

def kinetic_fields(integral_averages):
    inertial_amount = integral_averages[0]
    momentum = integral_averages[1:4]
    mean_flow_vector = momentum / inertial_amount
    mean_flow_norm_sq = lax.optimization_barrier(jnp.sum(mean_flow_vector * mean_flow_vector, axis=0))
    thermal_level = (integral_averages[4] - inertial_amount * mean_flow_norm_sq) / (3.0 * inertial_amount)
    fluid_stress_scalar = inertial_amount * thermal_level
    quadratic_average = [[integral_averages[5], integral_averages[6], integral_averages[7]], [integral_averages[6], integral_averages[8], integral_averages[9]], [integral_averages[7], integral_averages[9], integral_averages[4] - integral_averages[5] - integral_averages[8]]]
    stress_xx = integral_averages[5] - inertial_amount * mean_flow_vector[0] * mean_flow_vector[0] - fluid_stress_scalar
    stress_xy = integral_averages[6] - inertial_amount * mean_flow_vector[0] * mean_flow_vector[1]
    stress_xz = integral_averages[7] - inertial_amount * mean_flow_vector[0] * mean_flow_vector[2]
    heat_rows = []
    for index in range(3):
        contraction = quadratic_average[index][0] * mean_flow_vector[0] + quadratic_average[index][1] * mean_flow_vector[1] + quadratic_average[index][2] * mean_flow_vector[2]
        heat_rows.append(0.5 * (integral_averages[10 + index] - mean_flow_vector[index] * integral_averages[4] - 2.0 * contraction + 2.0 * inertial_amount * mean_flow_vector[index] * mean_flow_norm_sq))
    boltzmann_thermal_current = jnp.stack(heat_rows)
    invariant_quantities = jnp.concatenate([inertial_amount[None], momentum, 0.5 * integral_averages[4][None]])
    kinetic_terms = jnp.stack([stress_xx, stress_xy, stress_xz, boltzmann_thermal_current[0]])
    return (invariant_quantities, kinetic_terms, boltzmann_thermal_current)

def physical_quantities(invariant_quantities):
    inertial_amount = invariant_quantities[0]
    mean_flow_vector = invariant_quantities[1:4] / inertial_amount
    thermal_level = (2.0 * invariant_quantities[4] / inertial_amount - lax.optimization_barrier(jnp.sum(mean_flow_vector * mean_flow_vector, axis=0))) / 3.0
    return (inertial_amount, mean_flow_vector, thermal_level, inertial_amount * thermal_level)

def ns_sweep(extended_profile, closure_corrections, reduce_max):
    inertial_amount, mean_flow_vector, thermal_level, fluid_stress_scalar = physical_quantities(extended_profile)
    particle_rates = jnp.abs(mean_flow_vector[0, 1:-1]) + jnp.sqrt(ADIABATIC_INDEX * thermal_level[1:-1])
    signal = reduce_max(jnp.max(particle_rates))
    time_step = COURANT / signal
    euler = jnp.stack([inertial_amount * mean_flow_vector[0], inertial_amount * mean_flow_vector[0] * mean_flow_vector[0] + fluid_stress_scalar, inertial_amount * mean_flow_vector[0] * mean_flow_vector[1], inertial_amount * mean_flow_vector[0] * mean_flow_vector[2], (extended_profile[4] + fluid_stress_scalar) * mean_flow_vector[0]])
    shear_coefficient = SHEAR_REFERENCE * thermal_level ** SHEAR_EXPONENT
    interface_shear = 0.5 * (shear_coefficient[:-1] + shear_coefficient[1:])
    flow_diff = mean_flow_vector[:, 1:] - mean_flow_vector[:, :-1]
    thermal_contrast = thermal_level[1:] - thermal_level[:-1]
    face_flow = 0.5 * (mean_flow_vector[:, :-1] + mean_flow_vector[:, 1:])
    interface_correction = 0.5 * (closure_corrections[:, :-1] + closure_corrections[:, 1:])
    stress_xx = -(4.0 / 3.0) * interface_shear * flow_diff[0] + interface_correction[0]
    stress_xy = -interface_shear * flow_diff[1] + interface_correction[1]
    stress_xz = -interface_shear * flow_diff[2] + interface_correction[2]
    thermal_current_axial = -3.75 * interface_shear * thermal_contrast + interface_correction[3]
    viscous = jnp.stack([jnp.zeros_like(stress_xx), stress_xx, stress_xy, stress_xz, stress_xx * face_flow[0] + stress_xy * face_flow[1] + stress_xz * face_flow[2] + thermal_current_axial])
    face_total = 0.5 * (euler[:, :-1] + euler[:, 1:]) - 0.5 * signal * (extended_profile[:, 1:] - extended_profile[:, :-1]) + viscous
    return extended_profile[:, 1:-1] - time_step * (face_total[:, 1:] - face_total[:, :-1])

def ns_solve(integral_averages, pad_deep, pad_thin, reduce_max):
    invariant_quantities, kinetic_terms, boltzmann_thermal_current = kinetic_fields(integral_averages)
    extended_profile = pad_deep(jnp.concatenate([invariant_quantities, kinetic_terms]))
    extended_invariants = extended_profile[:5]
    extended_corrections = extended_profile[5:]
    inertial_amount, mean_flow_vector, thermal_level, fluid_stress_scalar = physical_quantities(extended_invariants)
    shear_coefficient = SHEAR_REFERENCE * thermal_level[1:-1] ** SHEAR_EXPONENT
    closure_corrections = jnp.stack([extended_corrections[0, 1:-1] + 4.0 / 3.0 * shear_coefficient * (mean_flow_vector[0, 2:] - mean_flow_vector[0, :-2]) * 0.5, extended_corrections[1, 1:-1] + shear_coefficient * (mean_flow_vector[1, 2:] - mean_flow_vector[1, :-2]) * 0.5, extended_corrections[2, 1:-1] + shear_coefficient * (mean_flow_vector[2, 2:] - mean_flow_vector[2, :-2]) * 0.5, extended_corrections[3, 1:-1] + 3.75 * shear_coefficient * (thermal_level[2:] - thermal_level[:-2]) * 0.5])
    first = ns_sweep(extended_invariants[:, 1:-1], closure_corrections, reduce_max)
    quadratic_average = ns_sweep(pad_thin(first), closure_corrections, reduce_max)
    inertial_amount, mean_flow_vector, thermal_level, fluid_stress_scalar = physical_quantities(quadratic_average)
    return jnp.concatenate([inertial_amount[None], mean_flow_vector, thermal_level[None], boltzmann_thermal_current])

def wrap_deep(values):
    return jnp.concatenate([values[:, -2:], values, values[:, :2]], axis=1)

def wrap_thin(values):
    return jnp.concatenate([values[:, -1:], values, values[:, :1]], axis=1)

def keep_max(value):
    return value

def reference(discrete_lattice_vectors, initial_compactness, initial_flow_vector, initial_thermal_level, initial_deviation):
    weights = quad_weights(discrete_lattice_vectors, VELOCITIES)
    weighted_basis = moment_basis(discrete_lattice_vectors) * weights[None, :]
    macro_profile = jnp.concatenate([initial_compactness[None], initial_flow_vector, initial_thermal_level[None], jnp.zeros((3, MESH_LENGTH), jnp.float32)])
    block_rows = math.gcd(VELOCITIES, 512)
    blocks = VELOCITIES // block_rows
    vel_blocks = discrete_lattice_vectors.reshape(3, blocks, block_rows).transpose(1, 0, 2)
    pert_blocks = initial_deviation.reshape(blocks, block_rows, MESH_LENGTH)
    start_fields = macro_profile
    distribution = lax.map(lambda item: equilibrium(item[0], start_fields) * (1.0 + item[1]), (vel_blocks, pert_blocks))
    for iteration in range(ITERS):
        integral_averages = jnp.dot(weighted_basis, distribution.reshape(VELOCITIES, MESH_LENGTH), precision=lax.Precision.HIGHEST)
        macro_profile = ns_solve(integral_averages, wrap_deep, wrap_thin, keep_max)
        now_fields = macro_profile
        distribution = lax.map(lambda item: kinetic_update(item[1], item[0], now_fields), (vel_blocks, distribution))
    return (distribution.reshape(VELOCITIES, MESH_LENGTH), macro_profile)
```

```python
import jax
import jax.numpy as jnp
from jax import lax
from jax.sharding import PartitionSpec as P

ITERS = 2


ADIABATIC_INDEX = 5.0 / 3.0
CONDUCTIVE_SHARE = 2.0 / 3.0
SHEAR_EXPONENT = 0.81
SHEAR_REFERENCE = 0.05
KINETIC_STEP = 0.05
COURANT = 0.4
SPREAD_SCALE = 1.5


def quad_weights(discrete_lattice_vectors, total_count):
    magnitude_sq = jnp.sum(discrete_lattice_vectors * discrete_lattice_vectors, axis=0)
    return SPREAD_SCALE**3 * jnp.exp(magnitude_sq / (2.0 * SPREAD_SCALE**2)) / total_count


def moment_basis(discrete_lattice_vectors):
    along_x, along_y, along_z = (
        discrete_lattice_vectors[0],
        discrete_lattice_vectors[1],
        discrete_lattice_vectors[2],
    )
    magnitude_sq = along_x * along_x + along_y * along_y + along_z * along_z
    return jnp.stack(
        [
            jnp.ones_like(along_x),
            along_x,
            along_y,
            along_z,
            magnitude_sq,
            along_x * along_x,
            along_x * along_y,
            along_x * along_z,
            along_y * along_y,
            along_y * along_z,
            along_x * magnitude_sq,
            along_y * magnitude_sq,
            along_z * magnitude_sq,
        ]
    )


def equilibrium(discrete_lattice_vectors, macro_profile):
    inertial_amount = macro_profile[0]
    mean_flow_vector = macro_profile[1:4]
    thermal_level = macro_profile[4]
    boltzmann_thermal_current = macro_profile[5:8]
    peculiar = discrete_lattice_vectors[:, :, None] - mean_flow_vector[:, None, :]
    magnitude_sq = jnp.sum(peculiar * peculiar, axis=0)
    gaussian_equilibrium = (
        inertial_amount * thermal_level ** (-1.5) * jnp.exp(-magnitude_sq / (2.0 * thermal_level))
    )
    thermal_current_factor = jnp.sum(peculiar * boltzmann_thermal_current[:, None, :], axis=0)
    fluid_stress_scalar = inertial_amount * thermal_level
    return gaussian_equilibrium * (
        1.0
        + (1.0 - CONDUCTIVE_SHARE)
        * thermal_current_factor
        * (magnitude_sq / thermal_level - 5.0)
        / (5.0 * fluid_stress_scalar * thermal_level)
    )


def kinetic_update(distribution, discrete_lattice_vectors, macro_profile):
    target = equilibrium(discrete_lattice_vectors, macro_profile)
    inertial_amount = macro_profile[0]
    thermal_level = macro_profile[4]
    collision_interval = (
        SHEAR_REFERENCE * thermal_level**SHEAR_EXPONENT / (inertial_amount * thermal_level)
    )
    relax_ratio = KINETIC_STEP / collision_interval
    left_diff = distribution - jnp.roll(distribution, 1, axis=1)
    right_diff = jnp.roll(distribution, -1, axis=1) - distribution
    slope = jnp.where(
        left_diff * right_diff > 0,
        jnp.sign(left_diff) * jnp.minimum(jnp.abs(left_diff), jnp.abs(right_diff)),
        0.0,
    )
    upwind_plus = distribution + 0.5 * slope
    upwind_minus = jnp.roll(distribution - 0.5 * slope, -1, axis=1)
    stream = discrete_lattice_vectors[0][:, None]
    face_flux = stream * jnp.where(stream > 0, upwind_plus, upwind_minus)
    divergence = face_flux - jnp.roll(face_flux, 1, axis=1)
    return (distribution - KINETIC_STEP * divergence + relax_ratio * target) / (1.0 + relax_ratio)


def kinetic_fields(integral_averages):
    inertial_amount = integral_averages[0]
    momentum = integral_averages[1:4]
    mean_flow_vector = momentum / inertial_amount
    mean_flow_norm_sq = jnp.sum(mean_flow_vector * mean_flow_vector, axis=0)
    thermal_level = (integral_averages[4] - inertial_amount * mean_flow_norm_sq) / (
        3.0 * inertial_amount
    )
    fluid_stress_scalar = inertial_amount * thermal_level
    quadratic_average = [
        [integral_averages[5], integral_averages[6], integral_averages[7]],
        [integral_averages[6], integral_averages[8], integral_averages[9]],
        [
            integral_averages[7],
            integral_averages[9],
            integral_averages[4] - integral_averages[5] - integral_averages[8],
        ],
    ]
    stress_xx = (
        integral_averages[5]
        - inertial_amount * mean_flow_vector[0] * mean_flow_vector[0]
        - fluid_stress_scalar
    )
    stress_xy = integral_averages[6] - inertial_amount * mean_flow_vector[0] * mean_flow_vector[1]
    stress_xz = integral_averages[7] - inertial_amount * mean_flow_vector[0] * mean_flow_vector[2]
    heat_rows = []
    for index in range(3):
        contraction = (
            quadratic_average[index][0] * mean_flow_vector[0]
            + quadratic_average[index][1] * mean_flow_vector[1]
            + quadratic_average[index][2] * mean_flow_vector[2]
        )
        heat_rows.append(
            0.5
            * (
                integral_averages[10 + index]
                - mean_flow_vector[index] * integral_averages[4]
                - 2.0 * contraction
                + 2.0 * inertial_amount * mean_flow_vector[index] * mean_flow_norm_sq
            )
        )
    boltzmann_thermal_current = jnp.stack(heat_rows)
    invariant_quantities = jnp.concatenate(
        [inertial_amount[None], momentum, 0.5 * integral_averages[4][None]]
    )
    kinetic_terms = jnp.stack([stress_xx, stress_xy, stress_xz, boltzmann_thermal_current[0]])
    return (invariant_quantities, kinetic_terms, boltzmann_thermal_current)


def physical_quantities(invariant_quantities):
    inertial_amount = invariant_quantities[0]
    mean_flow_vector = invariant_quantities[1:4] / inertial_amount
    thermal_level = (
        2.0 * invariant_quantities[4] / inertial_amount
        - jnp.sum(mean_flow_vector * mean_flow_vector, axis=0)
    ) / 3.0
    return (inertial_amount, mean_flow_vector, thermal_level, inertial_amount * thermal_level)


def ns_sweep(extended_profile, closure_corrections, reduce_max):
    inertial_amount, mean_flow_vector, thermal_level, fluid_stress_scalar = physical_quantities(
        extended_profile
    )
    particle_rates = jnp.abs(mean_flow_vector[0, 1:-1]) + jnp.sqrt(
        ADIABATIC_INDEX * thermal_level[1:-1]
    )
    signal = reduce_max(jnp.max(particle_rates))
    time_step = COURANT / signal
    euler = jnp.stack(
        [
            inertial_amount * mean_flow_vector[0],
            inertial_amount * mean_flow_vector[0] * mean_flow_vector[0] + fluid_stress_scalar,
            inertial_amount * mean_flow_vector[0] * mean_flow_vector[1],
            inertial_amount * mean_flow_vector[0] * mean_flow_vector[2],
            (extended_profile[4] + fluid_stress_scalar) * mean_flow_vector[0],
        ]
    )
    shear_coefficient = SHEAR_REFERENCE * thermal_level**SHEAR_EXPONENT
    interface_shear = 0.5 * (shear_coefficient[:-1] + shear_coefficient[1:])
    flow_diff = mean_flow_vector[:, 1:] - mean_flow_vector[:, :-1]
    thermal_contrast = thermal_level[1:] - thermal_level[:-1]
    face_flow = 0.5 * (mean_flow_vector[:, :-1] + mean_flow_vector[:, 1:])
    interface_correction = 0.5 * (closure_corrections[:, :-1] + closure_corrections[:, 1:])
    stress_xx = -(4.0 / 3.0) * interface_shear * flow_diff[0] + interface_correction[0]
    stress_xy = -interface_shear * flow_diff[1] + interface_correction[1]
    stress_xz = -interface_shear * flow_diff[2] + interface_correction[2]
    thermal_current_axial = -3.75 * interface_shear * thermal_contrast + interface_correction[3]
    viscous = jnp.stack(
        [
            jnp.zeros_like(stress_xx),
            stress_xx,
            stress_xy,
            stress_xz,
            stress_xx * face_flow[0]
            + stress_xy * face_flow[1]
            + stress_xz * face_flow[2]
            + thermal_current_axial,
        ]
    )
    face_total = (
        0.5 * (euler[:, :-1] + euler[:, 1:])
        - 0.5 * signal * (extended_profile[:, 1:] - extended_profile[:, :-1])
        + viscous
    )
    return extended_profile[:, 1:-1] - time_step * (face_total[:, 1:] - face_total[:, :-1])


def ns_solve(integral_averages, pad_deep, pad_thin, reduce_max):
    invariant_quantities, kinetic_terms, boltzmann_thermal_current = kinetic_fields(
        integral_averages
    )
    extended_profile = pad_deep(jnp.concatenate([invariant_quantities, kinetic_terms]))
    extended_invariants = extended_profile[:5]
    extended_corrections = extended_profile[5:]
    inertial_amount, mean_flow_vector, thermal_level, fluid_stress_scalar = physical_quantities(
        extended_invariants
    )
    shear_coefficient = SHEAR_REFERENCE * thermal_level[1:-1] ** SHEAR_EXPONENT
    closure_corrections = jnp.stack(
        [
            extended_corrections[0, 1:-1]
            + 4.0
            / 3.0
            * shear_coefficient
            * (mean_flow_vector[0, 2:] - mean_flow_vector[0, :-2])
            * 0.5,
            extended_corrections[1, 1:-1]
            + shear_coefficient * (mean_flow_vector[1, 2:] - mean_flow_vector[1, :-2]) * 0.5,
            extended_corrections[2, 1:-1]
            + shear_coefficient * (mean_flow_vector[2, 2:] - mean_flow_vector[2, :-2]) * 0.5,
            extended_corrections[3, 1:-1]
            + 3.75 * shear_coefficient * (thermal_level[2:] - thermal_level[:-2]) * 0.5,
        ]
    )
    first = ns_sweep(extended_invariants[:, 1:-1], closure_corrections, reduce_max)
    quadratic_average = ns_sweep(pad_thin(first), closure_corrections, reduce_max)
    inertial_amount, mean_flow_vector, thermal_level, fluid_stress_scalar = physical_quantities(
        quadratic_average
    )
    return jnp.concatenate(
        [inertial_amount[None], mean_flow_vector, thermal_level[None], boltzmann_thermal_current]
    )


def wrap_deep(values):
    return jnp.concatenate([values[:, -2:], values, values[:, :2]], axis=1)


def wrap_thin(values):
    return jnp.concatenate([values[:, -1:], values, values[:, :1]], axis=1)


def keep_max(value):
    return value


def stages(count):
    sizes = []
    for size in (2, 2):
        if count % size == 0 and count > 1:
            sizes.append(size)
            count //= size
    while count % 4 == 0:
        sizes.append(4)
        count //= 4
    while count % 2 == 0:
        sizes.append(2)
        count //= 2
    if count > 1:
        sizes.append(count)
    return sizes


def pairs(count, stride, size, shift):
    out = []
    for device in range(count):
        rank = device // stride % size
        other = (rank ^ shift) if size & (size - 1) == 0 else (shift - rank) % size
        out.append((device, device + (other - rank) * stride))
    return out


def staged_sum(values, count):
    index = lax.axis_index("vel")
    stride, trail = 1, []
    block = values
    for size in stages(count):
        rank = index // stride % size
        width = block.shape[1] // size
        total = lax.dynamic_slice_in_dim(block, rank * width, width, 1)
        for shift in range(1, size):
            other = rank ^ shift
            piece = lax.dynamic_slice_in_dim(block, other * width, width, 1)
            total = total + lax.ppermute(piece, "vel", pairs(count, stride, size, shift))
        trail.append((size, stride, rank, width))
        block = total
        stride *= size
    for size, stride, rank, width in reversed(trail):
        whole = jnp.zeros((block.shape[0], width * size), block.dtype)
        whole = lax.dynamic_update_slice_in_dim(whole, block, rank * width, 1)
        for shift in range(1, size):
            other = rank ^ shift
            piece = lax.ppermute(block, "vel", pairs(count, stride, size, shift))
            whole = lax.dynamic_update_slice_in_dim(whole, piece, other * width, 1)
        block = whole
    return block


def on_device(
    discrete_lattice_vectors,
    initial_compactness,
    initial_flow_vector,
    initial_thermal_level,
    initial_deviation,
):
    total_count = discrete_lattice_vectors.shape[1] * lax.axis_size("vel")
    weights = quad_weights(discrete_lattice_vectors, total_count)
    weighted_basis = moment_basis(discrete_lattice_vectors) * weights[None, :]
    number_of_cells = initial_compactness.shape[0]
    macro_profile = jnp.concatenate(
        [
            initial_compactness[None],
            initial_flow_vector,
            initial_thermal_level[None],
            jnp.zeros((3, number_of_cells), jnp.float32),
        ]
    )
    distribution = equilibrium(discrete_lattice_vectors, macro_profile) * (1.0 + initial_deviation)
    for iteration in range(ITERS):
        partial_moments = jnp.dot(weighted_basis, distribution, precision=lax.Precision.HIGHEST)
        summed = staged_sum(partial_moments, lax.axis_size("vel"))
        macro_profile = ns_solve(summed, wrap_deep, wrap_thin, keep_max)
        distribution = kinetic_update(distribution, discrete_lattice_vectors, macro_profile)
    return (distribution, macro_profile)


def solution(mesh):
    return jax.shard_map(
        on_device,
        mesh=mesh,
        in_specs=(P(None, "vel"), P("grp"), P(None, "grp"), P("grp"), P("vel", "grp")),
        out_specs=(P("vel", "grp"), P(None, "grp")),
        check_vma=False,
    )
```

```python
import functools

import jax
import jax.numpy as jnp
from jax import lax
from jax.experimental import pallas as pl
from jax.experimental.pallas import tpu as pltpu
from jax.sharding import PartitionSpec as P

ITERS = 2

ADIABATIC_INDEX = 5.0 / 3.0
CONDUCTIVE_SHARE = 2.0 / 3.0
SHEAR_EXPONENT = 0.81
SHEAR_REFERENCE = 0.05
KINETIC_STEP = 0.05
COURANT = 0.4
SPREAD_SCALE = 1.5

LOG2E = 1.4426950408889634
LANES = 128
TILE = 256
BASIS = 16
SENT = 14
COEF = 24
DAMP = 13
CHUNKS = 8
VMEM_BYTES = 24 * 1024 * 1024

WHOLE = pl.BlockSpec(memory_space=pltpu.VMEM)
OUTSIDE = pl.BlockSpec(memory_space=pltpu.HBM)
PARAMS = pltpu.CompilerParams(vmem_limit_bytes=VMEM_BYTES)


def dot(left, right):
    return jnp.dot(left, right, preferred_element_type=jnp.float32)


def rounded(values):
    return values.astype(jnp.bfloat16).astype(jnp.float32)


def phi_rows(velocities):
    vx, vy, vz = velocities[0:1], velocities[1:2], velocities[2:3]
    sq = vx * vx + vy * vy + vz * vz
    zero = jnp.zeros_like(vx)
    rows = [
        jnp.ones_like(vx), vx, vy, vz, sq, vx * vx, vx * vy, vx * vz, vy * vy, vy * vz,
        vx * sq, vy * sq, vz * sq, zero, zero, zero,
    ]
    return jnp.concatenate(rows, axis=0), sq


def make_tables(velocities, total_count):
    phi, sq = phi_rows(velocities)
    high = rounded(phi)
    middle = rounded(phi - high)
    low = phi - high - middle
    stacked = jnp.concatenate(
        [high, high, high, middle, middle, low, jnp.zeros((32, phi.shape[1]), jnp.float32)], axis=0
    )
    basis = stacked.T.astype(jnp.bfloat16)
    weighted = phi * (SPREAD_SCALE**3 * jnp.exp(sq / (2.0 * SPREAD_SCALE**2)) / total_count)
    top = rounded(weighted)
    rest = weighted - top
    moments = jnp.concatenate(
        [
            jnp.concatenate([top, top], axis=1),
            jnp.concatenate([rest, jnp.zeros_like(rest)], axis=1),
        ],
        axis=0,
    ).astype(jnp.bfloat16)
    return basis, moments


def expand(coefficients):
    high = coefficients.astype(jnp.bfloat16)
    rest = coefficients - high.astype(jnp.float32)
    middle = rest.astype(jnp.bfloat16)
    low = (rest - middle.astype(jnp.float32)).astype(jnp.bfloat16)
    zero = jnp.zeros((32, coefficients.shape[1]), jnp.bfloat16)
    return jnp.concatenate([high, middle, low, high, middle, high, zero], axis=0)


def store_moments(moments_ref, table, values, tile, blocks):
    high = values.astype(jnp.bfloat16)
    low = (values - high.astype(jnp.float32)).astype(jnp.bfloat16)
    both = dot(table, jnp.concatenate([high, low], axis=0))
    sums = both[:BASIS] + both[BASIS:]
    per_tile = TILE // LANES
    for part in range(per_tile):
        block = tile * per_tile + part
        moments_ref[pl.ds(block, SENT, stride=blocks), :] = sums[
            :SENT, part * LANES : (part + 1) * LANES
        ]


def start_kernel(
    total_count,
    vel_ref, density_ref, flow_ref, thermal_ref, deviation_ref,
    f_ref, moments_ref, basis_ref, table_ref,
    held, sems,
):
    cells = f_ref.shape[1]
    width = cells // CHUNKS
    copies = [
        pltpu.make_async_copy(
            deviation_ref.at[:, pl.ds(chunk * width, width)],
            held.at[:, pl.ds(chunk * width, width)],
            sems.at[chunk],
        )
        for chunk in range(CHUNKS)
    ]
    for copy in copies:
        copy.start()
    basis, table = make_tables(vel_ref[...], total_count)
    basis_ref[...] = basis
    table_ref[...] = table
    for chunk in range(CHUNKS):
        copies[chunk].wait()

        def step(local, carry, chunk=chunk):
            tile = chunk * (width // TILE) + local
            here = pl.ds(pl.multiple_of(tile * TILE, TILE), TILE)
            density, flow, thermal = density_ref[:, here], flow_ref[:, here], thermal_ref[:, here]
            rate = (0.5 * LOG2E) / thermal
            speed_sq = flow[0:1] * flow[0:1] + flow[1:2] * flow[1:2] + flow[2:3] * flow[2:3]
            rows = [-rate * speed_sq, 2.0 * rate * flow, -rate, jnp.zeros((11, TILE), jnp.float32)]
            exponent = dot(basis_ref[...], expand(jnp.concatenate(rows, axis=0)))
            scale = density / (thermal * jnp.sqrt(thermal))
            values = jnp.exp2(exponent) * (scale * (1.0 + held[:, here]))
            f_ref[:, here] = values
            store_moments(moments_ref, table_ref[...], values, tile, cells // LANES)
            return carry

        lax.fori_loop(0, width // TILE, step, 0, unroll=True)


def start_call(velocities, density, flow, thermal, deviation, total_count):
    local, cells = deviation.shape
    return pl.pallas_call(
        functools.partial(start_kernel, total_count),
        out_shape=(
            pltpu.VMEM((local, cells), jnp.float32),
            pltpu.VMEM((SENT * cells // LANES, LANES), jnp.float32),
            pltpu.VMEM((local, 128), jnp.bfloat16),
            pltpu.VMEM((2 * BASIS, 2 * local), jnp.bfloat16),
        ),
        in_specs=[WHOLE, WHOLE, WHOLE, WHOLE, OUTSIDE],
        out_specs=(WHOLE, WHOLE, WHOLE, WHOLE),
        scratch_shapes=[
            pltpu.VMEM((local, cells), jnp.float32),
            pltpu.SemaphoreType.DMA((CHUNKS,)),
        ],
        compiler_params=PARAMS,
        name="start",
    )(velocities, density.reshape(1, cells), flow, thermal.reshape(1, cells), deviation)


def transport_kernel(stream_ref, f_ref, g_ref):
    rows, cells = f_ref.shape
    chunk = min(1024, cells)
    blocks = cells // LANES
    per_chunk = chunk // LANES

    def row_step(row_tile, carry):
        here = pl.ds(pl.multiple_of(row_tile * 8, 8), 8)
        stream = jnp.broadcast_to(stream_ref[here, :], (8, LANES))
        rate = jnp.tile(KINETIC_STEP * jnp.abs(stream), (1, per_chunk + 2))
        half = jnp.tile(jnp.where(stream > 0, 0.5, -0.5), (1, per_chunk + 2))
        upward = half > 0
        for part in range(cells // chunk):
            first = part * per_chunk
            before = ((first - 1) % blocks) * LANES
            after = ((first + per_chunk) % blocks) * LANES
            x = jnp.concatenate(
                [
                    f_ref[here, before : before + LANES],
                    f_ref[here, part * chunk : (part + 1) * chunk],
                    f_ref[here, after : after + LANES],
                ],
                axis=1,
            )
            wide = x.shape[1]
            rise = x - pltpu.roll(x, 1, 1)
            ahead = pltpu.roll(rise, wide - 1, 1)
            slope = jnp.maximum(jnp.minimum(rise, ahead), 0.0) + jnp.minimum(
                jnp.maximum(rise, ahead), 0.0
            )
            face = x + half * slope
            other = jnp.where(upward, pltpu.roll(face, 1, 1), pltpu.roll(face, wide - 1, 1))
            moved = x - rate * (face - other)
            g_ref[here, part * chunk : (part + 1) * chunk] = moved[:, LANES : LANES + chunk]
        return carry

    lax.fori_loop(0, rows // 8, row_step, 0)


def transport_call(stream, f):
    return pl.pallas_call(
        transport_kernel,
        out_shape=pltpu.VMEM(f.shape, jnp.float32),
        in_specs=[WHOLE, WHOLE],
        out_specs=WHOLE,
        compiler_params=PARAMS,
        name="transport",
    )(stream, f)


def fluid_kernel(moments_ref, coef_ref, macro_ref):
    blocks = moments_ref.shape[0] // SENT
    m = [moments_ref[row * blocks : (row + 1) * blocks, :] for row in range(13)]
    lane = lax.broadcasted_iota(jnp.int32, (blocks, LANES), 1)

    def following(x):
        turned = pltpu.roll(x, LANES - 1, 1)
        return jnp.where(lane == LANES - 1, pltpu.roll(turned, blocks - 1, 0), turned)

    def preceding(x):
        turned = pltpu.roll(x, 1, 1)
        return jnp.where(lane == 0, pltpu.roll(turned, 1, 0), turned)

    def power(x, exponent):
        return jnp.exp2(exponent * jnp.log2(x))

    def primitives(w):
        inverse = 1.0 / w[0]
        u = [w[1] * inverse, w[2] * inverse, w[3] * inverse]
        uu = u[0] * u[0] + u[1] * u[1] + u[2] * u[2]
        t = (2.0 * w[4] * inverse - uu) * (1.0 / 3.0)
        return u, uu, t

    n = m[0]
    w = [n, m[1], m[2], m[3], 0.5 * m[4]]
    u, uu, t = primitives(w)
    p = n * t
    second = [[m[5], m[6], m[7]], [m[6], m[8], m[9]], [m[7], m[9], m[4] - m[5] - m[8]]]
    stress = [m[5] - m[1] * u[0] - p, m[6] - m[1] * u[1], m[7] - m[1] * u[2]]
    q = []
    for i in range(3):
        along = second[i][0] * u[0] + second[i][1] * u[1] + second[i][2] * u[2]
        q.append(0.5 * (m[10 + i] - u[i] * m[4] - 2.0 * along + 2.0 * n * u[i] * uu))

    shear = SHEAR_REFERENCE * power(t, SHEAR_EXPONENT)
    high_order = [
        stress[i] + ((4.0 / 3.0 if i == 0 else 1.0) * 0.5) * shear * (following(u[i]) - preceding(u[i]))
        for i in range(3)
    ]
    high_order.append(q[0] + (3.75 * 0.5) * shear * (following(t) - preceding(t)))
    half_order = [0.5 * h for h in high_order]
    face_order = [h + following(h) for h in half_order]

    def sweep(w, u, t, shear):
        rates = jnp.abs(u[0]) + jnp.sqrt(ADIABATIC_INDEX * t)
        signal = jnp.max(jnp.max(rates, axis=0, keepdims=True), axis=1, keepdims=True)
        step = COURANT / signal
        p = w[0] * t
        euler = [w[1], w[1] * u[0] + p, w[1] * u[1], w[1] * u[2], (w[4] + p) * u[0]]
        next_u = [following(x) for x in u]
        half_shear = 0.5 * shear
        face_shear = half_shear + following(half_shear)
        sxx = face_order[0] - (4.0 / 3.0) * face_shear * (next_u[0] - u[0])
        sxy = face_order[1] - face_shear * (next_u[1] - u[1])
        sxz = face_order[2] - face_shear * (next_u[2] - u[2])
        heat = face_order[3] - 3.75 * face_shear * (following(t) - t)
        work = 0.5 * (
            sxx * (u[0] + next_u[0]) + sxy * (u[1] + next_u[1]) + sxz * (u[2] + next_u[2])
        )
        viscous = [None, sxx, sxy, sxz, work + heat]
        out = []
        for i in range(5):
            spread = signal * w[i]
            total = 0.5 * ((euler[i] + spread) + following(euler[i] - spread))
            if viscous[i] is not None:
                total = total + viscous[i]
            out.append(w[i] - step * (total - preceding(total)))
        return out

    w = sweep(w, u, t, shear)
    u, uu, t = primitives(w)
    w = sweep(w, u, t, SHEAR_REFERENCE * power(t, SHEAR_EXPONENT))
    u, uu, t = primitives(w)
    n = w[0]

    for row, field in enumerate([n, u[0], u[1], u[2], t, q[0], q[1], q[2]]):
        macro_ref[pl.ds(row, blocks, stride=8), :] = field

    inverse = 1.0 / t
    relax = n * power(t, 1.0 - SHEAR_EXPONENT)
    damp = 1.0 / (1.0 + relax)
    scale = n * inverse * lax.rsqrt(t) * relax * damp
    beta = scale * ((1.0 - CONDUCTIVE_SHARE) / 5.0) * inverse * inverse / n
    cubic = beta * inverse
    qu = q[0] * u[0] + q[1] * u[1] + q[2] * u[2]
    offset = beta * (uu * inverse - 5.0)
    twice = 2.0 * cubic
    zz = q[2] * u[2]
    polynomial = [
        scale - qu * offset,
        offset * q[0] + twice * qu * u[0],
        offset * q[1] + twice * qu * u[1],
        offset * q[2] + twice * qu * u[2],
        -cubic * (qu + 2.0 * zz),
        -twice * (q[0] * u[0] - zz),
        -twice * (q[0] * u[1] + q[1] * u[0]),
        -twice * (q[0] * u[2] + q[2] * u[0]),
        -twice * (q[1] * u[1] - zz),
        -twice * (q[1] * u[2] + q[2] * u[1]),
        cubic * q[0],
        cubic * q[1],
        cubic * q[2],
    ]
    zero = jnp.zeros_like(n)
    rate = (0.5 * LOG2E) * inverse
    exponent = [-rate * uu, 2.0 * rate * u[0], 2.0 * rate * u[1], 2.0 * rate * u[2], -rate]
    rows = polynomial + [damp, zero, zero] + exponent + [zero, zero, zero]
    for row, field in enumerate(rows):
        coef_ref[pl.ds(row, blocks, stride=COEF), :] = field


def fluid_call(moments):
    blocks = moments.shape[0] // SENT
    return pl.pallas_call(
        fluid_kernel,
        out_shape=(
            pltpu.VMEM((blocks * COEF, LANES), jnp.float32),
            pltpu.VMEM((blocks * 8, LANES), jnp.float32),
        ),
        in_specs=[WHOLE],
        out_specs=(WHOLE, WHOLE),
        compiler_params=PARAMS,
        name="fluid",
    )(moments)


def relaxed(g, coef_ref, basis, tile):
    per_tile = TILE // LANES
    parts = [
        coef_ref[pl.ds(pl.multiple_of((tile * per_tile + part) * COEF, 8), COEF), :]
        for part in range(per_tile)
    ]
    coefficients = jnp.concatenate(parts, axis=1)
    polynomial = dot(basis, expand(coefficients[:BASIS]))
    rows = jnp.concatenate([coefficients[BASIS:], jnp.zeros((8, TILE), jnp.float32)], axis=0)
    exponent = dot(basis, expand(rows))
    return g * coefficients[DAMP : DAMP + 1] + jnp.exp2(exponent) * polynomial


def update_kernel(g_ref, coef_ref, basis_ref, table_ref, f_ref, moments_ref):
    cells = f_ref.shape[1]

    def step(tile, carry):
        here = pl.ds(pl.multiple_of(tile * TILE, TILE), TILE)
        values = relaxed(g_ref[:, here], coef_ref, basis_ref[...], tile)
        f_ref[:, here] = values
        store_moments(moments_ref, table_ref[...], values, tile, cells // LANES)
        return carry

    lax.fori_loop(0, cells // TILE, step, 0, unroll=4)


def update_call(g, coefficients, basis, table):
    cells = g.shape[1]
    return pl.pallas_call(
        update_kernel,
        out_shape=(
            pltpu.VMEM(g.shape, jnp.float32),
            pltpu.VMEM((SENT * cells // LANES, LANES), jnp.float32),
        ),
        in_specs=[WHOLE] * 4,
        out_specs=(WHOLE, WHOLE),
        compiler_params=PARAMS,
        name="update",
    )(g, coefficients, basis, table)


def finish_kernel(g_ref, coef_ref, macro_ref, basis_ref, f_ref, fields_ref, held, sems):
    cells = g_ref.shape[1]
    width = cells // CHUNKS
    copies = []
    for chunk in range(CHUNKS):

        def step(local, carry, chunk=chunk):
            tile = chunk * (width // TILE) + local
            here = pl.ds(pl.multiple_of(tile * TILE, TILE), TILE)
            held[:, here] = relaxed(g_ref[:, here], coef_ref, basis_ref[...], tile)
            for part in range(TILE // LANES):
                block = tile * (TILE // LANES) + part
                fields_ref[:, pl.ds(pl.multiple_of(block * LANES, LANES), LANES)] = macro_ref[
                    pl.ds(pl.multiple_of(block * 8, 8), 8), :
                ]
            return carry

        lax.fori_loop(0, width // TILE, step, 0, unroll=True)
        there = pl.ds(chunk * width, width)
        copy = pltpu.make_async_copy(held.at[:, there], f_ref.at[:, there], sems.at[chunk])
        copy.start()
        copies.append(copy)
    for copy in copies:
        copy.wait()


def finish_call(g, coefficients, macro, basis):
    cells = g.shape[1]
    return pl.pallas_call(
        finish_kernel,
        out_shape=(
            jax.ShapeDtypeStruct(g.shape, jnp.float32),
            jax.ShapeDtypeStruct((8, cells), jnp.float32),
        ),
        in_specs=[WHOLE] * 4,
        out_specs=(OUTSIDE, WHOLE),
        scratch_shapes=[
            pltpu.VMEM(g.shape, jnp.float32),
            pltpu.SemaphoreType.DMA((CHUNKS,)),
        ],
        compiler_params=PARAMS,
        name="finish",
    )(g, coefficients, macro, basis)


def stages(count):
    sizes = []
    for size in (2, 2):
        if count > 1 and count % size == 0:
            sizes.append(size)
            count //= size
    while count % 4 == 0:
        sizes.append(4)
        count //= 4
    while count % 2 == 0:
        sizes.append(2)
        count //= 2
    return sizes


def pairs(count, stride, size, shift):
    out = []
    for device in range(count):
        rank = device // stride % size
        out.append((device, device + ((rank ^ shift) - rank) * stride))
    return out


def staged_sum(values, count, beside):
    index = lax.axis_index("vel")
    stride, trail = 1, []
    block = values
    aside = None
    for number, size in enumerate(stages(count)):
        if number == 1:
            block, aside = beside(block)
        rank = index // stride % size
        width = block.shape[0] // size
        total = lax.dynamic_slice_in_dim(block, rank * width, width, 0)
        for shift in range(1, size):
            piece = lax.dynamic_slice_in_dim(block, (rank ^ shift) * width, width, 0)
            total = total + lax.ppermute(piece, "vel", pairs(count, stride, size, shift))
        if number == 1:
            total, aside = lax.optimization_barrier((total, aside))
        trail.append((size, stride, rank, width))
        block = total
        stride *= size
    for size, stride, rank, width in reversed(trail):
        whole = jnp.zeros((width * size, block.shape[1]), block.dtype)
        whole = lax.dynamic_update_slice_in_dim(whole, block, rank * width, 0)
        for shift in range(1, size):
            piece = lax.ppermute(block, "vel", pairs(count, stride, size, shift))
            whole = lax.dynamic_update_slice_in_dim(whole, piece, (rank ^ shift) * width, 0)
        block = whole
    return block, aside


def on_device(velocities, density, flow, thermal, deviation):
    count = lax.axis_size("vel")
    f, moments, basis, table = start_call(
        velocities, density, flow, thermal, deviation, velocities.shape[1] * count
    )
    stream = velocities[0][:, None]
    for iteration in range(ITERS):

        def beside(block):
            block, held = lax.optimization_barrier((block, f))
            return block, transport_call(stream, held)

        summed, g = staged_sum(moments, count, beside)
        coefficients, macro = fluid_call(summed)
        if iteration < ITERS - 1:
            f, moments = update_call(g, coefficients, basis, table)
    return finish_call(g, coefficients, macro, basis)


def solution(mesh):
    return jax.shard_map(
        on_device,
        mesh=mesh,
        in_specs=(P(None, "vel"), P("grp"), P(None, "grp"), P("grp"), P("vel", "grp")),
        out_specs=(P("vel", "grp"), P(None, "grp")),
        check_vma=False,
    )
```

```python
import functools

import jax
import jax.numpy as jnp
from jax import lax
from jax.experimental import pallas as pl
from jax.experimental.pallas import tpu as pltpu
from jax.sharding import PartitionSpec as P

ITERS = 2

ADIABATIC_INDEX = 5.0 / 3.0
CONDUCTIVE_SHARE = 2.0 / 3.0
SHEAR_EXPONENT = 0.81
SHEAR_REFERENCE = 0.05
KINETIC_STEP = 0.05
COURANT = 0.4
SPREAD_SCALE = 1.5

LOG2E = 1.4426950408889634
LANES = 128
TILE = 512
BASIS = 16
SENT = 14
COEF = 24
DAMP = 13
CHUNKS = 8
PARTS = 4
MIB = 1024 * 1024

WHOLE = pl.BlockSpec(memory_space=pltpu.VMEM)
OUTSIDE = pl.BlockSpec(memory_space=pltpu.HBM)


def params(mebibytes):
    return pltpu.CompilerParams(vmem_limit_bytes=mebibytes * MIB)


def near(values):
    return pltpu.with_memory_space_constraint(values, pltpu.VMEM)


def far(values):
    return pltpu.with_memory_space_constraint(values, pltpu.HBM)


def dot(left, right):
    return jnp.dot(left, right, preferred_element_type=jnp.float32)


def rounded(values):
    return values.astype(jnp.bfloat16).astype(jnp.float32)


def phi_rows(velocities):
    vx, vy, vz = velocities[0:1], velocities[1:2], velocities[2:3]
    sq = vx * vx + vy * vy + vz * vz
    zero = jnp.zeros_like(vx)
    rows = [
        jnp.ones_like(vx), vx, vy, vz, sq, vx * vx, vx * vy, vx * vz, vy * vy, vy * vz,
        vx * sq, vy * sq, vz * sq, zero, zero, zero,
    ]
    return jnp.concatenate(rows, axis=0), sq


def make_tables(velocities, total_count):
    phi, sq = phi_rows(velocities)
    high = rounded(phi)
    middle = rounded(phi - high)
    low = phi - high - middle
    stacked = jnp.concatenate(
        [high, high, high, middle, middle, low, jnp.zeros((32, phi.shape[1]), jnp.float32)], axis=0
    )
    basis = stacked.T.astype(jnp.bfloat16)
    weighted = phi * (SPREAD_SCALE**3 * jnp.exp(sq / (2.0 * SPREAD_SCALE**2)) / total_count)
    top = rounded(weighted)
    rest = weighted - top
    moments = jnp.concatenate(
        [
            jnp.concatenate([top, top], axis=1),
            jnp.concatenate([rest, jnp.zeros_like(rest)], axis=1),
        ],
        axis=0,
    ).astype(jnp.bfloat16)
    return basis, moments


def expand(coefficients):
    high = coefficients.astype(jnp.bfloat16)
    rest = coefficients - high.astype(jnp.float32)
    middle = rest.astype(jnp.bfloat16)
    low = (rest - middle.astype(jnp.float32)).astype(jnp.bfloat16)
    zero = jnp.zeros((32, coefficients.shape[1]), jnp.bfloat16)
    return jnp.concatenate([high, middle, low, high, middle, high, zero], axis=0)


def store_moments(moments_ref, table, values, tile, blocks):
    high = values.astype(jnp.bfloat16)
    low = (values - high.astype(jnp.float32)).astype(jnp.bfloat16)
    both = dot(table, jnp.concatenate([high, low], axis=0))
    sums = both[:BASIS] + both[BASIS:]
    per_tile = TILE // LANES
    for part in range(per_tile):
        block = tile * per_tile + part
        moments_ref[pl.ds(block, SENT, stride=blocks), :] = sums[
            :SENT, part * LANES : (part + 1) * LANES
        ]


def start_kernel(
    total_count,
    vel_hbm, density_hbm, flow_hbm, thermal_hbm, deviation_hbm,
    f_ref, moments_ref, basis_ref, table_ref, stream_ref,
    vel_ref, density_ref, flow_ref, thermal_ref, deviation_ref, small_sems, sems,
):
    cells = f_ref.shape[1]
    width = cells // CHUNKS
    small = [
        pltpu.make_async_copy(source, target, small_sems.at[number])
        for number, (source, target) in enumerate(
            [
                (vel_hbm, vel_ref),
                (density_hbm, density_ref),
                (flow_hbm, flow_ref),
                (thermal_hbm, thermal_ref),
            ]
        )
    ]
    for copy in small:
        copy.start()
    copies = [
        pltpu.make_async_copy(
            deviation_hbm.at[:, pl.ds(chunk * width, width)],
            deviation_ref.at[:, pl.ds(chunk * width, width)],
            sems.at[chunk],
        )
        for chunk in range(CHUNKS)
    ]
    for copy in copies:
        copy.start()
    small[0].wait()
    basis, table = make_tables(vel_ref[...], total_count)
    basis_ref[...] = basis
    table_ref[...] = table
    stream_ref[...] = jnp.broadcast_to(vel_ref[0:1, :], (LANES, vel_ref.shape[1])).T
    for copy in small[1:]:
        copy.wait()
    for chunk in range(CHUNKS):
        copies[chunk].wait()

        def step(local, carry, chunk=chunk):
            tile = chunk * (width // TILE) + local
            here = pl.ds(pl.multiple_of(tile * TILE, TILE), TILE)
            density, flow, thermal = density_ref[:, here], flow_ref[:, here], thermal_ref[:, here]
            rate = (0.5 * LOG2E) / thermal
            speed_sq = flow[0:1] * flow[0:1] + flow[1:2] * flow[1:2] + flow[2:3] * flow[2:3]
            rows = [-rate * speed_sq, 2.0 * rate * flow, -rate, jnp.zeros((11, TILE), jnp.float32)]
            exponent = dot(basis_ref[...], expand(jnp.concatenate(rows, axis=0)))
            scale = density / (thermal * jnp.sqrt(thermal))
            values = jnp.exp2(exponent) * (scale * (1.0 + deviation_ref[:, here]))
            f_ref[:, here] = values
            store_moments(moments_ref, table_ref[...], values, tile, cells // LANES)
            return carry

        lax.fori_loop(0, width // TILE, step, 0, unroll=True)


def start_call(velocities, density, flow, thermal, deviation, total_count):
    local, cells = deviation.shape
    return pl.pallas_call(
        functools.partial(start_kernel, total_count),
        out_shape=(
            pltpu.VMEM((local, cells), jnp.float32),
            pltpu.VMEM((SENT * cells // LANES, LANES), jnp.float32),
            pltpu.VMEM((local, 128), jnp.bfloat16),
            pltpu.VMEM((2 * BASIS, 2 * local), jnp.bfloat16),
            pltpu.VMEM((local, LANES), jnp.float32),
        ),
        in_specs=[OUTSIDE] * 5,
        out_specs=(WHOLE,) * 5,
        scratch_shapes=[
            pltpu.VMEM((3, local), jnp.float32),
            pltpu.VMEM((1, cells), jnp.float32),
            pltpu.VMEM((3, cells), jnp.float32),
            pltpu.VMEM((1, cells), jnp.float32),
            pltpu.VMEM((local, cells), jnp.float32),
            pltpu.SemaphoreType.DMA((4,)),
            pltpu.SemaphoreType.DMA((CHUNKS,)),
        ],
        compiler_params=params(16),
        name="start",
    )(
        far(velocities),
        far(density.reshape(1, cells)),
        far(flow),
        far(thermal.reshape(1, cells)),
        far(deviation),
    )


def transport_kernel(first_row, stream_ref, f_ref, g_ref):
    rows, cells = g_ref.shape
    blocks = cells // LANES
    lane = lax.broadcasted_iota(jnp.int32, (8, LANES), 1)
    at_first, at_last = lane == 0, lane == LANES - 1
    lag = 4

    def row_step(row_tile, carry):
        source = pl.ds(pl.multiple_of(first_row + row_tile * 8, 8), 8)
        target = pl.ds(pl.multiple_of(row_tile * 8, 8), 8)
        stream = stream_ref[source, :]
        upward = stream > 0
        rate = KINETIC_STEP * jnp.abs(stream)
        half = jnp.where(upward, 0.5, -0.5)
        x, up, rise, down, face, face_up, face_down = {}, {}, {}, {}, {}, {}, {}

        def load(b):
            at = (b % blocks) * LANES
            x[b] = f_ref[source, at : at + LANES]
            up[b] = pltpu.roll(x[b], 1, 1)

        def slope_in(b):
            rise[b] = x[b] - jnp.where(at_first, up[b - 1], up[b])
            down[b] = pltpu.roll(rise[b], LANES - 1, 1)

        def reconstruct(b):
            ahead = jnp.where(at_last, down[b + 1], down[b])
            slope = jnp.maximum(jnp.minimum(rise[b], ahead), 0.0) + jnp.minimum(
                jnp.maximum(rise[b], ahead), 0.0
            )
            face[b] = x[b] + half * slope
            face_up[b] = pltpu.roll(face[b], 1, 1)
            face_down[b] = pltpu.roll(face[b], LANES - 1, 1)

        def store(b):
            other = jnp.where(
                upward,
                jnp.where(at_first, face_up[b - 1], face_up[b]),
                jnp.where(at_last, face_down[b + 1], face_down[b]),
            )
            g_ref[target, b * LANES : (b + 1) * LANES] = x[b] - rate * (face[b] - other)

        for k in range(-2, blocks + 3 * lag + 4):
            for act, behind, low, high in (
                (load, 0, -2, blocks + 1),
                (slope_in, lag, -1, blocks + 1),
                (reconstruct, 2 * lag + 1, -1, blocks),
                (store, 3 * lag + 2, 0, blocks - 1),
            ):
                if low <= k - behind <= high:
                    act(k - behind)
        return carry

    lax.fori_loop(0, rows // 8, row_step, 0)


def transport_call(stream, f, part):
    local, cells = f.shape
    rows = local // PARTS
    return pl.pallas_call(
        functools.partial(transport_kernel, part * rows),
        out_shape=pltpu.VMEM((rows, cells), jnp.float32),
        in_specs=[WHOLE, WHOLE],
        out_specs=WHOLE,
        compiler_params=params(4),
        name="transport",
    )(near(stream), near(f))


def fluid_kernel(moments_ref, coef_ref, macro_ref):
    blocks = moments_ref.shape[0] // SENT
    m = [moments_ref[row * blocks : (row + 1) * blocks, :] for row in range(13)]
    lane = lax.broadcasted_iota(jnp.int32, (blocks, LANES), 1)

    def following(x):
        turned = pltpu.roll(x, LANES - 1, 1)
        return jnp.where(lane == LANES - 1, pltpu.roll(turned, blocks - 1, 0), turned)

    def preceding(x):
        turned = pltpu.roll(x, 1, 1)
        return jnp.where(lane == 0, pltpu.roll(turned, 1, 0), turned)

    def power(x, exponent):
        return jnp.exp2(exponent * jnp.log2(x))

    def primitives(w):
        inverse = 1.0 / w[0]
        u = [w[1] * inverse, w[2] * inverse, w[3] * inverse]
        uu = u[0] * u[0] + u[1] * u[1] + u[2] * u[2]
        t = (2.0 * w[4] * inverse - uu) * (1.0 / 3.0)
        return u, uu, t

    n = m[0]
    w = [n, m[1], m[2], m[3], 0.5 * m[4]]
    u, uu, t = primitives(w)
    p = n * t
    second = [[m[5], m[6], m[7]], [m[6], m[8], m[9]], [m[7], m[9], m[4] - m[5] - m[8]]]
    stress = [m[5] - m[1] * u[0] - p, m[6] - m[1] * u[1], m[7] - m[1] * u[2]]
    q = []
    for i in range(3):
        along = second[i][0] * u[0] + second[i][1] * u[1] + second[i][2] * u[2]
        q.append(0.5 * (m[10 + i] - u[i] * m[4] - 2.0 * along + 2.0 * n * u[i] * uu))

    shear = SHEAR_REFERENCE * power(t, SHEAR_EXPONENT)
    high_order = [
        stress[i] + ((4.0 / 3.0 if i == 0 else 1.0) * 0.5) * shear * (following(u[i]) - preceding(u[i]))
        for i in range(3)
    ]
    high_order.append(q[0] + (3.75 * 0.5) * shear * (following(t) - preceding(t)))
    half_order = [0.5 * h for h in high_order]
    face_order = [h + following(h) for h in half_order]

    def sweep(w, u, t, shear):
        rates = jnp.abs(u[0]) + jnp.sqrt(ADIABATIC_INDEX * t)
        signal = jnp.max(jnp.max(rates, axis=0, keepdims=True), axis=1, keepdims=True)
        step = COURANT / signal
        p = w[0] * t
        euler = [w[1], w[1] * u[0] + p, w[1] * u[1], w[1] * u[2], (w[4] + p) * u[0]]
        next_u = [following(x) for x in u]
        half_shear = 0.5 * shear
        face_shear = half_shear + following(half_shear)
        sxx = face_order[0] - (4.0 / 3.0) * face_shear * (next_u[0] - u[0])
        sxy = face_order[1] - face_shear * (next_u[1] - u[1])
        sxz = face_order[2] - face_shear * (next_u[2] - u[2])
        heat = face_order[3] - 3.75 * face_shear * (following(t) - t)
        work = 0.5 * (
            sxx * (u[0] + next_u[0]) + sxy * (u[1] + next_u[1]) + sxz * (u[2] + next_u[2])
        )
        viscous = [None, sxx, sxy, sxz, work + heat]
        out = []
        for i in range(5):
            spread = signal * w[i]
            total = 0.5 * ((euler[i] + spread) + following(euler[i] - spread))
            if viscous[i] is not None:
                total = total + viscous[i]
            out.append(w[i] - step * (total - preceding(total)))
        return out

    w = sweep(w, u, t, shear)
    u, uu, t = primitives(w)
    w = sweep(w, u, t, SHEAR_REFERENCE * power(t, SHEAR_EXPONENT))
    u, uu, t = primitives(w)
    n = w[0]

    for row, field in enumerate([n, u[0], u[1], u[2], t, q[0], q[1], q[2]]):
        macro_ref[pl.ds(row, blocks, stride=8), :] = field

    inverse = 1.0 / t
    relax = n * power(t, 1.0 - SHEAR_EXPONENT)
    damp = 1.0 / (1.0 + relax)
    scale = n * inverse * lax.rsqrt(t) * relax * damp
    beta = scale * ((1.0 - CONDUCTIVE_SHARE) / 5.0) * inverse * inverse / n
    cubic = beta * inverse
    qu = q[0] * u[0] + q[1] * u[1] + q[2] * u[2]
    offset = beta * (uu * inverse - 5.0)
    twice = 2.0 * cubic
    zz = q[2] * u[2]
    polynomial = [
        scale - qu * offset,
        offset * q[0] + twice * qu * u[0],
        offset * q[1] + twice * qu * u[1],
        offset * q[2] + twice * qu * u[2],
        -cubic * (qu + 2.0 * zz),
        -twice * (q[0] * u[0] - zz),
        -twice * (q[0] * u[1] + q[1] * u[0]),
        -twice * (q[0] * u[2] + q[2] * u[0]),
        -twice * (q[1] * u[1] - zz),
        -twice * (q[1] * u[2] + q[2] * u[1]),
        cubic * q[0],
        cubic * q[1],
        cubic * q[2],
    ]
    zero = jnp.zeros_like(n)
    rate = (0.5 * LOG2E) * inverse
    exponent = [-rate * uu, 2.0 * rate * u[0], 2.0 * rate * u[1], 2.0 * rate * u[2], -rate]
    rows = polynomial + [damp, zero, zero] + exponent + [zero, zero, zero]
    for row, field in enumerate(rows):
        coef_ref[pl.ds(row, blocks, stride=COEF), :] = field


def fluid_call(moments):
    blocks = moments.shape[0] // SENT
    return pl.pallas_call(
        fluid_kernel,
        out_shape=(
            pltpu.VMEM((blocks * COEF, LANES), jnp.float32),
            pltpu.VMEM((blocks * 8, LANES), jnp.float32),
        ),
        in_specs=[WHOLE],
        out_specs=(WHOLE, WHOLE),
        compiler_params=params(8),
        name="fluid",
    )(moments)


def relaxed(g, coef_ref, basis, tile):
    per_tile = TILE // LANES
    parts = [
        coef_ref[pl.ds(pl.multiple_of((tile * per_tile + part) * COEF, 8), COEF), :]
        for part in range(per_tile)
    ]
    coefficients = jnp.concatenate(parts, axis=1)
    polynomial = dot(basis, expand(coefficients[:BASIS]))
    rows = jnp.concatenate([coefficients[BASIS:], jnp.zeros((8, TILE), jnp.float32)], axis=0)
    exponent = dot(basis, expand(rows))
    return g * coefficients[DAMP : DAMP + 1] + jnp.exp2(exponent) * polynomial


def gathered(g_refs, here):
    return jnp.concatenate([ref[:, here] for ref in g_refs], axis=0)


def update_kernel(*refs):
    g_refs = refs[:PARTS]
    coef_ref, basis_ref, table_ref, f_ref, moments_ref = refs[PARTS:]
    cells = f_ref.shape[1]

    def step(tile, carry):
        here = pl.ds(pl.multiple_of(tile * TILE, TILE), TILE)
        values = relaxed(gathered(g_refs, here), coef_ref, basis_ref[...], tile)
        f_ref[:, here] = values
        store_moments(moments_ref, table_ref[...], values, tile, cells // LANES)
        return carry

    lax.fori_loop(0, cells // TILE, step, 0, unroll=4)


def update_call(g, coefficients, basis, table):
    rows, cells = g[0].shape
    return pl.pallas_call(
        update_kernel,
        out_shape=(
            pltpu.VMEM((rows * PARTS, cells), jnp.float32),
            pltpu.VMEM((SENT * cells // LANES, LANES), jnp.float32),
        ),
        in_specs=[WHOLE] * (PARTS + 3),
        out_specs=(WHOLE, WHOLE),
        compiler_params=params(8),
        name="update",
    )(*[near(part) for part in g], near(coefficients), near(basis), near(table))


def finish_kernel(*refs):
    g_refs = refs[:PARTS]
    coef_ref, macro_ref, basis_ref, f_ref, fields_ref, held, sems = refs[PARTS:]
    cells = held.shape[1]
    width = cells // CHUNKS
    copies = []
    for chunk in range(CHUNKS):

        def step(local, carry, chunk=chunk):
            tile = chunk * (width // TILE) + local
            here = pl.ds(pl.multiple_of(tile * TILE, TILE), TILE)
            held[:, here] = relaxed(gathered(g_refs, here), coef_ref, basis_ref[...], tile)
            for part in range(TILE // LANES):
                block = tile * (TILE // LANES) + part
                fields_ref[:, pl.ds(pl.multiple_of(block * LANES, LANES), LANES)] = macro_ref[
                    pl.ds(pl.multiple_of(block * 8, 8), 8), :
                ]
            return carry

        lax.fori_loop(0, width // TILE, step, 0, unroll=True)
        there = pl.ds(chunk * width, width)
        copy = pltpu.make_async_copy(held.at[:, there], f_ref.at[:, there], sems.at[chunk])
        copy.start()
        copies.append(copy)
    for copy in copies:
        copy.wait()


def finish_call(g, coefficients, macro, basis):
    rows, cells = g[0].shape
    return pl.pallas_call(
        finish_kernel,
        out_shape=(
            jax.ShapeDtypeStruct((rows * PARTS, cells), jnp.float32),
            jax.ShapeDtypeStruct((8, cells), jnp.float32),
        ),
        in_specs=[WHOLE] * (PARTS + 3),
        out_specs=(OUTSIDE, WHOLE),
        scratch_shapes=[
            pltpu.VMEM((rows * PARTS, cells), jnp.float32),
            pltpu.SemaphoreType.DMA((CHUNKS,)),
        ],
        compiler_params=params(16),
        name="finish",
    )(*[near(part) for part in g], near(coefficients), near(macro), near(basis))


def stages(count):
    sizes = []
    for size in (2, 2):
        if count > 1 and count % size == 0:
            sizes.append(size)
            count //= size
    while count % 4 == 0:
        sizes.append(4)
        count //= 4
    while count % 2 == 0:
        sizes.append(2)
        count //= 2
    return sizes


def pairs(count, stride, size, shift):
    out = []
    for device in range(count):
        rank = device // stride % size
        out.append((device, device + ((rank ^ shift) - rank) * stride))
    return out


def staged_sum(values, count, f, tasks):
    index = lax.axis_index("vel")
    stride, trail, results = 1, [], []
    block = values
    number = 0

    def before(block):
        if 0 < number <= len(tasks):
            block, held = lax.optimization_barrier((block, f))
            results.append(tasks[number - 1](held))
        return block

    def after(block):
        if 0 < number <= len(tasks):
            block, results[-1] = lax.optimization_barrier((block, results[-1]))
        return block

    for size in stages(count):
        block = before(block)
        rank = index // stride % size
        width = block.shape[0] // size
        total = lax.dynamic_slice_in_dim(block, rank * width, width, 0)
        for shift in range(1, size):
            piece = lax.dynamic_slice_in_dim(block, (rank ^ shift) * width, width, 0)
            total = total + lax.ppermute(piece, "vel", pairs(count, stride, size, shift))
        trail.append((size, stride, rank, width))
        block = after(total)
        stride *= size
        number += 1
    for size, stride, rank, width in reversed(trail):
        block = before(block)
        whole = jnp.zeros((width * size, block.shape[1]), block.dtype)
        whole = lax.dynamic_update_slice_in_dim(whole, block, rank * width, 0)
        for shift in range(1, size):
            piece = lax.ppermute(block, "vel", pairs(count, stride, size, shift))
            whole = lax.dynamic_update_slice_in_dim(whole, piece, (rank ^ shift) * width, 0)
        block = after(whole)
        number += 1
    return block, results


def on_device(velocities, density, flow, thermal, deviation):
    count = lax.axis_size("vel")
    f, moments, basis, table, stream = start_call(
        velocities, density, flow, thermal, deviation, velocities.shape[1] * count
    )
    for iteration in range(ITERS):
        tasks = [
            functools.partial(lambda held, part: transport_call(stream, held, part), part=part)
            for part in range(PARTS)
        ]
        summed, g = staged_sum(moments, count, f, tasks)
        coefficients, macro = fluid_call(summed)
        if iteration < ITERS - 1:
            f, moments = update_call(g, coefficients, basis, table)
    return finish_call(g, coefficients, macro, basis)


def solution(mesh):
    return jax.shard_map(
        on_device,
        mesh=mesh,
        in_specs=(P(None, "vel"), P("grp"), P(None, "grp"), P("grp"), P("vel", "grp")),
        out_specs=(P("vel", "grp"), P(None, "grp")),
        check_vma=False,
    )
```

```python
import functools

import jax
import jax.numpy as jnp
from jax import lax
from jax.experimental import pallas as pl
from jax.experimental.pallas import tpu as pltpu
from jax.sharding import PartitionSpec as P

ITERS = 2

ADIABATIC_INDEX = 5.0 / 3.0
CONDUCTIVE_SHARE = 2.0 / 3.0
SHEAR_EXPONENT = 0.81
SHEAR_REFERENCE = 0.05
KINETIC_STEP = 0.05
COURANT = 0.4
SPREAD_SCALE = 1.5

LOG2E = 1.4426950408889634
LANES = 128
TILE = 512
BASIS = 16
SENT = 14
COEF = 24
DAMP = 13
CHUNKS = 8
PARTS = 4
MIB = 1024 * 1024

WHOLE = pl.BlockSpec(memory_space=pltpu.VMEM)
OUTSIDE = pl.BlockSpec(memory_space=pltpu.HBM)


def params(mebibytes):
    return pltpu.CompilerParams(vmem_limit_bytes=mebibytes * MIB)


def near(values):
    return pltpu.with_memory_space_constraint(values, pltpu.VMEM)


def far(values):
    return pltpu.with_memory_space_constraint(values, pltpu.HBM)


def dot(left, right):
    return jnp.dot(left, right, preferred_element_type=jnp.float32)


def rounded(values):
    return values.astype(jnp.bfloat16).astype(jnp.float32)


def phi_rows(velocities):
    vx, vy, vz = velocities[0:1], velocities[1:2], velocities[2:3]
    sq = vx * vx + vy * vy + vz * vz
    zero = jnp.zeros_like(vx)
    rows = [
        jnp.ones_like(vx), vx, vy, vz, sq, vx * vx, vx * vy, vx * vz, vy * vy, vy * vz,
        vx * sq, vy * sq, vz * sq, zero, zero, zero,
    ]
    return jnp.concatenate(rows, axis=0), sq


def make_tables(velocities, total_count):
    phi, sq = phi_rows(velocities)
    high = rounded(phi)
    middle = rounded(phi - high)
    low = phi - high - middle
    stacked = jnp.concatenate(
        [high, high, high, middle, middle, low, jnp.zeros((32, phi.shape[1]), jnp.float32)], axis=0
    )
    basis = stacked.T.astype(jnp.bfloat16)
    weighted = phi * (SPREAD_SCALE**3 * jnp.exp(sq / (2.0 * SPREAD_SCALE**2)) / total_count)
    top = rounded(weighted)
    rest = weighted - top
    moments = jnp.concatenate(
        [
            jnp.concatenate([top, top], axis=1),
            jnp.concatenate([rest, jnp.zeros_like(rest)], axis=1),
        ],
        axis=0,
    ).astype(jnp.bfloat16)
    return basis, moments


def expand(coefficients):
    high = coefficients.astype(jnp.bfloat16)
    rest = coefficients - high.astype(jnp.float32)
    middle = rest.astype(jnp.bfloat16)
    low = (rest - middle.astype(jnp.float32)).astype(jnp.bfloat16)
    zero = jnp.zeros((32, coefficients.shape[1]), jnp.bfloat16)
    return jnp.concatenate([high, middle, low, high, middle, high, zero], axis=0)


def store_moments(moments_ref, table, values, tile, blocks):
    high = values.astype(jnp.bfloat16)
    low = (values - high.astype(jnp.float32)).astype(jnp.bfloat16)
    both = dot(table, jnp.concatenate([high, low], axis=0))
    sums = both[:BASIS] + both[BASIS:]
    per_tile = TILE // LANES
    for part in range(per_tile):
        block = tile * per_tile + part
        moments_ref[pl.ds(block, SENT, stride=blocks), :] = sums[
            :SENT, part * LANES : (part + 1) * LANES
        ]


def start_kernel(
    total_count,
    vel_hbm, density_hbm, flow_hbm, thermal_hbm, deviation_hbm,
    f_ref, moments_ref, basis_ref, table_ref, stream_ref,
    vel_ref, density_ref, flow_ref, thermal_ref, deviation_ref, small_sems, sems,
):
    cells = f_ref.shape[1]
    width = cells // CHUNKS
    small = [
        pltpu.make_async_copy(source, target, small_sems.at[number])
        for number, (source, target) in enumerate(
            [
                (vel_hbm, vel_ref),
                (density_hbm, density_ref),
                (flow_hbm, flow_ref),
                (thermal_hbm, thermal_ref),
            ]
        )
    ]
    for copy in small:
        copy.start()
    copies = [
        pltpu.make_async_copy(
            deviation_hbm.at[:, pl.ds(chunk * width, width)],
            deviation_ref.at[:, pl.ds(chunk * width, width)],
            sems.at[chunk],
        )
        for chunk in range(CHUNKS)
    ]
    for copy in copies:
        copy.start()
    small[0].wait()
    basis, table = make_tables(vel_ref[...], total_count)
    basis_ref[...] = basis
    table_ref[...] = table
    stream_ref[...] = jnp.broadcast_to(vel_ref[0:1, :], (LANES, vel_ref.shape[1])).T
    for copy in small[1:]:
        copy.wait()
    for chunk in range(CHUNKS):
        copies[chunk].wait()

        def step(local, carry, chunk=chunk):
            tile = chunk * (width // TILE) + local
            here = pl.ds(pl.multiple_of(tile * TILE, TILE), TILE)
            density, flow, thermal = density_ref[:, here], flow_ref[:, here], thermal_ref[:, here]
            rate = (0.5 * LOG2E) / thermal
            speed_sq = flow[0:1] * flow[0:1] + flow[1:2] * flow[1:2] + flow[2:3] * flow[2:3]
            rows = [-rate * speed_sq, 2.0 * rate * flow, -rate, jnp.zeros((11, TILE), jnp.float32)]
            exponent = dot(basis_ref[...], expand(jnp.concatenate(rows, axis=0)))
            scale = density / (thermal * jnp.sqrt(thermal))
            values = jnp.exp2(exponent) * (scale * (1.0 + deviation_ref[:, here]))
            f_ref[:, here] = values
            store_moments(moments_ref, table_ref[...], values, tile, cells // LANES)
            return carry

        lax.fori_loop(0, width // TILE, step, 0, unroll=True)


def start_call(velocities, density, flow, thermal, deviation, total_count):
    local, cells = deviation.shape
    return pl.pallas_call(
        functools.partial(start_kernel, total_count),
        out_shape=(
            pltpu.VMEM((local, cells), jnp.float32),
            pltpu.VMEM((SENT * cells // LANES, LANES), jnp.float32),
            pltpu.VMEM((local, 128), jnp.bfloat16),
            pltpu.VMEM((2 * BASIS, 2 * local), jnp.bfloat16),
            pltpu.VMEM((local, LANES), jnp.float32),
        ),
        in_specs=[OUTSIDE] * 5,
        out_specs=(WHOLE,) * 5,
        scratch_shapes=[
            pltpu.VMEM((3, local), jnp.float32),
            pltpu.VMEM((1, cells), jnp.float32),
            pltpu.VMEM((3, cells), jnp.float32),
            pltpu.VMEM((1, cells), jnp.float32),
            pltpu.VMEM((local, cells), jnp.float32),
            pltpu.SemaphoreType.DMA((4,)),
            pltpu.SemaphoreType.DMA((CHUNKS,)),
        ],
        compiler_params=params(16),
        name="start",
    )(
        far(velocities),
        far(density.reshape(1, cells)),
        far(flow),
        far(thermal.reshape(1, cells)),
        far(deviation),
    )


def transport_kernel(first_row, stream_ref, f_ref, g_ref):
    rows, cells = g_ref.shape
    blocks = cells // LANES
    lane = lax.broadcasted_iota(jnp.int32, (8, LANES), 1)
    at_first, at_last = lane == 0, lane == LANES - 1
    lag = 4

    def row_step(row_tile, carry):
        source = pl.ds(pl.multiple_of(first_row + row_tile * 8, 8), 8)
        target = pl.ds(pl.multiple_of(row_tile * 8, 8), 8)
        stream = stream_ref[source, :]
        upward = stream > 0
        rate = KINETIC_STEP * jnp.abs(stream)
        half = jnp.where(upward, 0.5, -0.5)
        x, up, rise, down, face, face_up, face_down = {}, {}, {}, {}, {}, {}, {}

        def load(b):
            at = (b % blocks) * LANES
            x[b] = f_ref[source, at : at + LANES]
            up[b] = pltpu.roll(x[b], 1, 1)

        def slope_in(b):
            rise[b] = x[b] - jnp.where(at_first, up[b - 1], up[b])
            down[b] = pltpu.roll(rise[b], LANES - 1, 1)

        def reconstruct(b):
            ahead = jnp.where(at_last, down[b + 1], down[b])
            slope = jnp.maximum(jnp.minimum(rise[b], ahead), 0.0) + jnp.minimum(
                jnp.maximum(rise[b], ahead), 0.0
            )
            face[b] = x[b] + half * slope
            face_up[b] = pltpu.roll(face[b], 1, 1)
            face_down[b] = pltpu.roll(face[b], LANES - 1, 1)

        def store(b):
            other = jnp.where(
                upward,
                jnp.where(at_first, face_up[b - 1], face_up[b]),
                jnp.where(at_last, face_down[b + 1], face_down[b]),
            )
            g_ref[target, b * LANES : (b + 1) * LANES] = x[b] - rate * (face[b] - other)

        for k in range(-2, blocks + 3 * lag + 4):
            for act, behind, low, high in (
                (load, 0, -2, blocks + 1),
                (slope_in, lag, -1, blocks + 1),
                (reconstruct, 2 * lag + 1, -1, blocks),
                (store, 3 * lag + 2, 0, blocks - 1),
            ):
                if low <= k - behind <= high:
                    act(k - behind)
        return carry

    lax.fori_loop(0, rows // 8, row_step, 0)


def transport_call(stream, f, part):
    local, cells = f.shape
    rows = local // PARTS
    return pl.pallas_call(
        functools.partial(transport_kernel, part * rows),
        out_shape=pltpu.VMEM((rows, cells), jnp.float32),
        in_specs=[WHOLE, WHOLE],
        out_specs=WHOLE,
        compiler_params=params(4),
        name="transport",
    )(near(stream), near(f))


def fluid_kernel(moments_ref, coef_ref, macro_ref):
    blocks = moments_ref.shape[0] // SENT
    m = [moments_ref[row * blocks : (row + 1) * blocks, :] for row in range(13)]
    lane = lax.broadcasted_iota(jnp.int32, (blocks, LANES), 1)

    def following(x):
        turned = pltpu.roll(x, LANES - 1, 1)
        return jnp.where(lane == LANES - 1, pltpu.roll(turned, blocks - 1, 0), turned)

    def preceding(x):
        turned = pltpu.roll(x, 1, 1)
        return jnp.where(lane == 0, pltpu.roll(turned, 1, 0), turned)

    def power(x, exponent):
        return jnp.exp2(exponent * jnp.log2(x))

    def primitives(w):
        inverse = 1.0 / w[0]
        u = [w[1] * inverse, w[2] * inverse, w[3] * inverse]
        uu = u[0] * u[0] + u[1] * u[1] + u[2] * u[2]
        t = (2.0 * w[4] * inverse - uu) * (1.0 / 3.0)
        return u, uu, t

    n = m[0]
    w = [n, m[1], m[2], m[3], 0.5 * m[4]]
    u, uu, t = primitives(w)
    p = n * t
    second = [[m[5], m[6], m[7]], [m[6], m[8], m[9]], [m[7], m[9], m[4] - m[5] - m[8]]]
    stress = [m[5] - m[1] * u[0] - p, m[6] - m[1] * u[1], m[7] - m[1] * u[2]]
    q = []
    for i in range(3):
        along = second[i][0] * u[0] + second[i][1] * u[1] + second[i][2] * u[2]
        q.append(0.5 * (m[10 + i] - u[i] * m[4] - 2.0 * along + 2.0 * n * u[i] * uu))

    shear = SHEAR_REFERENCE * power(t, SHEAR_EXPONENT)
    high_order = [
        stress[i] + ((4.0 / 3.0 if i == 0 else 1.0) * 0.5) * shear * (following(u[i]) - preceding(u[i]))
        for i in range(3)
    ]
    high_order.append(q[0] + (3.75 * 0.5) * shear * (following(t) - preceding(t)))
    half_order = [0.5 * h for h in high_order]
    face_order = [h + following(h) for h in half_order]

    def sweep(w, u, t, shear):
        rates = jnp.abs(u[0]) + jnp.sqrt(ADIABATIC_INDEX * t)
        signal = jnp.max(jnp.max(rates, axis=0, keepdims=True), axis=1, keepdims=True)
        step = COURANT / signal
        p = w[0] * t
        euler = [w[1], w[1] * u[0] + p, w[1] * u[1], w[1] * u[2], (w[4] + p) * u[0]]
        next_u = [following(x) for x in u]
        half_shear = 0.5 * shear
        face_shear = half_shear + following(half_shear)
        sxx = face_order[0] - (4.0 / 3.0) * face_shear * (next_u[0] - u[0])
        sxy = face_order[1] - face_shear * (next_u[1] - u[1])
        sxz = face_order[2] - face_shear * (next_u[2] - u[2])
        heat = face_order[3] - 3.75 * face_shear * (following(t) - t)
        work = 0.5 * (
            sxx * (u[0] + next_u[0]) + sxy * (u[1] + next_u[1]) + sxz * (u[2] + next_u[2])
        )
        viscous = [None, sxx, sxy, sxz, work + heat]
        out = []
        for i in range(5):
            spread = signal * w[i]
            total = 0.5 * ((euler[i] + spread) + following(euler[i] - spread))
            if viscous[i] is not None:
                total = total + viscous[i]
            out.append(w[i] - step * (total - preceding(total)))
        return out

    w = sweep(w, u, t, shear)
    u, uu, t = primitives(w)
    w = sweep(w, u, t, SHEAR_REFERENCE * power(t, SHEAR_EXPONENT))
    u, uu, t = primitives(w)
    n = w[0]

    for row, field in enumerate([n, u[0], u[1], u[2], t, q[0], q[1], q[2]]):
        macro_ref[pl.ds(row, blocks, stride=8), :] = field

    inverse = 1.0 / t
    relax = n * power(t, 1.0 - SHEAR_EXPONENT)
    damp = 1.0 / (1.0 + relax)
    scale = n * inverse * lax.rsqrt(t) * relax * damp
    beta = scale * ((1.0 - CONDUCTIVE_SHARE) / 5.0) * inverse * inverse / n
    cubic = beta * inverse
    qu = q[0] * u[0] + q[1] * u[1] + q[2] * u[2]
    offset = beta * (uu * inverse - 5.0)
    twice = 2.0 * cubic
    zz = q[2] * u[2]
    polynomial = [
        scale - qu * offset,
        offset * q[0] + twice * qu * u[0],
        offset * q[1] + twice * qu * u[1],
        offset * q[2] + twice * qu * u[2],
        -cubic * (qu + 2.0 * zz),
        -twice * (q[0] * u[0] - zz),
        -twice * (q[0] * u[1] + q[1] * u[0]),
        -twice * (q[0] * u[2] + q[2] * u[0]),
        -twice * (q[1] * u[1] - zz),
        -twice * (q[1] * u[2] + q[2] * u[1]),
        cubic * q[0],
        cubic * q[1],
        cubic * q[2],
    ]
    zero = jnp.zeros_like(n)
    rate = (0.5 * LOG2E) * inverse
    exponent = [-rate * uu, 2.0 * rate * u[0], 2.0 * rate * u[1], 2.0 * rate * u[2], -rate]
    rows = polynomial + [damp, zero, zero] + exponent + [zero, zero, zero]
    for row, field in enumerate(rows):
        coef_ref[pl.ds(row, blocks, stride=COEF), :] = field


def fluid_call(moments):
    blocks = moments.shape[0] // SENT
    return pl.pallas_call(
        fluid_kernel,
        out_shape=(
            pltpu.VMEM((blocks * COEF, LANES), jnp.float32),
            pltpu.VMEM((blocks * 8, LANES), jnp.float32),
        ),
        in_specs=[WHOLE],
        out_specs=(WHOLE, WHOLE),
        compiler_params=params(8),
        name="fluid",
    )(moments)


def relaxed(g, coef_ref, basis, tile):
    per_tile = TILE // LANES
    parts = [
        coef_ref[pl.ds(pl.multiple_of((tile * per_tile + part) * COEF, 8), COEF), :]
        for part in range(per_tile)
    ]
    coefficients = jnp.concatenate(parts, axis=1)
    polynomial = dot(basis, expand(coefficients[:BASIS]))
    rows = jnp.concatenate([coefficients[BASIS:], jnp.zeros((8, TILE), jnp.float32)], axis=0)
    exponent = dot(basis, expand(rows))
    return g * coefficients[DAMP : DAMP + 1] + jnp.exp2(exponent) * polynomial


def gathered(g_refs, here):
    return jnp.concatenate([ref[:, here] for ref in g_refs], axis=0)


def update_kernel(*refs):
    g_refs = refs[:PARTS]
    coef_ref, basis_ref, table_ref, f_ref, moments_ref = refs[PARTS:]
    cells = f_ref.shape[1]

    def step(tile, carry):
        here = pl.ds(pl.multiple_of(tile * TILE, TILE), TILE)
        values = relaxed(gathered(g_refs, here), coef_ref, basis_ref[...], tile)
        f_ref[:, here] = values
        store_moments(moments_ref, table_ref[...], values, tile, cells // LANES)
        return carry

    lax.fori_loop(0, cells // TILE, step, 0, unroll=4)


def update_call(g, coefficients, basis, table):
    rows, cells = g[0].shape
    return pl.pallas_call(
        update_kernel,
        out_shape=(
            pltpu.VMEM((rows * PARTS, cells), jnp.float32),
            pltpu.VMEM((SENT * cells // LANES, LANES), jnp.float32),
        ),
        in_specs=[WHOLE] * (PARTS + 3),
        out_specs=(WHOLE, WHOLE),
        compiler_params=params(8),
        name="update",
    )(*[near(part) for part in g], near(coefficients), near(basis), near(table))


def finish_kernel(*refs):
    g_refs = refs[:PARTS]
    coef_ref, macro_ref, basis_ref, f_ref, fields_ref, held, sems = refs[PARTS:]
    cells = held.shape[1]
    width = cells // CHUNKS
    copies = []
    for chunk in range(CHUNKS):

        def step(local, carry, chunk=chunk):
            tile = chunk * (width // TILE) + local
            here = pl.ds(pl.multiple_of(tile * TILE, TILE), TILE)
            held[:, here] = relaxed(gathered(g_refs, here), coef_ref, basis_ref[...], tile)
            for part in range(TILE // LANES):
                block = tile * (TILE // LANES) + part
                fields_ref[:, pl.ds(pl.multiple_of(block * LANES, LANES), LANES)] = macro_ref[
                    pl.ds(pl.multiple_of(block * 8, 8), 8), :
                ]
            return carry

        lax.fori_loop(0, width // TILE, step, 0, unroll=True)
        there = pl.ds(chunk * width, width)
        copy = pltpu.make_async_copy(held.at[:, there], f_ref.at[:, there], sems.at[chunk])
        copy.start()
        copies.append(copy)
    for copy in copies:
        copy.wait()


def finish_call(g, coefficients, macro, basis):
    rows, cells = g[0].shape
    return pl.pallas_call(
        finish_kernel,
        out_shape=(
            jax.ShapeDtypeStruct((rows * PARTS, cells), jnp.float32),
            jax.ShapeDtypeStruct((8, cells), jnp.float32),
        ),
        in_specs=[WHOLE] * (PARTS + 3),
        out_specs=(OUTSIDE, WHOLE),
        scratch_shapes=[
            pltpu.VMEM((rows * PARTS, cells), jnp.float32),
            pltpu.SemaphoreType.DMA((CHUNKS,)),
        ],
        compiler_params=params(16),
        name="finish",
    )(*[near(part) for part in g], near(coefficients), near(macro), near(basis))


def swap(values, count):
    return lax.ppermute(values, "vel", [(device, device ^ 1) for device in range(count)])


def staged_sum(values, count, offsets, f, tasks):
    chips = count // 2
    groups = [list(range(part, count, 2)) for part in range(2)]
    rows, lanes = values.shape
    half, width = rows // 2, rows // count
    results = []

    def exchange(block, some):
        block, held = lax.optimization_barrier((block, f))
        made = [task(held) for task in some]
        out = lax.all_to_all(block, "vel", 0, 0, axis_index_groups=groups, tiled=True)
        out, made = lax.optimization_barrier((out, made))
        results.extend(made)
        return out

    own = lax.dynamic_slice_in_dim(values, offsets[0], half, 0, allow_negative_indices=False)
    other = lax.dynamic_slice_in_dim(values, offsets[1], half, 0, allow_negative_indices=False)
    block = own + swap(other, count)
    block = jnp.sum(exchange(block.reshape(chips, width, lanes), tasks[: PARTS // 2]), axis=0)
    copies = jnp.broadcast_to(block[None], (chips, width, lanes))
    block = exchange(copies, tasks[PARTS // 2 :]).reshape(half, lanes)
    whole = jnp.zeros((rows, lanes), values.dtype)
    for part, offset in ((block, offsets[0]), (swap(block, count), offsets[1])):
        whole = lax.dynamic_update_slice(
            whole, part, (offset, 0), allow_negative_indices=(False, False)
        )
    return whole, results


def on_device(velocities, density, flow, thermal, deviation):
    count = lax.axis_size("vel")
    half = SENT * density.shape[0] // LANES // 2
    mine = (lax.axis_index("vel") & 1) * half
    offsets = (mine, half - mine)
    velocities, offsets = lax.optimization_barrier((velocities, offsets))
    f, moments, basis, table, stream = start_call(
        velocities, density, flow, thermal, deviation, velocities.shape[1] * count
    )
    for iteration in range(ITERS):
        tasks = [
            functools.partial(lambda held, part: transport_call(stream, held, part), part=part)
            for part in range(PARTS)
        ]
        summed, g = staged_sum(moments, count, offsets, f, tasks)
        coefficients, macro = fluid_call(summed)
        if iteration < ITERS - 1:
            f, moments = update_call(g, coefficients, basis, table)
    return finish_call(g, coefficients, macro, basis)


def solution(mesh):
    return jax.shard_map(
        on_device,
        mesh=mesh,
        in_specs=(P(None, "vel"), P("grp"), P(None, "grp"), P("grp"), P("vel", "grp")),
        out_specs=(P("vel", "grp"), P(None, "grp")),
        check_vma=False,
    )
```

```python
import functools

import jax
import jax.numpy as jnp
from jax import lax
from jax.experimental import pallas as pl
from jax.experimental.pallas import tpu as pltpu
from jax.sharding import PartitionSpec as P

ITERS = 2

ADIABATIC_INDEX = 5.0 / 3.0
CONDUCTIVE_SHARE = 2.0 / 3.0
SHEAR_EXPONENT = 0.81
SHEAR_REFERENCE = 0.05
KINETIC_STEP = 0.05
COURANT = 0.4
SPREAD_SCALE = 1.5

LOG2E = 1.4426950408889634
LANES = 128
TILE = 256
BASIS = 16
SENT = 13
COEF = 24
DAMP = 13
CHUNKS = 8
PARTS = 4
MIB = 1024 * 1024

WHOLE = pl.BlockSpec(memory_space=pltpu.VMEM)
OUTSIDE = pl.BlockSpec(memory_space=pltpu.HBM)


def params(mebibytes):
    return pltpu.CompilerParams(vmem_limit_bytes=mebibytes * MIB)


def near(values):
    return pltpu.with_memory_space_constraint(values, pltpu.VMEM)


def far(values):
    return pltpu.with_memory_space_constraint(values, pltpu.HBM)


def dot(left, right):
    return jnp.dot(left, right, preferred_element_type=jnp.float32)


def rounded(values):
    return values.astype(jnp.bfloat16).astype(jnp.float32)


def phi_rows(velocities):
    vx, vy, vz = velocities[0:1], velocities[1:2], velocities[2:3]
    sq = vx * vx + vy * vy + vz * vz
    zero = jnp.zeros_like(vx)
    rows = [
        jnp.ones_like(vx), vx, vy, vz, sq, vx * vx, vx * vy, vx * vz, vy * vy, vy * vz,
        vx * sq, vy * sq, vz * sq, zero, zero, zero,
    ]
    return jnp.concatenate(rows, axis=0), sq


def make_tables(velocities, total_count):
    phi, sq = phi_rows(velocities)
    high = rounded(phi)
    middle = rounded(phi - high)
    low = phi - high - middle
    stacked = jnp.concatenate(
        [high, high, high, middle, middle, low, jnp.zeros((32, phi.shape[1]), jnp.float32)], axis=0
    )
    basis = stacked.T.astype(jnp.bfloat16)
    weighted = phi * (SPREAD_SCALE**3 * jnp.exp(sq / (2.0 * SPREAD_SCALE**2)) / total_count)
    top = rounded(weighted)
    rest = weighted - top
    moments = jnp.concatenate(
        [
            jnp.concatenate([top, top], axis=1),
            jnp.concatenate([rest, jnp.zeros_like(rest)], axis=1),
        ],
        axis=0,
    ).astype(jnp.bfloat16)
    return basis, moments


def expand(coefficients):
    high = coefficients.astype(jnp.bfloat16)
    rest = coefficients - high.astype(jnp.float32)
    middle = rest.astype(jnp.bfloat16)
    low = (rest - middle.astype(jnp.float32)).astype(jnp.bfloat16)
    zero = jnp.zeros((32, coefficients.shape[1]), jnp.bfloat16)
    return jnp.concatenate([high, middle, low, high, middle, high, zero], axis=0)


def store_moments(moments_ref, table, values, tile, blocks):
    high = values.astype(jnp.bfloat16)
    low = (values - high.astype(jnp.float32)).astype(jnp.bfloat16)
    both = dot(table, jnp.concatenate([high, low], axis=0))
    sums = both[:BASIS] + both[BASIS:]
    per_tile = TILE // LANES
    for part in range(per_tile):
        block = tile * per_tile + part
        moments_ref[pl.ds(block, SENT, stride=blocks), :] = sums[
            :SENT, part * LANES : (part + 1) * LANES
        ]


def start_kernel(
    total_count,
    vel_hbm, density_hbm, flow_hbm, thermal_hbm, deviation_hbm,
    f_ref, moments_ref, basis_ref, table_ref, stream_ref,
    vel_ref, density_ref, flow_ref, thermal_ref, deviation_ref, small_sems, sems,
):
    cells = f_ref.shape[1]
    width = cells // CHUNKS
    small = [
        pltpu.make_async_copy(source, target, small_sems.at[number])
        for number, (source, target) in enumerate(
            [
                (vel_hbm, vel_ref),
                (density_hbm, density_ref),
                (flow_hbm, flow_ref),
                (thermal_hbm, thermal_ref),
            ]
        )
    ]
    for copy in small:
        copy.start()
    copies = [
        pltpu.make_async_copy(
            deviation_hbm.at[:, pl.ds(chunk * width, width)],
            deviation_ref.at[:, pl.ds(chunk * width, width)],
            sems.at[chunk],
        )
        for chunk in range(CHUNKS)
    ]
    for copy in copies:
        copy.start()
    small[0].wait()
    basis, table = make_tables(vel_ref[...], total_count)
    basis_ref[...] = basis
    table_ref[...] = table
    stream_ref[...] = jnp.broadcast_to(vel_ref[0:1, :], (LANES, vel_ref.shape[1])).T
    for copy in small[1:]:
        copy.wait()
    for chunk in range(CHUNKS):
        copies[chunk].wait()

        def step(local, carry, chunk=chunk):
            tile = chunk * (width // TILE) + local
            here = pl.ds(pl.multiple_of(tile * TILE, TILE), TILE)
            density, flow, thermal = density_ref[:, here], flow_ref[:, here], thermal_ref[:, here]
            rate = (0.5 * LOG2E) / thermal
            speed_sq = flow[0:1] * flow[0:1] + flow[1:2] * flow[1:2] + flow[2:3] * flow[2:3]
            rows = [-rate * speed_sq, 2.0 * rate * flow, -rate, jnp.zeros((11, TILE), jnp.float32)]
            exponent = dot(basis_ref[...], expand(jnp.concatenate(rows, axis=0)))
            scale = density / (thermal * jnp.sqrt(thermal))
            values = jnp.exp2(exponent) * (scale * (1.0 + deviation_ref[:, here]))
            f_ref[:, here] = values
            store_moments(moments_ref, table_ref[...], values, tile, cells // LANES)
            return carry

        lax.fori_loop(0, width // TILE, step, 0, unroll=True)


def start_call(velocities, density, flow, thermal, deviation, total_count):
    local, cells = deviation.shape
    return pl.pallas_call(
        functools.partial(start_kernel, total_count),
        out_shape=(
            pltpu.VMEM((local, cells), jnp.float32),
            pltpu.VMEM((SENT * cells // LANES, LANES), jnp.float32),
            pltpu.VMEM((local, 128), jnp.bfloat16),
            pltpu.VMEM((2 * BASIS, 2 * local), jnp.bfloat16),
            pltpu.VMEM((local, LANES), jnp.float32),
        ),
        in_specs=[OUTSIDE] * 5,
        out_specs=(WHOLE,) * 5,
        scratch_shapes=[
            pltpu.VMEM((3, local), jnp.float32),
            pltpu.VMEM((1, cells), jnp.float32),
            pltpu.VMEM((3, cells), jnp.float32),
            pltpu.VMEM((1, cells), jnp.float32),
            pltpu.VMEM((local, cells), jnp.float32),
            pltpu.SemaphoreType.DMA((4,)),
            pltpu.SemaphoreType.DMA((CHUNKS,)),
        ],
        compiler_params=params(16),
        name="start",
    )(
        far(velocities),
        far(density.reshape(1, cells)),
        far(flow),
        far(thermal.reshape(1, cells)),
        far(deviation),
    )


def transport_kernel(first_row, stream_ref, f_ref, g_ref):
    rows, cells = g_ref.shape
    blocks = cells // LANES
    lane = lax.broadcasted_iota(jnp.int32, (8, LANES), 1)
    at_first, at_last = lane == 0, lane == LANES - 1
    lag = 4

    def row_step(row_tile, carry):
        source = pl.ds(pl.multiple_of(first_row + row_tile * 8, 8), 8)
        target = pl.ds(pl.multiple_of(row_tile * 8, 8), 8)
        stream = stream_ref[source, :]
        upward = stream > 0
        rate = KINETIC_STEP * jnp.abs(stream)
        half = jnp.where(upward, 0.5, -0.5)
        x, up, rise, down, face, face_up, face_down = {}, {}, {}, {}, {}, {}, {}

        def load(b):
            at = (b % blocks) * LANES
            x[b] = f_ref[source, at : at + LANES]
            up[b] = pltpu.roll(x[b], 1, 1)

        def slope_in(b):
            rise[b] = x[b] - jnp.where(at_first, up[b - 1], up[b])
            down[b] = pltpu.roll(rise[b], LANES - 1, 1)

        def reconstruct(b):
            ahead = jnp.where(at_last, down[b + 1], down[b])
            slope = jnp.maximum(jnp.minimum(rise[b], ahead), 0.0) + jnp.minimum(
                jnp.maximum(rise[b], ahead), 0.0
            )
            face[b] = x[b] + half * slope
            face_up[b] = pltpu.roll(face[b], 1, 1)
            face_down[b] = pltpu.roll(face[b], LANES - 1, 1)

        def store(b):
            other = jnp.where(
                upward,
                jnp.where(at_first, face_up[b - 1], face_up[b]),
                jnp.where(at_last, face_down[b + 1], face_down[b]),
            )
            g_ref[target, b * LANES : (b + 1) * LANES] = x[b] - rate * (face[b] - other)

        for k in range(-2, blocks + 3 * lag + 4):
            for act, behind, low, high in (
                (load, 0, -2, blocks + 1),
                (slope_in, lag, -1, blocks + 1),
                (reconstruct, 2 * lag + 1, -1, blocks),
                (store, 3 * lag + 2, 0, blocks - 1),
            ):
                if low <= k - behind <= high:
                    act(k - behind)
        return carry

    lax.fori_loop(0, rows // 8, row_step, 0)


def transport_call(stream, f, part):
    local, cells = f.shape
    rows = local // PARTS
    return pl.pallas_call(
        functools.partial(transport_kernel, part * rows),
        out_shape=pltpu.VMEM((rows, cells), jnp.float32),
        in_specs=[WHOLE, WHOLE],
        out_specs=WHOLE,
        compiler_params=params(4),
        name="transport",
    )(near(stream), near(f))


def fluid_kernel(moments_ref, coef_ref, macro_ref):
    blocks = moments_ref.shape[0] // SENT
    m = [moments_ref[row * blocks : (row + 1) * blocks, :] for row in range(13)]
    lane = lax.broadcasted_iota(jnp.int32, (blocks, LANES), 1)

    def following(x):
        turned = pltpu.roll(x, LANES - 1, 1)
        return jnp.where(lane == LANES - 1, pltpu.roll(turned, blocks - 1, 0), turned)

    def preceding(x):
        turned = pltpu.roll(x, 1, 1)
        return jnp.where(lane == 0, pltpu.roll(turned, 1, 0), turned)

    def power(x, exponent):
        return jnp.exp2(exponent * jnp.log2(x))

    def primitives(w):
        inverse = 1.0 / w[0]
        u = [w[1] * inverse, w[2] * inverse, w[3] * inverse]
        uu = u[0] * u[0] + u[1] * u[1] + u[2] * u[2]
        t = (2.0 * w[4] * inverse - uu) * (1.0 / 3.0)
        return u, uu, t

    n = m[0]
    w = [n, m[1], m[2], m[3], 0.5 * m[4]]
    u, uu, t = primitives(w)
    p = n * t
    second = [[m[5], m[6], m[7]], [m[6], m[8], m[9]], [m[7], m[9], m[4] - m[5] - m[8]]]
    stress = [m[5] - m[1] * u[0] - p, m[6] - m[1] * u[1], m[7] - m[1] * u[2]]
    q = []
    for i in range(3):
        along = second[i][0] * u[0] + second[i][1] * u[1] + second[i][2] * u[2]
        q.append(0.5 * (m[10 + i] - u[i] * m[4] - 2.0 * along + 2.0 * n * u[i] * uu))

    shear = SHEAR_REFERENCE * power(t, SHEAR_EXPONENT)
    high_order = [
        stress[i] + ((4.0 / 3.0 if i == 0 else 1.0) * 0.5) * shear * (following(u[i]) - preceding(u[i]))
        for i in range(3)
    ]
    high_order.append(q[0] + (3.75 * 0.5) * shear * (following(t) - preceding(t)))
    half_order = [0.5 * h for h in high_order]
    face_order = [h + following(h) for h in half_order]

    def sweep(w, u, t, shear):
        rates = jnp.abs(u[0]) + jnp.sqrt(ADIABATIC_INDEX * t)
        signal = jnp.max(jnp.max(rates, axis=0, keepdims=True), axis=1, keepdims=True)
        step = COURANT / signal
        p = w[0] * t
        euler = [w[1], w[1] * u[0] + p, w[1] * u[1], w[1] * u[2], (w[4] + p) * u[0]]
        next_u = [following(x) for x in u]
        half_shear = 0.5 * shear
        face_shear = half_shear + following(half_shear)
        sxx = face_order[0] - (4.0 / 3.0) * face_shear * (next_u[0] - u[0])
        sxy = face_order[1] - face_shear * (next_u[1] - u[1])
        sxz = face_order[2] - face_shear * (next_u[2] - u[2])
        heat = face_order[3] - 3.75 * face_shear * (following(t) - t)
        work = 0.5 * (
            sxx * (u[0] + next_u[0]) + sxy * (u[1] + next_u[1]) + sxz * (u[2] + next_u[2])
        )
        viscous = [None, sxx, sxy, sxz, work + heat]
        out = []
        for i in range(5):
            spread = signal * w[i]
            total = 0.5 * ((euler[i] + spread) + following(euler[i] - spread))
            if viscous[i] is not None:
                total = total + viscous[i]
            out.append(w[i] - step * (total - preceding(total)))
        return out

    w = sweep(w, u, t, shear)
    u, uu, t = primitives(w)
    w = sweep(w, u, t, SHEAR_REFERENCE * power(t, SHEAR_EXPONENT))
    u, uu, t = primitives(w)
    n = w[0]

    for row, field in enumerate([n, u[0], u[1], u[2], t, q[0], q[1], q[2]]):
        macro_ref[pl.ds(row, blocks, stride=8), :] = field

    inverse = 1.0 / t
    relax = n * power(t, 1.0 - SHEAR_EXPONENT)
    damp = 1.0 / (1.0 + relax)
    scale = n * inverse * lax.rsqrt(t) * relax * damp
    beta = scale * ((1.0 - CONDUCTIVE_SHARE) / 5.0) * inverse * inverse / n
    cubic = beta * inverse
    qu = q[0] * u[0] + q[1] * u[1] + q[2] * u[2]
    offset = beta * (uu * inverse - 5.0)
    twice = 2.0 * cubic
    zz = q[2] * u[2]
    polynomial = [
        scale - qu * offset,
        offset * q[0] + twice * qu * u[0],
        offset * q[1] + twice * qu * u[1],
        offset * q[2] + twice * qu * u[2],
        -cubic * (qu + 2.0 * zz),
        -twice * (q[0] * u[0] - zz),
        -twice * (q[0] * u[1] + q[1] * u[0]),
        -twice * (q[0] * u[2] + q[2] * u[0]),
        -twice * (q[1] * u[1] - zz),
        -twice * (q[1] * u[2] + q[2] * u[1]),
        cubic * q[0],
        cubic * q[1],
        cubic * q[2],
    ]
    zero = jnp.zeros_like(n)
    rate = (0.5 * LOG2E) * inverse
    exponent = [-rate * uu, 2.0 * rate * u[0], 2.0 * rate * u[1], 2.0 * rate * u[2], -rate]
    rows = polynomial + [damp, zero, zero] + exponent + [zero, zero, zero]
    for row, field in enumerate(rows):
        coef_ref[pl.ds(row, blocks, stride=COEF), :] = field


def fluid_call(moments):
    blocks = moments.shape[0] // SENT
    return pl.pallas_call(
        fluid_kernel,
        out_shape=(
            pltpu.VMEM((blocks * COEF, LANES), jnp.float32),
            pltpu.VMEM((blocks * 8, LANES), jnp.float32),
        ),
        in_specs=[WHOLE],
        out_specs=(WHOLE, WHOLE),
        compiler_params=params(8),
        name="fluid",
    )(moments)


def relaxed(g, coef_ref, basis, tile):
    per_tile = TILE // LANES
    parts = [
        coef_ref[pl.ds((tile * per_tile + part) * COEF, COEF), :]
        for part in range(per_tile)
    ]
    coefficients = jnp.concatenate(parts, axis=1)
    polynomial = dot(basis, expand(coefficients[:BASIS]))
    rows = jnp.concatenate([coefficients[BASIS:], jnp.zeros((8, TILE), jnp.float32)], axis=0)
    exponent = dot(basis, expand(rows))
    return g * coefficients[DAMP : DAMP + 1] + jnp.exp2(exponent) * polynomial


def gathered(g_refs, here):
    return jnp.concatenate([ref[:, here] for ref in g_refs], axis=0)


def update_kernel(*refs):
    g_refs = refs[:PARTS]
    coef_ref, basis_ref, table_ref, f_ref, moments_ref = refs[PARTS:]
    cells = f_ref.shape[1]

    def front(tile):
        here = pl.ds(tile * TILE, TILE)
        return relaxed(gathered(g_refs, here), coef_ref, basis_ref[...], tile)

    def back(tile, values):
        f_ref[:, tile * TILE : (tile + 1) * TILE] = values
        store_moments(moments_ref, table_ref[...], values, tile, cells // LANES)

    values = front(0)
    for tile in range(1, cells // TILE):
        upcoming = front(tile)
        back(tile - 1, values)
        values = upcoming
    back(cells // TILE - 1, values)


def update_call(g, coefficients, basis, table):
    rows, cells = g[0].shape
    return pl.pallas_call(
        update_kernel,
        out_shape=(
            pltpu.VMEM((rows * PARTS, cells), jnp.float32),
            pltpu.VMEM((SENT * cells // LANES, LANES), jnp.float32),
        ),
        in_specs=[WHOLE] * (PARTS + 3),
        out_specs=(WHOLE, WHOLE),
        compiler_params=params(8),
        name="update",
    )(*[near(part) for part in g], near(coefficients), near(basis), near(table))


def finish_kernel(*refs):
    g_refs = refs[:PARTS]
    coef_ref, macro_ref, basis_ref, f_ref, fields_ref, held, sems = refs[PARTS:]
    cells = held.shape[1]
    width = cells // CHUNKS
    copies = []
    for chunk in range(CHUNKS):
        for local in range(width // TILE):
            tile = chunk * (width // TILE) + local
            here = pl.ds(tile * TILE, TILE)
            held[:, here] = relaxed(gathered(g_refs, here), coef_ref, basis_ref[...], tile)
            for block in range(tile * TILE // LANES, (tile + 1) * TILE // LANES):
                fields_ref[:, pl.ds(block * LANES, LANES)] = macro_ref[pl.ds(block * 8, 8), :]
        there = pl.ds(chunk * width, width)
        copy = pltpu.make_async_copy(held.at[:, there], f_ref.at[:, there], sems.at[chunk])
        copy.start()
        copies.append(copy)
    for copy in copies:
        copy.wait()


def finish_call(g, coefficients, macro, basis):
    rows, cells = g[0].shape
    return pl.pallas_call(
        finish_kernel,
        out_shape=(
            jax.ShapeDtypeStruct((rows * PARTS, cells), jnp.float32),
            jax.ShapeDtypeStruct((8, cells), jnp.float32),
        ),
        in_specs=[WHOLE] * (PARTS + 3),
        out_specs=(OUTSIDE, WHOLE),
        scratch_shapes=[
            pltpu.VMEM((rows * PARTS, cells), jnp.float32),
            pltpu.SemaphoreType.DMA((CHUNKS,)),
        ],
        compiler_params=params(16),
        name="finish",
    )(*[near(part) for part in g], near(coefficients), near(macro), near(basis))


def add_kernel(left_ref, right_ref, out_ref):
    out_ref[...] = left_ref[...] + right_ref[...]


def add_call(left, right):
    return pl.pallas_call(
        add_kernel,
        out_shape=pltpu.VMEM(left.shape, left.dtype),
        in_specs=[WHOLE, WHOLE],
        out_specs=WHOLE,
        compiler_params=params(1),
        name="add",
    )(near(left), near(right))


def plan(count):
    strides = [1 << bit for bit in range(count.bit_length() - 1)]
    return strides[:2], strides[2:]


def swap(values, count, stride):
    return lax.ppermute(values, "vel", [(device, device ^ stride) for device in range(count)])


def staged_sum(values, count, sides, f, tasks):
    splits, sums = plan(count)
    results, waiting = [], list(tasks)

    def exchange(block, stride, sent):
        if stride == 1 or not waiting:
            return block, swap(sent, count, stride)
        block, sent, held = lax.optimization_barrier((block, sent, f))
        made = waiting.pop(0)(held)
        block, got, made = lax.optimization_barrier((block, swap(sent, count, stride), made))
        results.append(made)
        return block, got

    block = values
    for stride, lower_side in zip(splits, sides):
        half = block.shape[0] // 2
        first, second = block[:half], block[half:]
        kept, sent = jnp.where(lower_side, first, second), jnp.where(lower_side, second, first)
        kept, got = exchange(kept, stride, sent)
        block = kept + got
    for stride in sums:
        block, got = exchange(block, stride, block)
        block = add_call(block, got)
    for stride, lower_side in reversed(list(zip(splits, sides))):
        block, got = exchange(block, stride, block)
        lower, upper = jnp.where(lower_side, block, got), jnp.where(lower_side, got, block)
        block = jnp.concatenate([lower, upper], axis=0)
    for task in waiting:
        results.append(task(f))
    return block, results


def on_device(velocities, density, flow, thermal, deviation):
    count = lax.axis_size("vel")
    place = lax.axis_index("vel")
    sides = [place & stride == 0 for stride in plan(count)[0]]
    velocities, sides = lax.optimization_barrier((velocities, sides))
    f, moments, basis, table, stream = start_call(
        velocities, density, flow, thermal, deviation, velocities.shape[1] * count
    )
    for iteration in range(ITERS):
        tasks = [
            functools.partial(lambda held, part: transport_call(stream, held, part), part=part)
            for part in range(PARTS)
        ]
        summed, g = staged_sum(moments, count, sides, f, tasks)
        coefficients, macro = fluid_call(summed)
        if iteration < ITERS - 1:
            f, moments = update_call(g, coefficients, basis, table)
    return finish_call(g, coefficients, macro, basis)


def solution(mesh):
    return jax.shard_map(
        on_device,
        mesh=mesh,
        in_specs=(P(None, "vel"), P("grp"), P(None, "grp"), P("grp"), P("vel", "grp")),
        out_specs=(P("vel", "grp"), P(None, "grp")),
        check_vma=False,
    )
```

```python
import functools

import jax
import jax.numpy as jnp
from jax import lax
from jax.experimental import pallas as pl
from jax.experimental.pallas import tpu as pltpu
from jax.sharding import PartitionSpec as P

ITERS = 2

ADIABATIC_INDEX = 5.0 / 3.0
CONDUCTIVE_SHARE = 2.0 / 3.0
SHEAR_EXPONENT = 0.81
SHEAR_REFERENCE = 0.05
KINETIC_STEP = 0.05
COURANT = 0.4
SPREAD_SCALE = 1.5

LOG2E = 1.4426950408889634
LANES = 128
TILE = 256
BASIS = 16
SENT = 13
COEF = 24
DAMP = 13
CHUNKS = 8
PARTS = 8
BESIDE = (1, 2, 1, 2, 1, 1)
MIB = 1024 * 1024

WHOLE = pl.BlockSpec(memory_space=pltpu.VMEM)
OUTSIDE = pl.BlockSpec(memory_space=pltpu.HBM)


def params(mebibytes):
    return pltpu.CompilerParams(vmem_limit_bytes=mebibytes * MIB)


def near(values):
    return pltpu.with_memory_space_constraint(values, pltpu.VMEM)


def far(values):
    return pltpu.with_memory_space_constraint(values, pltpu.HBM)


def dot(left, right):
    return jnp.dot(left, right, preferred_element_type=jnp.float32)


def rounded(values):
    return values.astype(jnp.bfloat16).astype(jnp.float32)


def phi_rows(velocities):
    vx, vy, vz = velocities[0:1], velocities[1:2], velocities[2:3]
    sq = vx * vx + vy * vy + vz * vz
    zero = jnp.zeros_like(vx)
    rows = [
        jnp.ones_like(vx), vx, vy, vz, sq, vx * vx, vx * vy, vx * vz, vy * vy, vy * vz,
        vx * sq, vy * sq, vz * sq, zero, zero, zero,
    ]
    return jnp.concatenate(rows, axis=0), sq


def make_tables(velocities, total_count):
    phi, sq = phi_rows(velocities)
    high = rounded(phi)
    middle = rounded(phi - high)
    low = phi - high - middle
    stacked = jnp.concatenate(
        [high, high, high, middle, middle, low, jnp.zeros((32, phi.shape[1]), jnp.float32)], axis=0
    )
    basis = stacked.T.astype(jnp.bfloat16)
    weighted = phi * (SPREAD_SCALE**3 * jnp.exp(sq / (2.0 * SPREAD_SCALE**2)) / total_count)
    top = rounded(weighted)
    rest = weighted - top
    moments = jnp.concatenate(
        [
            jnp.concatenate([top, top], axis=1),
            jnp.concatenate([rest, jnp.zeros_like(rest)], axis=1),
        ],
        axis=0,
    ).astype(jnp.bfloat16)
    return basis, moments


def expand(coefficients):
    high = coefficients.astype(jnp.bfloat16)
    rest = coefficients - high.astype(jnp.float32)
    middle = rest.astype(jnp.bfloat16)
    low = (rest - middle.astype(jnp.float32)).astype(jnp.bfloat16)
    zero = jnp.zeros((32, coefficients.shape[1]), jnp.bfloat16)
    return jnp.concatenate([high, middle, low, high, middle, high, zero], axis=0)


def store_moments(moments_ref, table, values, tile, blocks):
    high = values.astype(jnp.bfloat16)
    low = (values - high.astype(jnp.float32)).astype(jnp.bfloat16)
    both = dot(table, jnp.concatenate([high, low], axis=0))
    sums = both[:BASIS] + both[BASIS:]
    per_tile = TILE // LANES
    for part in range(per_tile):
        block = tile * per_tile + part
        moments_ref[pl.ds(block, SENT, stride=blocks), :] = sums[
            :SENT, part * LANES : (part + 1) * LANES
        ]


def start_kernel(
    total_count,
    vel_hbm, density_hbm, flow_hbm, thermal_hbm, deviation_hbm,
    f_ref, moments_ref, basis_ref, table_ref, stream_ref,
    vel_ref, density_ref, flow_ref, thermal_ref, deviation_ref, small_sems, sems,
):
    cells = f_ref.shape[1]
    width = cells // CHUNKS
    small = [
        pltpu.make_async_copy(source, target, small_sems.at[number])
        for number, (source, target) in enumerate(
            [
                (vel_hbm, vel_ref),
                (density_hbm, density_ref),
                (flow_hbm, flow_ref),
                (thermal_hbm, thermal_ref),
            ]
        )
    ]
    for copy in small:
        copy.start()
    copies = [
        pltpu.make_async_copy(
            deviation_hbm.at[:, pl.ds(chunk * width, width)],
            deviation_ref.at[:, pl.ds(chunk * width, width)],
            sems.at[chunk],
        )
        for chunk in range(CHUNKS)
    ]
    for copy in copies:
        copy.start()
    small[0].wait()
    basis, table = make_tables(vel_ref[...], total_count)
    basis_ref[...] = basis
    table_ref[...] = table
    stream_ref[...] = jnp.broadcast_to(vel_ref[0:1, :], (LANES, vel_ref.shape[1])).T
    for copy in small[1:]:
        copy.wait()
    for chunk in range(CHUNKS):
        copies[chunk].wait()

        def step(local, carry, chunk=chunk):
            tile = chunk * (width // TILE) + local
            here = pl.ds(pl.multiple_of(tile * TILE, TILE), TILE)
            density, flow, thermal = density_ref[:, here], flow_ref[:, here], thermal_ref[:, here]
            rate = (0.5 * LOG2E) / thermal
            speed_sq = flow[0:1] * flow[0:1] + flow[1:2] * flow[1:2] + flow[2:3] * flow[2:3]
            rows = [-rate * speed_sq, 2.0 * rate * flow, -rate, jnp.zeros((11, TILE), jnp.float32)]
            exponent = dot(basis_ref[...], expand(jnp.concatenate(rows, axis=0)))
            scale = density / (thermal * jnp.sqrt(thermal))
            values = jnp.exp2(exponent) * (scale * (1.0 + deviation_ref[:, here]))
            f_ref[:, here] = values
            store_moments(moments_ref, table_ref[...], values, tile, cells // LANES)
            return carry

        lax.fori_loop(0, width // TILE, step, 0, unroll=True)


def start_call(velocities, density, flow, thermal, deviation, total_count):
    local, cells = deviation.shape
    return pl.pallas_call(
        functools.partial(start_kernel, total_count),
        out_shape=(
            pltpu.VMEM((local, cells), jnp.float32),
            pltpu.VMEM((SENT * cells // LANES, LANES), jnp.float32),
            pltpu.VMEM((local, 128), jnp.bfloat16),
            pltpu.VMEM((2 * BASIS, 2 * local), jnp.bfloat16),
            pltpu.VMEM((local, LANES), jnp.float32),
        ),
        in_specs=[OUTSIDE] * 5,
        out_specs=(WHOLE,) * 5,
        scratch_shapes=[
            pltpu.VMEM((3, local), jnp.float32),
            pltpu.VMEM((1, cells), jnp.float32),
            pltpu.VMEM((3, cells), jnp.float32),
            pltpu.VMEM((1, cells), jnp.float32),
            pltpu.VMEM((local, cells), jnp.float32),
            pltpu.SemaphoreType.DMA((4,)),
            pltpu.SemaphoreType.DMA((CHUNKS,)),
        ],
        compiler_params=params(16),
        name="start",
    )(
        far(velocities),
        far(density.reshape(1, cells)),
        far(flow),
        far(thermal.reshape(1, cells)),
        far(deviation),
    )


def transport_kernel(first_row, stream_ref, f_ref, g_ref):
    rows, cells = g_ref.shape
    blocks = cells // LANES
    lane = lax.broadcasted_iota(jnp.int32, (8, LANES), 1)
    at_first, at_last = lane == 0, lane == LANES - 1
    lag = 4

    def row_step(row_tile, carry):
        source = pl.ds(pl.multiple_of(first_row + row_tile * 8, 8), 8)
        target = pl.ds(pl.multiple_of(row_tile * 8, 8), 8)
        stream = stream_ref[source, :]
        upward = stream > 0
        rate = KINETIC_STEP * jnp.abs(stream)
        half = jnp.where(upward, 0.5, -0.5)
        x, up, rise, down, face, face_up, face_down = {}, {}, {}, {}, {}, {}, {}

        def load(b):
            at = (b % blocks) * LANES
            x[b] = f_ref[source, at : at + LANES]
            up[b] = pltpu.roll(x[b], 1, 1)

        def slope_in(b):
            rise[b] = x[b] - jnp.where(at_first, up[b - 1], up[b])
            down[b] = pltpu.roll(rise[b], LANES - 1, 1)

        def reconstruct(b):
            ahead = jnp.where(at_last, down[b + 1], down[b])
            slope = jnp.maximum(jnp.minimum(rise[b], ahead), 0.0) + jnp.minimum(
                jnp.maximum(rise[b], ahead), 0.0
            )
            face[b] = x[b] + half * slope
            face_up[b] = pltpu.roll(face[b], 1, 1)
            face_down[b] = pltpu.roll(face[b], LANES - 1, 1)

        def store(b):
            other = jnp.where(
                upward,
                jnp.where(at_first, face_up[b - 1], face_up[b]),
                jnp.where(at_last, face_down[b + 1], face_down[b]),
            )
            g_ref[target, b * LANES : (b + 1) * LANES] = x[b] - rate * (face[b] - other)

        for k in range(-2, blocks + 3 * lag + 4):
            for act, behind, low, high in (
                (load, 0, -2, blocks + 1),
                (slope_in, lag, -1, blocks + 1),
                (reconstruct, 2 * lag + 1, -1, blocks),
                (store, 3 * lag + 2, 0, blocks - 1),
            ):
                if low <= k - behind <= high:
                    act(k - behind)
        return carry

    lax.fori_loop(0, rows // 8, row_step, 0)


def transport_call(stream, f, part):
    local, cells = f.shape
    rows = local // PARTS
    return pl.pallas_call(
        functools.partial(transport_kernel, part * rows),
        out_shape=pltpu.VMEM((rows, cells), jnp.float32),
        in_specs=[WHOLE, WHOLE],
        out_specs=WHOLE,
        compiler_params=params(4),
        name="transport",
    )(near(stream), near(f))


def fluid_kernel(moments_ref, coef_ref, macro_ref):
    blocks = moments_ref.shape[0] // SENT
    m = [moments_ref[row * blocks : (row + 1) * blocks, :] for row in range(13)]
    lane = lax.broadcasted_iota(jnp.int32, (blocks, LANES), 1)

    def following(x):
        turned = pltpu.roll(x, LANES - 1, 1)
        return jnp.where(lane == LANES - 1, pltpu.roll(turned, blocks - 1, 0), turned)

    def preceding(x):
        turned = pltpu.roll(x, 1, 1)
        return jnp.where(lane == 0, pltpu.roll(turned, 1, 0), turned)

    def power(x, exponent):
        return jnp.exp2(exponent * jnp.log2(x))

    def primitives(w):
        inverse = 1.0 / w[0]
        u = [w[1] * inverse, w[2] * inverse, w[3] * inverse]
        uu = u[0] * u[0] + u[1] * u[1] + u[2] * u[2]
        t = (2.0 * w[4] * inverse - uu) * (1.0 / 3.0)
        return u, uu, t

    n = m[0]
    w = [n, m[1], m[2], m[3], 0.5 * m[4]]
    u, uu, t = primitives(w)
    p = n * t
    second = [[m[5], m[6], m[7]], [m[6], m[8], m[9]], [m[7], m[9], m[4] - m[5] - m[8]]]
    stress = [m[5] - m[1] * u[0] - p, m[6] - m[1] * u[1], m[7] - m[1] * u[2]]
    q = []
    for i in range(3):
        along = second[i][0] * u[0] + second[i][1] * u[1] + second[i][2] * u[2]
        q.append(0.5 * (m[10 + i] - u[i] * m[4] - 2.0 * along + 2.0 * n * u[i] * uu))

    shear = SHEAR_REFERENCE * power(t, SHEAR_EXPONENT)
    high_order = [
        stress[i] + ((4.0 / 3.0 if i == 0 else 1.0) * 0.5) * shear * (following(u[i]) - preceding(u[i]))
        for i in range(3)
    ]
    high_order.append(q[0] + (3.75 * 0.5) * shear * (following(t) - preceding(t)))
    half_order = [0.5 * h for h in high_order]
    face_order = [h + following(h) for h in half_order]

    def sweep(w, u, t, shear):
        rates = jnp.abs(u[0]) + jnp.sqrt(ADIABATIC_INDEX * t)
        signal = jnp.max(jnp.max(rates, axis=0, keepdims=True), axis=1, keepdims=True)
        step = COURANT / signal
        p = w[0] * t
        euler = [w[1], w[1] * u[0] + p, w[1] * u[1], w[1] * u[2], (w[4] + p) * u[0]]
        next_u = [following(x) for x in u]
        half_shear = 0.5 * shear
        face_shear = half_shear + following(half_shear)
        sxx = face_order[0] - (4.0 / 3.0) * face_shear * (next_u[0] - u[0])
        sxy = face_order[1] - face_shear * (next_u[1] - u[1])
        sxz = face_order[2] - face_shear * (next_u[2] - u[2])
        heat = face_order[3] - 3.75 * face_shear * (following(t) - t)
        work = 0.5 * (
            sxx * (u[0] + next_u[0]) + sxy * (u[1] + next_u[1]) + sxz * (u[2] + next_u[2])
        )
        viscous = [None, sxx, sxy, sxz, work + heat]
        out = []
        for i in range(5):
            spread = signal * w[i]
            total = 0.5 * ((euler[i] + spread) + following(euler[i] - spread))
            if viscous[i] is not None:
                total = total + viscous[i]
            out.append(w[i] - step * (total - preceding(total)))
        return out

    w = sweep(w, u, t, shear)
    u, uu, t = primitives(w)
    w = sweep(w, u, t, SHEAR_REFERENCE * power(t, SHEAR_EXPONENT))
    u, uu, t = primitives(w)
    n = w[0]

    for row, field in enumerate([n, u[0], u[1], u[2], t, q[0], q[1], q[2]]):
        macro_ref[pl.ds(row, blocks, stride=8), :] = field

    inverse = 1.0 / t
    relax = n * power(t, 1.0 - SHEAR_EXPONENT)
    damp = 1.0 / (1.0 + relax)
    scale = n * inverse * lax.rsqrt(t) * relax * damp
    beta = scale * ((1.0 - CONDUCTIVE_SHARE) / 5.0) * inverse * inverse / n
    cubic = beta * inverse
    qu = q[0] * u[0] + q[1] * u[1] + q[2] * u[2]
    offset = beta * (uu * inverse - 5.0)
    twice = 2.0 * cubic
    zz = q[2] * u[2]
    polynomial = [
        scale - qu * offset,
        offset * q[0] + twice * qu * u[0],
        offset * q[1] + twice * qu * u[1],
        offset * q[2] + twice * qu * u[2],
        -cubic * (qu + 2.0 * zz),
        -twice * (q[0] * u[0] - zz),
        -twice * (q[0] * u[1] + q[1] * u[0]),
        -twice * (q[0] * u[2] + q[2] * u[0]),
        -twice * (q[1] * u[1] - zz),
        -twice * (q[1] * u[2] + q[2] * u[1]),
        cubic * q[0],
        cubic * q[1],
        cubic * q[2],
    ]
    zero = jnp.zeros_like(n)
    rate = (0.5 * LOG2E) * inverse
    exponent = [-rate * uu, 2.0 * rate * u[0], 2.0 * rate * u[1], 2.0 * rate * u[2], -rate]
    rows = polynomial + [damp, zero, zero] + exponent + [zero, zero, zero]
    for row, field in enumerate(rows):
        coef_ref[pl.ds(row, blocks, stride=COEF), :] = field


def fluid_call(moments):
    blocks = moments.shape[0] // SENT
    return pl.pallas_call(
        fluid_kernel,
        out_shape=(
            pltpu.VMEM((blocks * COEF, LANES), jnp.float32),
            pltpu.VMEM((blocks * 8, LANES), jnp.float32),
        ),
        in_specs=[WHOLE],
        out_specs=(WHOLE, WHOLE),
        compiler_params=params(8),
        name="fluid",
    )(moments)


def relaxed(g, coef_ref, basis, tile):
    per_tile = TILE // LANES
    parts = [
        coef_ref[pl.ds((tile * per_tile + part) * COEF, COEF), :]
        for part in range(per_tile)
    ]
    coefficients = jnp.concatenate(parts, axis=1)
    polynomial = dot(basis, expand(coefficients[:BASIS]))
    rows = jnp.concatenate([coefficients[BASIS:], jnp.zeros((8, TILE), jnp.float32)], axis=0)
    exponent = dot(basis, expand(rows))
    return g * coefficients[DAMP : DAMP + 1] + jnp.exp2(exponent) * polynomial


def gathered(g_refs, here):
    return jnp.concatenate([ref[:, here] for ref in g_refs], axis=0)


def update_kernel(*refs):
    g_refs = refs[:PARTS]
    coef_ref, basis_ref, table_ref, f_ref, moments_ref = refs[PARTS:]
    cells = f_ref.shape[1]

    def front(tile):
        here = pl.ds(tile * TILE, TILE)
        return relaxed(gathered(g_refs, here), coef_ref, basis_ref[...], tile)

    def back(tile, values):
        f_ref[:, tile * TILE : (tile + 1) * TILE] = values
        store_moments(moments_ref, table_ref[...], values, tile, cells // LANES)

    values = front(0)
    for tile in range(1, cells // TILE):
        upcoming = front(tile)
        back(tile - 1, values)
        values = upcoming
    back(cells // TILE - 1, values)


def update_call(g, coefficients, basis, table):
    rows, cells = g[0].shape
    return pl.pallas_call(
        update_kernel,
        out_shape=(
            pltpu.VMEM((rows * PARTS, cells), jnp.float32),
            pltpu.VMEM((SENT * cells // LANES, LANES), jnp.float32),
        ),
        in_specs=[WHOLE] * (PARTS + 3),
        out_specs=(WHOLE, WHOLE),
        compiler_params=params(8),
        name="update",
    )(*[near(part) for part in g], near(coefficients), near(basis), near(table))


def finish_kernel(*refs):
    g_refs = refs[:PARTS]
    coef_ref, macro_ref, basis_ref, f_ref, fields_ref, held, sems = refs[PARTS:]
    cells = held.shape[1]
    width = cells // CHUNKS
    copies = []
    for chunk in range(CHUNKS):
        for local in range(width // TILE):
            tile = chunk * (width // TILE) + local
            here = pl.ds(tile * TILE, TILE)
            held[:, here] = relaxed(gathered(g_refs, here), coef_ref, basis_ref[...], tile)
            for block in range(tile * TILE // LANES, (tile + 1) * TILE // LANES):
                fields_ref[:, pl.ds(block * LANES, LANES)] = macro_ref[pl.ds(block * 8, 8), :]
        there = pl.ds(chunk * width, width)
        copy = pltpu.make_async_copy(held.at[:, there], f_ref.at[:, there], sems.at[chunk])
        copy.start()
        copies.append(copy)
    for copy in copies:
        copy.wait()


def finish_call(g, coefficients, macro, basis):
    rows, cells = g[0].shape
    return pl.pallas_call(
        finish_kernel,
        out_shape=(
            jax.ShapeDtypeStruct((rows * PARTS, cells), jnp.float32),
            jax.ShapeDtypeStruct((8, cells), jnp.float32),
        ),
        in_specs=[WHOLE] * (PARTS + 3),
        out_specs=(OUTSIDE, WHOLE),
        scratch_shapes=[
            pltpu.VMEM((rows * PARTS, cells), jnp.float32),
            pltpu.SemaphoreType.DMA((CHUNKS,)),
        ],
        compiler_params=params(16),
        name="finish",
    )(*[near(part) for part in g], near(coefficients), near(macro), near(basis))


def add_kernel(left_ref, right_ref, out_ref):
    out_ref[...] = left_ref[...] + right_ref[...]


def add_call(left, right):
    return pl.pallas_call(
        add_kernel,
        out_shape=pltpu.VMEM(left.shape, left.dtype),
        in_specs=[WHOLE, WHOLE],
        out_specs=WHOLE,
        compiler_params=params(1),
        name="add",
    )(near(left), near(right))


def plan(count):
    strides = [1 << bit for bit in range(count.bit_length() - 1)]
    return strides[:2], strides[2:]


def swap(values, count, stride):
    return lax.ppermute(values, "vel", [(device, device ^ stride) for device in range(count)])


def staged_sum(values, count, sides, f, tasks):
    splits, sums = plan(count)
    results, waiting, portions = [], list(tasks), list(BESIDE)

    def exchange(chunks, stride):
        got = [swap(chunk, count, stride) for chunk in chunks]
        portion = portions.pop(0) if portions else 0
        if portion:
            _, held = lax.optimization_barrier((chunks[-1], f))
            made = [task(held) for task in waiting[:portion]]
            del waiting[:portion]
            got[0], made = lax.optimization_barrier((got[0], made))
            results.extend(made)
        return got

    def split(chunks, stride, lower_side):
        kept, sent = [], []
        for chunk in chunks:
            half = chunk.shape[0] // 2
            first, second = chunk[:half], chunk[half:]
            kept.append(jnp.where(lower_side, first, second))
            sent.append(jnp.where(lower_side, second, first))
        sent = lax.optimization_barrier(sent)
        got = exchange(sent, stride)
        if len(chunks) == 1:
            return [kept[0] + got[0]]
        return [add_call(own, other) for own, other in zip(kept, got)]

    def join(chunks, stride, lower_side):
        out = []
        for own, got in zip(chunks, exchange(chunks, stride)):
            lower = jnp.where(lower_side, own, got)
            upper = jnp.where(lower_side, got, own)
            out.append((lower, upper))
        return out

    (block,) = split([values], splits[0], sides[0])
    half = block.shape[0] // 2
    chunks = [block[:half], block[half:]]
    for stride, lower_side in zip(splits[1:], sides[1:]):
        chunks = split(chunks, stride, lower_side)
    for stride in sums:
        chunks = [add_call(own, got) for own, got in zip(chunks, exchange(chunks, stride))]
    for stride, lower_side in reversed(list(zip(splits[1:], sides[1:]))):
        chunks = [jnp.concatenate(both, axis=0) for both in join(chunks, stride, lower_side)]
    lowers, uppers = zip(*join(chunks, splits[0], sides[0]))
    results.extend(task(f) for task in waiting)
    return jnp.concatenate(lowers + uppers, axis=0), results


def on_device(velocities, density, flow, thermal, deviation):
    count = lax.axis_size("vel")
    place = lax.axis_index("vel")
    sides = [place & stride == 0 for stride in plan(count)[0]]
    velocities, sides = lax.optimization_barrier((velocities, sides))
    f, moments, basis, table, stream = start_call(
        velocities, density, flow, thermal, deviation, velocities.shape[1] * count
    )
    for iteration in range(ITERS):
        tasks = [
            functools.partial(lambda held, part: transport_call(stream, held, part), part=part)
            for part in range(PARTS)
        ]
        summed, g = staged_sum(moments, count, sides, f, tasks)
        coefficients, macro = fluid_call(summed)
        if iteration < ITERS - 1:
            f, moments = update_call(g, coefficients, basis, table)
    return finish_call(g, coefficients, macro, basis)


def solution(mesh):
    return jax.shard_map(
        on_device,
        mesh=mesh,
        in_specs=(P(None, "vel"), P("grp"), P(None, "grp"), P("grp"), P("vel", "grp")),
        out_specs=(P("vel", "grp"), P(None, "grp")),
        check_vma=False,
    )
```

```python
import functools

import jax
import jax.numpy as jnp
from jax import lax
from jax.experimental import pallas as pl
from jax.experimental.pallas import tpu as pltpu
from jax.sharding import PartitionSpec as P

ITERS = 2

ADIABATIC_INDEX = 5.0 / 3.0
CONDUCTIVE_SHARE = 2.0 / 3.0
SHEAR_EXPONENT = 0.81
SHEAR_REFERENCE = 0.05
KINETIC_STEP = 0.05
COURANT = 0.4
SPREAD_SCALE = 1.5

LOG2E = 1.4426950408889634
LANES = 128
TILE = 256
BASIS = 16
SENT = 13
COEF = 24
DAMP = 13
CHUNKS = 8
PARTS = 8
BESIDE = (1, 2, 1, 2, 1, 1)
MIB = 1024 * 1024

WHOLE = pl.BlockSpec(memory_space=pltpu.VMEM)
OUTSIDE = pl.BlockSpec(memory_space=pltpu.HBM)


def params(mebibytes):
    return pltpu.CompilerParams(vmem_limit_bytes=mebibytes * MIB)


def near(values):
    return pltpu.with_memory_space_constraint(values, pltpu.VMEM)


def far(values):
    return pltpu.with_memory_space_constraint(values, pltpu.HBM)


def dot(left, right):
    return jnp.dot(left, right, preferred_element_type=jnp.float32)


def rounded(values):
    return values.astype(jnp.bfloat16).astype(jnp.float32)


def phi_rows(velocities):
    vx, vy, vz = velocities[0:1], velocities[1:2], velocities[2:3]
    sq = vx * vx + vy * vy + vz * vz
    zero = jnp.zeros_like(vx)
    rows = [
        jnp.ones_like(vx), vx, vy, vz, sq, vx * vx, vx * vy, vx * vz, vy * vy, vy * vz,
        vx * sq, vy * sq, vz * sq, zero, zero, zero,
    ]
    return jnp.concatenate(rows, axis=0), sq


def make_tables(velocities, total_count):
    phi, sq = phi_rows(velocities)
    high = rounded(phi)
    middle = rounded(phi - high)
    low = phi - high - middle
    stacked = jnp.concatenate(
        [high, high, high, middle, middle, low, jnp.zeros((32, phi.shape[1]), jnp.float32)], axis=0
    )
    basis = stacked.T.astype(jnp.bfloat16)
    weighted = phi * (SPREAD_SCALE**3 * jnp.exp(sq / (2.0 * SPREAD_SCALE**2)) / total_count)
    top = rounded(weighted)
    rest = weighted - top
    moments = jnp.concatenate(
        [
            jnp.concatenate([top, top], axis=1),
            jnp.concatenate([rest, jnp.zeros_like(rest)], axis=1),
        ],
        axis=0,
    ).astype(jnp.bfloat16)
    return basis, moments


def expand(coefficients):
    high = coefficients.astype(jnp.bfloat16)
    rest = coefficients - high.astype(jnp.float32)
    middle = rest.astype(jnp.bfloat16)
    low = (rest - middle.astype(jnp.float32)).astype(jnp.bfloat16)
    zero = jnp.zeros((32, coefficients.shape[1]), jnp.bfloat16)
    return jnp.concatenate([high, middle, low, high, middle, high, zero], axis=0)


def store_moments(moments_ref, table, values, tile, blocks):
    high = values.astype(jnp.bfloat16)
    low = (values - high.astype(jnp.float32)).astype(jnp.bfloat16)
    both = dot(table, jnp.concatenate([high, low], axis=0))
    sums = both[:BASIS] + both[BASIS:]
    per_tile = TILE // LANES
    for part in range(per_tile):
        block = tile * per_tile + part
        moments_ref[pl.ds(block, SENT, stride=blocks), :] = sums[
            :SENT, part * LANES : (part + 1) * LANES
        ]


def start_kernel(
    total_count,
    vel_hbm, density_hbm, flow_hbm, thermal_hbm, deviation_hbm,
    f_ref, moments_ref, basis_ref, table_ref, stream_ref,
    vel_ref, density_ref, flow_ref, thermal_ref, deviation_ref, small_sems, sems,
):
    cells = f_ref.shape[1]
    width = cells // CHUNKS
    small = [
        pltpu.make_async_copy(source, target, small_sems.at[number])
        for number, (source, target) in enumerate(
            [
                (vel_hbm, vel_ref),
                (density_hbm, density_ref),
                (flow_hbm, flow_ref),
                (thermal_hbm, thermal_ref),
            ]
        )
    ]
    for copy in small:
        copy.start()
    copies = [
        pltpu.make_async_copy(
            deviation_hbm.at[:, pl.ds(chunk * width, width)],
            deviation_ref.at[:, pl.ds(chunk * width, width)],
            sems.at[chunk],
        )
        for chunk in range(CHUNKS)
    ]
    for copy in copies:
        copy.start()
    small[0].wait()
    basis, table = make_tables(vel_ref[...], total_count)
    basis_ref[...] = basis
    table_ref[...] = table
    stream_ref[...] = jnp.broadcast_to(vel_ref[0:1, :], (LANES, vel_ref.shape[1])).T
    for copy in small[1:]:
        copy.wait()
    for chunk in range(CHUNKS):
        copies[chunk].wait()

        def step(local, carry, chunk=chunk):
            tile = chunk * (width // TILE) + local
            here = pl.ds(pl.multiple_of(tile * TILE, TILE), TILE)
            density, flow, thermal = density_ref[:, here], flow_ref[:, here], thermal_ref[:, here]
            rate = (0.5 * LOG2E) / thermal
            speed_sq = flow[0:1] * flow[0:1] + flow[1:2] * flow[1:2] + flow[2:3] * flow[2:3]
            rows = [-rate * speed_sq, 2.0 * rate * flow, -rate, jnp.zeros((11, TILE), jnp.float32)]
            exponent = dot(basis_ref[...], expand(jnp.concatenate(rows, axis=0)))
            scale = density / (thermal * jnp.sqrt(thermal))
            values = jnp.exp2(exponent) * (scale * (1.0 + deviation_ref[:, here]))
            f_ref[:, here] = values
            store_moments(moments_ref, table_ref[...], values, tile, cells // LANES)
            return carry

        lax.fori_loop(0, width // TILE, step, 0, unroll=True)


def start_call(velocities, density, flow, thermal, deviation, total_count):
    local, cells = deviation.shape
    return pl.pallas_call(
        functools.partial(start_kernel, total_count),
        out_shape=(
            pltpu.VMEM((local, cells), jnp.float32),
            pltpu.VMEM((SENT * cells // LANES, LANES), jnp.float32),
            pltpu.VMEM((local, 128), jnp.bfloat16),
            pltpu.VMEM((2 * BASIS, 2 * local), jnp.bfloat16),
            pltpu.VMEM((local, LANES), jnp.float32),
        ),
        in_specs=[OUTSIDE] * 5,
        out_specs=(WHOLE,) * 5,
        scratch_shapes=[
            pltpu.VMEM((3, local), jnp.float32),
            pltpu.VMEM((1, cells), jnp.float32),
            pltpu.VMEM((3, cells), jnp.float32),
            pltpu.VMEM((1, cells), jnp.float32),
            pltpu.VMEM((local, cells), jnp.float32),
            pltpu.SemaphoreType.DMA((4,)),
            pltpu.SemaphoreType.DMA((CHUNKS,)),
        ],
        compiler_params=params(16),
        name="start",
    )(
        far(velocities),
        far(density.reshape(1, cells)),
        far(flow),
        far(thermal.reshape(1, cells)),
        far(deviation),
    )


def transport_kernel(first_row, stream_ref, f_ref, g_ref):
    rows, cells = g_ref.shape
    blocks = cells // LANES
    lane = lax.broadcasted_iota(jnp.int32, (8, LANES), 1)
    at_first, at_last = lane == 0, lane == LANES - 1
    lag = 4

    def row_step(row_tile, carry):
        source = pl.ds(pl.multiple_of(first_row + row_tile * 8, 8), 8)
        target = pl.ds(pl.multiple_of(row_tile * 8, 8), 8)
        stream = stream_ref[source, :]
        upward = stream > 0
        rate = KINETIC_STEP * jnp.abs(stream)
        half = jnp.where(upward, 0.5, -0.5)
        x, up, rise, down, face, face_up, face_down = {}, {}, {}, {}, {}, {}, {}

        def load(b):
            at = (b % blocks) * LANES
            x[b] = f_ref[source, at : at + LANES]
            up[b] = pltpu.roll(x[b], 1, 1)

        def slope_in(b):
            rise[b] = x[b] - jnp.where(at_first, up[b - 1], up[b])
            down[b] = pltpu.roll(rise[b], LANES - 1, 1)

        def reconstruct(b):
            ahead = jnp.where(at_last, down[b + 1], down[b])
            slope = jnp.maximum(jnp.minimum(rise[b], ahead), 0.0) + jnp.minimum(
                jnp.maximum(rise[b], ahead), 0.0
            )
            face[b] = x[b] + half * slope
            face_up[b] = pltpu.roll(face[b], 1, 1)
            face_down[b] = pltpu.roll(face[b], LANES - 1, 1)

        def store(b):
            other = jnp.where(
                upward,
                jnp.where(at_first, face_up[b - 1], face_up[b]),
                jnp.where(at_last, face_down[b + 1], face_down[b]),
            )
            g_ref[target, b * LANES : (b + 1) * LANES] = x[b] - rate * (face[b] - other)

        for k in range(-2, blocks + 3 * lag + 4):
            for act, behind, low, high in (
                (load, 0, -2, blocks + 1),
                (slope_in, lag, -1, blocks + 1),
                (reconstruct, 2 * lag + 1, -1, blocks),
                (store, 3 * lag + 2, 0, blocks - 1),
            ):
                if low <= k - behind <= high:
                    act(k - behind)
        return carry

    lax.fori_loop(0, rows // 8, row_step, 0)


def transport_call(stream, f, part):
    local, cells = f.shape
    rows = local // PARTS
    return pl.pallas_call(
        functools.partial(transport_kernel, part * rows),
        out_shape=pltpu.VMEM((rows, cells), jnp.float32),
        in_specs=[WHOLE, WHOLE],
        out_specs=WHOLE,
        compiler_params=params(4),
        name="transport",
    )(near(stream), near(f))


def fluid_kernel(moments_ref, coef_ref, macro_ref):
    blocks = moments_ref.shape[0] // SENT
    m = [moments_ref[row * blocks : (row + 1) * blocks, :] for row in range(13)]
    lane = lax.broadcasted_iota(jnp.int32, (blocks, LANES), 1)

    def following(x):
        turned = pltpu.roll(x, LANES - 1, 1)
        return jnp.where(lane == LANES - 1, pltpu.roll(turned, blocks - 1, 0), turned)

    def preceding(x):
        turned = pltpu.roll(x, 1, 1)
        return jnp.where(lane == 0, pltpu.roll(turned, 1, 0), turned)

    def power(x, exponent):
        return jnp.exp2(exponent * jnp.log2(x))

    def primitives(w):
        inverse = 1.0 / w[0]
        u = [w[1] * inverse, w[2] * inverse, w[3] * inverse]
        uu = u[0] * u[0] + u[1] * u[1] + u[2] * u[2]
        t = (2.0 * w[4] * inverse - uu) * (1.0 / 3.0)
        return u, uu, t

    n = m[0]
    w = [n, m[1], m[2], m[3], 0.5 * m[4]]
    u, uu, t = primitives(w)
    p = n * t
    second = [[m[5], m[6], m[7]], [m[6], m[8], m[9]], [m[7], m[9], m[4] - m[5] - m[8]]]
    stress = [m[5] - m[1] * u[0] - p, m[6] - m[1] * u[1], m[7] - m[1] * u[2]]
    q = []
    for i in range(3):
        along = second[i][0] * u[0] + second[i][1] * u[1] + second[i][2] * u[2]
        q.append(0.5 * (m[10 + i] - u[i] * m[4] - 2.0 * along + 2.0 * n * u[i] * uu))

    shear = SHEAR_REFERENCE * power(t, SHEAR_EXPONENT)
    high_order = [
        stress[i] + ((4.0 / 3.0 if i == 0 else 1.0) * 0.5) * shear * (following(u[i]) - preceding(u[i]))
        for i in range(3)
    ]
    high_order.append(q[0] + (3.75 * 0.5) * shear * (following(t) - preceding(t)))
    half_order = [0.5 * h for h in high_order]
    face_order = [h + following(h) for h in half_order]

    def sweep(w, u, t, shear):
        rates = jnp.abs(u[0]) + jnp.sqrt(ADIABATIC_INDEX * t)
        signal = jnp.max(jnp.max(rates, axis=0, keepdims=True), axis=1, keepdims=True)
        step = COURANT / signal
        p = w[0] * t
        euler = [w[1], w[1] * u[0] + p, w[1] * u[1], w[1] * u[2], (w[4] + p) * u[0]]
        next_u = [following(x) for x in u]
        half_shear = 0.5 * shear
        face_shear = half_shear + following(half_shear)
        sxx = face_order[0] - (4.0 / 3.0) * face_shear * (next_u[0] - u[0])
        sxy = face_order[1] - face_shear * (next_u[1] - u[1])
        sxz = face_order[2] - face_shear * (next_u[2] - u[2])
        heat = face_order[3] - 3.75 * face_shear * (following(t) - t)
        work = 0.5 * (
            sxx * (u[0] + next_u[0]) + sxy * (u[1] + next_u[1]) + sxz * (u[2] + next_u[2])
        )
        viscous = [None, sxx, sxy, sxz, work + heat]
        out = []
        for i in range(5):
            spread = signal * w[i]
            total = 0.5 * ((euler[i] + spread) + following(euler[i] - spread))
            if viscous[i] is not None:
                total = total + viscous[i]
            out.append(w[i] - step * (total - preceding(total)))
        return out

    w = sweep(w, u, t, shear)
    u, uu, t = primitives(w)
    w = sweep(w, u, t, SHEAR_REFERENCE * power(t, SHEAR_EXPONENT))
    u, uu, t = primitives(w)
    n = w[0]

    for row, field in enumerate([n, u[0], u[1], u[2], t, q[0], q[1], q[2]]):
        macro_ref[pl.ds(row, blocks, stride=8), :] = field

    inverse = 1.0 / t
    relax = n * power(t, 1.0 - SHEAR_EXPONENT)
    damp = 1.0 / (1.0 + relax)
    scale = n * inverse * lax.rsqrt(t) * relax * damp
    beta = scale * ((1.0 - CONDUCTIVE_SHARE) / 5.0) * inverse * inverse / n
    cubic = beta * inverse
    qu = q[0] * u[0] + q[1] * u[1] + q[2] * u[2]
    offset = beta * (uu * inverse - 5.0)
    twice = 2.0 * cubic
    zz = q[2] * u[2]
    polynomial = [
        scale - qu * offset,
        offset * q[0] + twice * qu * u[0],
        offset * q[1] + twice * qu * u[1],
        offset * q[2] + twice * qu * u[2],
        -cubic * (qu + 2.0 * zz),
        -twice * (q[0] * u[0] - zz),
        -twice * (q[0] * u[1] + q[1] * u[0]),
        -twice * (q[0] * u[2] + q[2] * u[0]),
        -twice * (q[1] * u[1] - zz),
        -twice * (q[1] * u[2] + q[2] * u[1]),
        cubic * q[0],
        cubic * q[1],
        cubic * q[2],
    ]
    zero = jnp.zeros_like(n)
    rate = (0.5 * LOG2E) * inverse
    exponent = [-rate * uu, 2.0 * rate * u[0], 2.0 * rate * u[1], 2.0 * rate * u[2], -rate]
    rows = polynomial + [damp, zero, zero] + exponent + [zero, zero, zero]
    for row, field in enumerate(rows):
        coef_ref[pl.ds(row, blocks, stride=COEF), :] = field


def fluid_call(moments):
    blocks = moments.shape[0] // SENT
    return pl.pallas_call(
        fluid_kernel,
        out_shape=(
            pltpu.VMEM((blocks * COEF, LANES), jnp.float32),
            pltpu.VMEM((blocks * 8, LANES), jnp.float32),
        ),
        in_specs=[WHOLE],
        out_specs=(WHOLE, WHOLE),
        compiler_params=params(8),
        name="fluid",
    )(moments)


def relaxed(g, coef_ref, basis, tile):
    per_tile = TILE // LANES
    parts = [
        coef_ref[pl.ds((tile * per_tile + part) * COEF, COEF), :]
        for part in range(per_tile)
    ]
    coefficients = jnp.concatenate(parts, axis=1)
    polynomial = dot(basis, expand(coefficients[:BASIS]))
    rows = jnp.concatenate([coefficients[BASIS:], jnp.zeros((8, TILE), jnp.float32)], axis=0)
    exponent = dot(basis, expand(rows))
    return g * coefficients[DAMP : DAMP + 1] + jnp.exp2(exponent) * polynomial


def gathered(g_refs, here):
    return jnp.concatenate([ref[:, here] for ref in g_refs], axis=0)


def update_kernel(*refs):
    g_refs = refs[:PARTS]
    coef_ref, basis_ref, table_ref, f_ref, moments_ref = refs[PARTS:]
    cells = f_ref.shape[1]

    def front(tile):
        here = pl.ds(tile * TILE, TILE)
        return relaxed(gathered(g_refs, here), coef_ref, basis_ref[...], tile)

    def back(tile, values):
        f_ref[:, tile * TILE : (tile + 1) * TILE] = values
        store_moments(moments_ref, table_ref[...], values, tile, cells // LANES)

    values = front(0)
    for tile in range(1, cells // TILE):
        upcoming = front(tile)
        back(tile - 1, values)
        values = upcoming
    back(cells // TILE - 1, values)


def update_call(g, coefficients, basis, table):
    rows, cells = g[0].shape
    return pl.pallas_call(
        update_kernel,
        out_shape=(
            pltpu.VMEM((rows * PARTS, cells), jnp.float32),
            pltpu.VMEM((SENT * cells // LANES, LANES), jnp.float32),
        ),
        in_specs=[WHOLE] * (PARTS + 3),
        out_specs=(WHOLE, WHOLE),
        compiler_params=params(8),
        name="update",
    )(*[near(part) for part in g], near(coefficients), near(basis), near(table))


def finish_kernel(*refs):
    g_refs = refs[:PARTS]
    coef_ref, macro_ref, basis_ref, f_ref, fields_ref, held, sems = refs[PARTS:]
    cells = held.shape[1]
    width = cells // CHUNKS
    copies = []
    for chunk in range(CHUNKS):
        for local in range(width // TILE):
            tile = chunk * (width // TILE) + local
            here = pl.ds(tile * TILE, TILE)
            held[:, here] = relaxed(gathered(g_refs, here), coef_ref, basis_ref[...], tile)
            for block in range(tile * TILE // LANES, (tile + 1) * TILE // LANES):
                fields_ref[:, pl.ds(block * LANES, LANES)] = macro_ref[pl.ds(block * 8, 8), :]
        there = pl.ds(chunk * width, width)
        copy = pltpu.make_async_copy(held.at[:, there], f_ref.at[:, there], sems.at[chunk])
        copy.start()
        copies.append(copy)
    for copy in copies:
        copy.wait()


def finish_call(g, coefficients, macro, basis):
    rows, cells = g[0].shape
    return pl.pallas_call(
        finish_kernel,
        out_shape=(
            jax.ShapeDtypeStruct((rows * PARTS, cells), jnp.float32),
            jax.ShapeDtypeStruct((8, cells), jnp.float32),
        ),
        in_specs=[WHOLE] * (PARTS + 3),
        out_specs=(OUTSIDE, WHOLE),
        scratch_shapes=[
            pltpu.VMEM((rows * PARTS, cells), jnp.float32),
            pltpu.SemaphoreType.DMA((CHUNKS,)),
        ],
        compiler_params=params(16),
        name="finish",
    )(*[near(part) for part in g], near(coefficients), near(macro), near(basis))


def add_kernel(left_ref, right_ref, out_ref):
    out_ref[...] = left_ref[...] + right_ref[...]


def add_call(left, right):
    return pl.pallas_call(
        add_kernel,
        out_shape=pltpu.VMEM(left.shape, left.dtype),
        in_specs=[WHOLE, WHOLE],
        out_specs=WHOLE,
        compiler_params=params(1),
        name="add",
    )(near(left), near(right))


def plan(count):
    strides = [1 << bit for bit in range(count.bit_length() - 1)]
    return strides[:2], strides[2:]


def swap(values, count, stride, odd_only=False):
    pairs = [(device, device ^ stride) for device in range(count) if device & 1 or not odd_only]
    return lax.ppermute(values, "vel", pairs)


def staged_sum(values, count, sides, f, tasks):
    splits, sums = plan(count)
    results, waiting, portions = [], list(tasks), list(BESIDE)
    even = sides[0]

    def beside(sent, got):
        portion = portions.pop(0) if portions else 0
        if portion:
            _, held = lax.optimization_barrier((sent, f))
            made = [task(held) for task in waiting[:portion]]
            del waiting[:portion]
            got, made = lax.optimization_barrier((got, made))
            results.extend(made)
        return got

    def exchange(chunks, stride):
        shared, extra = chunks
        got = swap(shared, count, stride)
        more = swap(extra, count, stride, odd_only=True)
        return beside(extra, got), more

    def add(chunks, received):
        shared = add_call(chunks[0], received[0])
        shared, more = lax.optimization_barrier((shared, received[1]))
        return [shared, add_call(chunks[1], more)]

    def split(chunks, stride, lower_side):
        kept, sent = [], []
        for chunk in chunks:
            half = chunk.shape[0] // 2
            first, second = chunk[:half], chunk[half:]
            kept.append(jnp.where(lower_side, first, second))
            sent.append(jnp.where(lower_side, second, first))
        sent = lax.optimization_barrier(sent)
        return add(kept, exchange(sent, stride))

    def join(chunks, stride, lower_side):
        def both(own, got):
            return jnp.concatenate(
                [jnp.where(lower_side, own, got), jnp.where(lower_side, got, own)], axis=0
            )

        got, more = exchange(chunks, stride)
        shared, more = lax.optimization_barrier((both(chunks[0], got), more))
        return [shared, both(chunks[1], more)]

    portion = values.shape[0] // SENT
    evens, odds, extra = values[: 5 * portion], values[5 * portion : 10 * portion], values[10 * portion :]
    kept, sent = jnp.where(even, evens, odds), jnp.where(even, odds, evens)
    to_odd = [(device, device + 1) for device in range(0, count, 2)]
    to_even = [(device + 1, device) for device in range(0, count, 2)]
    got, more = swap(sent, count, 1), lax.ppermute(extra, "vel", to_odd)
    chunks = add([kept, extra], [beside(sent, got), more])
    for stride, lower_side in zip(splits[1:], sides[1:]):
        chunks = split(chunks, stride, lower_side)
    for stride in sums:
        chunks = add(chunks, exchange(chunks, stride))
    for stride, lower_side in reversed(list(zip(splits[1:], sides[1:]))):
        chunks = join(chunks, stride, lower_side)
    shared, extra = chunks
    got, more = swap(shared, count, 1), lax.ppermute(extra, "vel", to_even)
    got = beside(shared, got)
    results.extend(task(f) for task in waiting)
    whole = [
        jnp.where(even, shared, got),
        jnp.where(even, got, shared),
        jnp.where(even, more, extra),
    ]
    return jnp.concatenate(whole, axis=0), results


def on_device(velocities, density, flow, thermal, deviation):
    count = lax.axis_size("vel")
    place = lax.axis_index("vel")
    sides = [place & stride == 0 for stride in plan(count)[0]]
    velocities, sides = lax.optimization_barrier((velocities, sides))
    f, moments, basis, table, stream = start_call(
        velocities, density, flow, thermal, deviation, velocities.shape[1] * count
    )
    for iteration in range(ITERS):
        tasks = [
            functools.partial(lambda held, part: transport_call(stream, held, part), part=part)
            for part in range(PARTS)
        ]
        summed, g = staged_sum(moments, count, sides, f, tasks)
        coefficients, macro = fluid_call(summed)
        if iteration < ITERS - 1:
            f, moments = update_call(g, coefficients, basis, table)
    return finish_call(g, coefficients, macro, basis)


def solution(mesh):
    return jax.shard_map(
        on_device,
        mesh=mesh,
        in_specs=(P(None, "vel"), P("grp"), P(None, "grp"), P("grp"), P("vel", "grp")),
        out_specs=(P("vel", "grp"), P(None, "grp")),
        check_vma=False,
    )
```

```python
import functools

import jax
import jax.numpy as jnp
from jax import lax
from jax.experimental import pallas as pl
from jax.experimental.pallas import tpu as pltpu
from jax.sharding import PartitionSpec as P

ITERS = 2

ADIABATIC_INDEX = 5.0 / 3.0
CONDUCTIVE_SHARE = 2.0 / 3.0
SHEAR_EXPONENT = 0.81
SHEAR_REFERENCE = 0.05
KINETIC_STEP = 0.05
COURANT = 0.4
SPREAD_SCALE = 1.5

LOG2E = 1.4426950408889634
LANES = 128
TILE = 256
BASIS = 16
SENT = 13
COEF = 24
DAMP = 13
CHUNKS = 8
PARTS = 8
BESIDE = (1, 2, 1, 2, 1, 1)
MIB = 1024 * 1024

WHOLE = pl.BlockSpec(memory_space=pltpu.VMEM)
OUTSIDE = pl.BlockSpec(memory_space=pltpu.HBM)


def params(mebibytes):
    return pltpu.CompilerParams(vmem_limit_bytes=mebibytes * MIB)


def near(values):
    return pltpu.with_memory_space_constraint(values, pltpu.VMEM)


def far(values):
    return pltpu.with_memory_space_constraint(values, pltpu.HBM)


def dot(left, right):
    return jnp.dot(left, right, preferred_element_type=jnp.float32)


def rounded(values):
    return values.astype(jnp.bfloat16).astype(jnp.float32)


def phi_rows(velocities):
    vx, vy, vz = velocities[0:1], velocities[1:2], velocities[2:3]
    sq = vx * vx + vy * vy + vz * vz
    zero = jnp.zeros_like(vx)
    rows = [
        jnp.ones_like(vx), vx, vy, vz, sq, vx * vx, vx * vy, vx * vz, vy * vy, vy * vz,
        vx * sq, vy * sq, vz * sq, zero, zero, zero,
    ]
    return jnp.concatenate(rows, axis=0), sq


def make_tables(velocities, total_count):
    phi, sq = phi_rows(velocities)
    high = rounded(phi)
    middle = rounded(phi - high)
    low = phi - high - middle
    stacked = jnp.concatenate(
        [high, high, high, middle, middle, low, jnp.zeros((32, phi.shape[1]), jnp.float32)], axis=0
    )
    basis = stacked.T.astype(jnp.bfloat16)
    weighted = phi * (SPREAD_SCALE**3 * jnp.exp(sq / (2.0 * SPREAD_SCALE**2)) / total_count)
    top = rounded(weighted)
    rest = weighted - top
    moments = jnp.concatenate(
        [
            jnp.concatenate([top, top], axis=1),
            jnp.concatenate([rest, jnp.zeros_like(rest)], axis=1),
        ],
        axis=0,
    ).astype(jnp.bfloat16)
    return basis, moments


def expand(coefficients):
    high = coefficients.astype(jnp.bfloat16)
    rest = coefficients - high.astype(jnp.float32)
    middle = rest.astype(jnp.bfloat16)
    low = (rest - middle.astype(jnp.float32)).astype(jnp.bfloat16)
    zero = jnp.zeros((32, coefficients.shape[1]), jnp.bfloat16)
    return jnp.concatenate([high, middle, low, high, middle, high, zero], axis=0)


def store_moments(moments_ref, table, values, tile, blocks):
    high = values.astype(jnp.bfloat16)
    low = (values - high.astype(jnp.float32)).astype(jnp.bfloat16)
    both = dot(table, jnp.concatenate([high, low], axis=0))
    sums = both[:BASIS] + both[BASIS:]
    per_tile = TILE // LANES
    for part in range(per_tile):
        block = tile * per_tile + part
        moments_ref[pl.ds(block, SENT, stride=blocks), :] = sums[
            :SENT, part * LANES : (part + 1) * LANES
        ]


def in_turn(front, back, tiles):
    values = front(0)
    for tile in range(1, tiles):
        upcoming = front(tile)
        back(tile - 1, values)
        values = upcoming
    back(tiles - 1, values)


def start_kernel(
    total_count,
    vel_hbm, density_hbm, flow_hbm, thermal_hbm, deviation_hbm,
    f_ref, moments_ref, basis_ref, table_ref, stream_ref,
    vel_ref, density_ref, flow_ref, thermal_ref, deviation_ref, small_sems, sems,
):
    cells = f_ref.shape[1]
    width = cells // CHUNKS
    small = [
        pltpu.make_async_copy(source, target, small_sems.at[number])
        for number, (source, target) in enumerate(
            [
                (vel_hbm, vel_ref),
                (density_hbm, density_ref),
                (flow_hbm, flow_ref),
                (thermal_hbm, thermal_ref),
            ]
        )
    ]
    for copy in small:
        copy.start()
    copies = [
        pltpu.make_async_copy(
            deviation_hbm.at[:, pl.ds(chunk * width, width)],
            deviation_ref.at[:, pl.ds(chunk * width, width)],
            sems.at[chunk],
        )
        for chunk in range(CHUNKS)
    ]
    for copy in copies:
        copy.start()
    small[0].wait()
    basis, table = make_tables(vel_ref[...], total_count)
    basis_ref[...] = basis
    table_ref[...] = table
    stream_ref[...] = jnp.broadcast_to(vel_ref[0:1, :], (LANES, vel_ref.shape[1])).T
    for copy in small[1:]:
        copy.wait()
    def front(tile):
        here = pl.ds(tile * TILE, TILE)
        density, flow, thermal = density_ref[:, here], flow_ref[:, here], thermal_ref[:, here]
        rate = (0.5 * LOG2E) / thermal
        speed_sq = flow[0:1] * flow[0:1] + flow[1:2] * flow[1:2] + flow[2:3] * flow[2:3]
        rows = [-rate * speed_sq, 2.0 * rate * flow, -rate, jnp.zeros((11, TILE), jnp.float32)]
        exponent = dot(basis, expand(jnp.concatenate(rows, axis=0)))
        scale = density / (thermal * jnp.sqrt(thermal))
        return jnp.exp2(exponent) * (scale * (1.0 + deviation_ref[:, here]))

    def back(tile, values):
        f_ref[:, tile * TILE : (tile + 1) * TILE] = values
        store_moments(moments_ref, table, values, tile, cells // LANES)

    def front_when_here(tile):
        if tile * TILE % width == 0:
            copies[tile * TILE // width].wait()
        return front(tile)

    in_turn(front_when_here, back, cells // TILE)


def start_call(velocities, density, flow, thermal, deviation, total_count):
    local, cells = deviation.shape
    return pl.pallas_call(
        functools.partial(start_kernel, total_count),
        out_shape=(
            pltpu.VMEM((local, cells), jnp.float32),
            pltpu.VMEM((SENT * cells // LANES, LANES), jnp.float32),
            pltpu.VMEM((local, 128), jnp.bfloat16),
            pltpu.VMEM((2 * BASIS, 2 * local), jnp.bfloat16),
            pltpu.VMEM((local, LANES), jnp.float32),
        ),
        in_specs=[OUTSIDE] * 5,
        out_specs=(WHOLE,) * 5,
        scratch_shapes=[
            pltpu.VMEM((3, local), jnp.float32),
            pltpu.VMEM((1, cells), jnp.float32),
            pltpu.VMEM((3, cells), jnp.float32),
            pltpu.VMEM((1, cells), jnp.float32),
            pltpu.VMEM((local, cells), jnp.float32),
            pltpu.SemaphoreType.DMA((4,)),
            pltpu.SemaphoreType.DMA((CHUNKS,)),
        ],
        compiler_params=params(16),
        name="start",
    )(
        far(velocities),
        far(density.reshape(1, cells)),
        far(flow),
        far(thermal.reshape(1, cells)),
        far(deviation),
    )


def transport_kernel(first_row, stream_ref, f_ref, g_ref):
    rows, cells = g_ref.shape
    blocks = cells // LANES
    lane = lax.broadcasted_iota(jnp.int32, (8, LANES), 1)
    at_first, at_last = lane == 0, lane == LANES - 1
    lag = 4

    def row_step(row_tile, carry):
        source = pl.ds(pl.multiple_of(first_row + row_tile * 8, 8), 8)
        target = pl.ds(pl.multiple_of(row_tile * 8, 8), 8)
        stream = stream_ref[source, :]
        upward = stream > 0
        rate = KINETIC_STEP * jnp.abs(stream)
        half = jnp.where(upward, 0.5, -0.5)
        x, up, rise, down, face, face_up, face_down = {}, {}, {}, {}, {}, {}, {}

        def load(b):
            at = (b % blocks) * LANES
            x[b] = f_ref[source, at : at + LANES]
            up[b] = pltpu.roll(x[b], 1, 1)

        def slope_in(b):
            rise[b] = x[b] - jnp.where(at_first, up[b - 1], up[b])
            down[b] = pltpu.roll(rise[b], LANES - 1, 1)

        def reconstruct(b):
            ahead = jnp.where(at_last, down[b + 1], down[b])
            slope = jnp.maximum(jnp.minimum(rise[b], ahead), 0.0) + jnp.minimum(
                jnp.maximum(rise[b], ahead), 0.0
            )
            face[b] = x[b] + half * slope
            face_up[b] = pltpu.roll(face[b], 1, 1)
            face_down[b] = pltpu.roll(face[b], LANES - 1, 1)

        def store(b):
            other = jnp.where(
                upward,
                jnp.where(at_first, face_up[b - 1], face_up[b]),
                jnp.where(at_last, face_down[b + 1], face_down[b]),
            )
            g_ref[target, b * LANES : (b + 1) * LANES] = x[b] - rate * (face[b] - other)

        for k in range(-2, blocks + 3 * lag + 4):
            for act, behind, low, high in (
                (load, 0, -2, blocks + 1),
                (slope_in, lag, -1, blocks + 1),
                (reconstruct, 2 * lag + 1, -1, blocks),
                (store, 3 * lag + 2, 0, blocks - 1),
            ):
                if low <= k - behind <= high:
                    act(k - behind)
        return carry

    lax.fori_loop(0, rows // 8, row_step, 0)


def transport_call(stream, f, part):
    local, cells = f.shape
    rows = local // PARTS
    return pl.pallas_call(
        functools.partial(transport_kernel, part * rows),
        out_shape=pltpu.VMEM((rows, cells), jnp.float32),
        in_specs=[WHOLE, WHOLE],
        out_specs=WHOLE,
        compiler_params=params(4),
        name="transport",
    )(near(stream), near(f))


def fluid_kernel(moments_ref, coef_ref, macro_ref=None):
    blocks = moments_ref.shape[0] // SENT
    m = [moments_ref[row * blocks : (row + 1) * blocks, :] for row in range(13)]
    lane = lax.broadcasted_iota(jnp.int32, (blocks, LANES), 1)

    def following(x):
        turned = pltpu.roll(x, LANES - 1, 1)
        return jnp.where(lane == LANES - 1, pltpu.roll(turned, blocks - 1, 0), turned)

    def preceding(x):
        turned = pltpu.roll(x, 1, 1)
        return jnp.where(lane == 0, pltpu.roll(turned, 1, 0), turned)

    def power(x, exponent):
        return jnp.exp2(exponent * jnp.log2(x))

    def primitives(w):
        inverse = 1.0 / w[0]
        u = [w[1] * inverse, w[2] * inverse, w[3] * inverse]
        uu = u[0] * u[0] + u[1] * u[1] + u[2] * u[2]
        t = (2.0 * w[4] * inverse - uu) * (1.0 / 3.0)
        return u, uu, t

    n = m[0]
    w = [n, m[1], m[2], m[3], 0.5 * m[4]]
    u, uu, t = primitives(w)
    p = n * t
    second = [[m[5], m[6], m[7]], [m[6], m[8], m[9]], [m[7], m[9], m[4] - m[5] - m[8]]]
    stress = [m[5] - m[1] * u[0] - p, m[6] - m[1] * u[1], m[7] - m[1] * u[2]]
    q = []
    for i in range(3):
        along = second[i][0] * u[0] + second[i][1] * u[1] + second[i][2] * u[2]
        q.append(0.5 * (m[10 + i] - u[i] * m[4] - 2.0 * along + 2.0 * n * u[i] * uu))

    shear = SHEAR_REFERENCE * power(t, SHEAR_EXPONENT)
    high_order = [
        stress[i] + ((4.0 / 3.0 if i == 0 else 1.0) * 0.5) * shear * (following(u[i]) - preceding(u[i]))
        for i in range(3)
    ]
    high_order.append(q[0] + (3.75 * 0.5) * shear * (following(t) - preceding(t)))
    half_order = [0.5 * h for h in high_order]
    face_order = [h + following(h) for h in half_order]

    def sweep(w, u, t, shear):
        rates = jnp.abs(u[0]) + jnp.sqrt(ADIABATIC_INDEX * t)
        signal = jnp.max(jnp.max(rates, axis=0, keepdims=True), axis=1, keepdims=True)
        step = COURANT / signal
        p = w[0] * t
        euler = [w[1], w[1] * u[0] + p, w[1] * u[1], w[1] * u[2], (w[4] + p) * u[0]]
        next_u = [following(x) for x in u]
        half_shear = 0.5 * shear
        face_shear = half_shear + following(half_shear)
        sxx = face_order[0] - (4.0 / 3.0) * face_shear * (next_u[0] - u[0])
        sxy = face_order[1] - face_shear * (next_u[1] - u[1])
        sxz = face_order[2] - face_shear * (next_u[2] - u[2])
        heat = face_order[3] - 3.75 * face_shear * (following(t) - t)
        work = 0.5 * (
            sxx * (u[0] + next_u[0]) + sxy * (u[1] + next_u[1]) + sxz * (u[2] + next_u[2])
        )
        viscous = [None, sxx, sxy, sxz, work + heat]
        out = []
        for i in range(5):
            spread = signal * w[i]
            total = 0.5 * ((euler[i] + spread) + following(euler[i] - spread))
            if viscous[i] is not None:
                total = total + viscous[i]
            out.append(w[i] - step * (total - preceding(total)))
        return out

    w = sweep(w, u, t, shear)
    u, uu, t = primitives(w)
    w = sweep(w, u, t, SHEAR_REFERENCE * power(t, SHEAR_EXPONENT))
    u, uu, t = primitives(w)
    n = w[0]

    if macro_ref is not None:
        for row, field in enumerate([n, u[0], u[1], u[2], t, q[0], q[1], q[2]]):
            macro_ref[pl.ds(row, blocks, stride=8), :] = field

    inverse = 1.0 / t
    relax = n * power(t, 1.0 - SHEAR_EXPONENT)
    damp = 1.0 / (1.0 + relax)
    scale = n * inverse * lax.rsqrt(t) * relax * damp
    beta = scale * ((1.0 - CONDUCTIVE_SHARE) / 5.0) * inverse * inverse / n
    cubic = beta * inverse
    qu = q[0] * u[0] + q[1] * u[1] + q[2] * u[2]
    offset = beta * (uu * inverse - 5.0)
    twice = 2.0 * cubic
    zz = q[2] * u[2]
    polynomial = [
        scale - qu * offset,
        offset * q[0] + twice * qu * u[0],
        offset * q[1] + twice * qu * u[1],
        offset * q[2] + twice * qu * u[2],
        -cubic * (qu + 2.0 * zz),
        -twice * (q[0] * u[0] - zz),
        -twice * (q[0] * u[1] + q[1] * u[0]),
        -twice * (q[0] * u[2] + q[2] * u[0]),
        -twice * (q[1] * u[1] - zz),
        -twice * (q[1] * u[2] + q[2] * u[1]),
        cubic * q[0],
        cubic * q[1],
        cubic * q[2],
    ]
    zero = jnp.zeros_like(n)
    rate = (0.5 * LOG2E) * inverse
    exponent = [-rate * uu, 2.0 * rate * u[0], 2.0 * rate * u[1], 2.0 * rate * u[2], -rate]
    rows = polynomial + [damp, zero, zero] + exponent + [zero, zero, zero]
    for row, field in enumerate(rows):
        coef_ref[pl.ds(row, blocks, stride=COEF), :] = field


def fluid_call(moments, last):
    blocks = moments.shape[0] // SENT
    shapes = [pltpu.VMEM((blocks * COEF, LANES), jnp.float32)]
    if last:
        shapes.append(pltpu.VMEM((blocks * 8, LANES), jnp.float32))
    return pl.pallas_call(
        fluid_kernel,
        out_shape=shapes,
        in_specs=[WHOLE],
        out_specs=[WHOLE] * len(shapes),
        compiler_params=params(8),
        name="fluid",
    )(near(moments))


def relaxed(g, coef_ref, basis, tile):
    per_tile = TILE // LANES
    parts = [
        coef_ref[pl.ds((tile * per_tile + part) * COEF, COEF), :]
        for part in range(per_tile)
    ]
    coefficients = jnp.concatenate(parts, axis=1)
    polynomial = dot(basis, expand(coefficients[:BASIS]))
    rows = jnp.concatenate([coefficients[BASIS:], jnp.zeros((8, TILE), jnp.float32)], axis=0)
    exponent = dot(basis, expand(rows))
    return g * coefficients[DAMP : DAMP + 1] + jnp.exp2(exponent) * polynomial


def gathered(g_refs, here):
    return jnp.concatenate([ref[:, here] for ref in g_refs], axis=0)


def update_kernel(*refs):
    g_refs = refs[:PARTS]
    coef_ref, basis_ref, table_ref, f_ref, moments_ref = refs[PARTS:]
    cells = f_ref.shape[1]

    def front(tile):
        here = pl.ds(tile * TILE, TILE)
        return relaxed(gathered(g_refs, here), coef_ref, basis_ref[...], tile)

    def back(tile, values):
        f_ref[:, tile * TILE : (tile + 1) * TILE] = values
        store_moments(moments_ref, table_ref[...], values, tile, cells // LANES)

    in_turn(front, back, cells // TILE)


def update_call(g, coefficients, basis, table):
    rows, cells = g[0].shape
    return pl.pallas_call(
        update_kernel,
        out_shape=(
            pltpu.VMEM((rows * PARTS, cells), jnp.float32),
            pltpu.VMEM((SENT * cells // LANES, LANES), jnp.float32),
        ),
        in_specs=[WHOLE] * (PARTS + 3),
        out_specs=(WHOLE, WHOLE),
        compiler_params=params(8),
        name="update",
    )(*[near(part) for part in g], near(coefficients), near(basis), near(table))


def finish_kernel(*refs):
    g_refs = refs[:PARTS]
    coef_ref, macro_ref, basis_ref, f_ref, fields_ref, held, sems = refs[PARTS:]
    cells = held.shape[1]
    width = cells // CHUNKS
    copies = []
    for chunk in range(CHUNKS):
        for local in range(width // TILE):
            tile = chunk * (width // TILE) + local
            here = pl.ds(tile * TILE, TILE)
            held[:, here] = relaxed(gathered(g_refs, here), coef_ref, basis_ref[...], tile)
            for block in range(tile * TILE // LANES, (tile + 1) * TILE // LANES):
                fields_ref[:, pl.ds(block * LANES, LANES)] = macro_ref[pl.ds(block * 8, 8), :]
        there = pl.ds(chunk * width, width)
        copy = pltpu.make_async_copy(held.at[:, there], f_ref.at[:, there], sems.at[chunk])
        copy.start()
        copies.append(copy)
    for copy in copies:
        copy.wait()


def finish_call(g, coefficients, macro, basis):
    rows, cells = g[0].shape
    return pl.pallas_call(
        finish_kernel,
        out_shape=(
            jax.ShapeDtypeStruct((rows * PARTS, cells), jnp.float32),
            jax.ShapeDtypeStruct((8, cells), jnp.float32),
        ),
        in_specs=[WHOLE] * (PARTS + 3),
        out_specs=(OUTSIDE, WHOLE),
        scratch_shapes=[
            pltpu.VMEM((rows * PARTS, cells), jnp.float32),
            pltpu.SemaphoreType.DMA((CHUNKS,)),
        ],
        compiler_params=params(16),
        name="finish",
    )(*[near(part) for part in g], near(coefficients), near(macro), near(basis))


def add_kernel(left_ref, right_ref, out_ref):
    out_ref[...] = left_ref[...] + right_ref[...]


def add_call(left, right):
    return pl.pallas_call(
        add_kernel,
        out_shape=pltpu.VMEM(left.shape, left.dtype),
        in_specs=[WHOLE, WHOLE],
        out_specs=WHOLE,
        compiler_params=params(1),
        name="add",
    )(near(left), near(right))


def plan(count):
    strides = [1 << bit for bit in range(count.bit_length() - 1)]
    return strides[:2], strides[2:]


def swap(values, count, stride):
    return lax.ppermute(values, "vel", [(device, device ^ stride) for device in range(count)])


def staged_sum(values, count, sides, f, tasks):
    splits, sums = plan(count)
    results, waiting, portions = [], list(tasks), list(BESIDE)

    def exchange(chunks, stride):
        got = [swap(chunk, count, stride) for chunk in chunks]
        portion = portions.pop(0) if portions else 0
        if portion:
            _, held = lax.optimization_barrier((chunks[-1], f))
            made = [task(held) for task in waiting[:portion]]
            del waiting[:portion]
            got[0], made = lax.optimization_barrier((got[0], made))
            results.extend(made)
        return got

    def split(chunks, stride, lower_side):
        kept, sent = [], []
        for chunk in chunks:
            half = chunk.shape[0] // 2
            first, second = chunk[:half], chunk[half:]
            kept.append(jnp.where(lower_side, first, second))
            sent.append(jnp.where(lower_side, second, first))
        sent = lax.optimization_barrier(sent)
        got = exchange(sent, stride)
        if len(chunks) == 1:
            return [kept[0] + got[0]]
        return [add_call(own, other) for own, other in zip(kept, got)]

    def join(chunks, stride, lower_side):
        out = []
        for own, got in zip(chunks, exchange(chunks, stride)):
            lower = jnp.where(lower_side, own, got)
            upper = jnp.where(lower_side, got, own)
            out.append((lower, upper))
        return out

    (block,) = split([values], splits[0], sides[0])
    half = block.shape[0] // 2
    chunks = [block[:half], block[half:]]
    for stride, lower_side in zip(splits[1:], sides[1:]):
        chunks = split(chunks, stride, lower_side)
    for stride in sums:
        chunks = [add_call(own, got) for own, got in zip(chunks, exchange(chunks, stride))]
    for stride, lower_side in reversed(list(zip(splits[1:], sides[1:]))):
        chunks = [jnp.concatenate(both, axis=0) for both in join(chunks, stride, lower_side)]
    lowers, uppers = zip(*join(chunks, splits[0], sides[0]))
    results.extend(task(f) for task in waiting)
    return jnp.concatenate(lowers + uppers, axis=0), results


def on_device(velocities, density, flow, thermal, deviation):
    count = lax.axis_size("vel")
    place = lax.axis_index("vel")
    sides = [place & stride == 0 for stride in plan(count)[0]]
    velocities, sides = lax.optimization_barrier((velocities, sides))
    f, moments, basis, table, stream = start_call(
        velocities, density, flow, thermal, deviation, velocities.shape[1] * count
    )
    for iteration in range(ITERS):
        tasks = [
            functools.partial(lambda held, part: transport_call(stream, held, part), part=part)
            for part in range(PARTS)
        ]
        summed, g = staged_sum(moments, count, sides, f, tasks)
        last = iteration == ITERS - 1
        coefficients, *macro = fluid_call(summed, last)
        if not last:
            f, moments = update_call(g, coefficients, basis, table)
    return finish_call(g, coefficients, macro[0], basis)


def solution(mesh):
    return jax.shard_map(
        on_device,
        mesh=mesh,
        in_specs=(P(None, "vel"), P("grp"), P(None, "grp"), P("grp"), P("vel", "grp")),
        out_specs=(P("vel", "grp"), P(None, "grp")),
        check_vma=False,
    )
```

```python
import functools

import jax
import jax.numpy as jnp
from jax import lax
from jax.experimental import pallas as pl
from jax.experimental.pallas import tpu as pltpu
from jax.sharding import PartitionSpec as P

ITERS = 2

ADIABATIC_INDEX = 5.0 / 3.0
CONDUCTIVE_SHARE = 2.0 / 3.0
SHEAR_EXPONENT = 0.81
SHEAR_REFERENCE = 0.05
KINETIC_STEP = 0.05
COURANT = 0.4
SPREAD_SCALE = 1.5

LOG2E = 1.4426950408889634
LANES = 128
TILE = 256
BASIS = 16
SENT = 13
COEF = 24
DAMP = 13
CHUNKS = 8
PARTS = 8
BESIDE = (1, 2, 1, 2, 1, 1)
MIB = 1024 * 1024

WHOLE = pl.BlockSpec(memory_space=pltpu.VMEM)
OUTSIDE = pl.BlockSpec(memory_space=pltpu.HBM)


def params(mebibytes):
    return pltpu.CompilerParams(vmem_limit_bytes=mebibytes * MIB)


def near(values):
    return pltpu.with_memory_space_constraint(values, pltpu.VMEM)


def far(values):
    return pltpu.with_memory_space_constraint(values, pltpu.HBM)


def dot(left, right):
    return jnp.dot(left, right, preferred_element_type=jnp.float32)


def rounded(values):
    return values.astype(jnp.bfloat16).astype(jnp.float32)


def phi_rows(velocities):
    vx, vy, vz = velocities[0:1], velocities[1:2], velocities[2:3]
    sq = vx * vx + vy * vy + vz * vz
    zero = jnp.zeros_like(vx)
    rows = [
        jnp.ones_like(vx), vx, vy, vz, sq, vx * vx, vx * vy, vx * vz, vy * vy, vy * vz,
        vx * sq, vy * sq, vz * sq, zero, zero, zero,
    ]
    return jnp.concatenate(rows, axis=0), sq


def parts_of(values):
    high = rounded(values)
    middle = rounded(values - high)
    return high, middle, values - high - middle


def make_tables(velocities, total_count):
    phi, sq = phi_rows(velocities)
    high, middle, low = parts_of(phi)
    three = [high[:8], high[:8], high[:8], middle[:8], middle[:8], low[:8]]
    wide = jnp.zeros((128 - 6 * 8, phi.shape[1]), jnp.float32)
    exponent = jnp.concatenate(three + [wide], axis=0).T[:, : 6 * 8].astype(jnp.bfloat16)
    two = [high, high, middle]
    polynomial = jnp.concatenate(two + [wide], axis=0).T[:, : 3 * BASIS].astype(jnp.bfloat16)
    weighted = phi * (SPREAD_SCALE**3 * jnp.exp(sq / (2.0 * SPREAD_SCALE**2)) / total_count)
    top = rounded(weighted)
    rest = weighted - top
    moments = jnp.concatenate(
        [
            jnp.concatenate([top, top], axis=1),
            jnp.concatenate([rest, jnp.zeros_like(rest)], axis=1),
        ],
        axis=0,
    ).astype(jnp.bfloat16)
    return exponent, polynomial, moments


def expand_exponent(rows):
    high, middle, low = parts_of(rows)
    return jnp.concatenate([high, middle, low, high, middle, high], axis=0).astype(jnp.bfloat16)


def expand_polynomial(rows):
    high = rows.astype(jnp.bfloat16)
    middle = (rows - high.astype(jnp.float32)).astype(jnp.bfloat16)
    return jnp.concatenate([high, middle, high], axis=0)


def store_moments(moments_ref, table, values, tile, blocks):
    high = values.astype(jnp.bfloat16)
    low = (values - high.astype(jnp.float32)).astype(jnp.bfloat16)
    both = dot(table, jnp.concatenate([high, low], axis=0))
    sums = both[:BASIS] + both[BASIS:]
    per_tile = TILE // LANES
    for part in range(per_tile):
        block = tile * per_tile + part
        moments_ref[pl.ds(block, SENT, stride=blocks), :] = sums[
            :SENT, part * LANES : (part + 1) * LANES
        ]


def in_turn(front, back, tiles):
    values = front(0)
    for tile in range(1, tiles):
        upcoming = front(tile)
        back(tile - 1, values)
        values = upcoming
    back(tiles - 1, values)


def start_kernel(
    total_count,
    vel_hbm, density_hbm, flow_hbm, thermal_hbm, deviation_hbm,
    f_ref, moments_ref, exponent_ref, polynomial_ref, table_ref, stream_ref,
    vel_ref, density_ref, flow_ref, thermal_ref, deviation_ref, small_sems, sems,
):
    cells = f_ref.shape[1]
    width = cells // CHUNKS
    small = [
        pltpu.make_async_copy(source, target, small_sems.at[number])
        for number, (source, target) in enumerate(
            [
                (vel_hbm, vel_ref),
                (density_hbm, density_ref),
                (flow_hbm, flow_ref),
                (thermal_hbm, thermal_ref),
            ]
        )
    ]
    for copy in small:
        copy.start()
    copies = [
        pltpu.make_async_copy(
            deviation_hbm.at[:, pl.ds(chunk * width, width)],
            deviation_ref.at[:, pl.ds(chunk * width, width)],
            sems.at[chunk],
        )
        for chunk in range(CHUNKS)
    ]
    for copy in copies:
        copy.start()
    small[0].wait()
    exponent_table, polynomial_table, table = make_tables(vel_ref[...], total_count)
    exponent_ref[...] = exponent_table
    polynomial_ref[...] = polynomial_table
    table_ref[...] = table
    stream_ref[...] = jnp.broadcast_to(vel_ref[0:1, :], (LANES, vel_ref.shape[1])).T
    for copy in small[1:]:
        copy.wait()
    def front(tile):
        here = pl.ds(tile * TILE, TILE)
        density, flow, thermal = density_ref[:, here], flow_ref[:, here], thermal_ref[:, here]
        rate = (0.5 * LOG2E) / thermal
        speed_sq = flow[0:1] * flow[0:1] + flow[1:2] * flow[1:2] + flow[2:3] * flow[2:3]
        rows = [-rate * speed_sq, 2.0 * rate * flow, -rate, jnp.zeros((3, TILE), jnp.float32)]
        exponent = dot(exponent_table, expand_exponent(jnp.concatenate(rows, axis=0)))
        scale = density / (thermal * jnp.sqrt(thermal))
        return jnp.exp2(exponent) * (scale * (1.0 + deviation_ref[:, here]))

    def back(tile, values):
        f_ref[:, tile * TILE : (tile + 1) * TILE] = values
        store_moments(moments_ref, table, values, tile, cells // LANES)

    def front_when_here(tile):
        if tile * TILE % width == 0:
            copies[tile * TILE // width].wait()
        return front(tile)

    in_turn(front_when_here, back, cells // TILE)


def start_call(velocities, density, flow, thermal, deviation, total_count):
    local, cells = deviation.shape
    return pl.pallas_call(
        functools.partial(start_kernel, total_count),
        out_shape=(
            pltpu.VMEM((local, cells), jnp.float32),
            pltpu.VMEM((SENT * cells // LANES, LANES), jnp.float32),
            pltpu.VMEM((local, 6 * 8), jnp.bfloat16),
            pltpu.VMEM((local, 3 * BASIS), jnp.bfloat16),
            pltpu.VMEM((2 * BASIS, 2 * local), jnp.bfloat16),
            pltpu.VMEM((local, LANES), jnp.float32),
        ),
        in_specs=[OUTSIDE] * 5,
        out_specs=(WHOLE,) * 6,
        scratch_shapes=[
            pltpu.VMEM((3, local), jnp.float32),
            pltpu.VMEM((1, cells), jnp.float32),
            pltpu.VMEM((3, cells), jnp.float32),
            pltpu.VMEM((1, cells), jnp.float32),
            pltpu.VMEM((local, cells), jnp.float32),
            pltpu.SemaphoreType.DMA((4,)),
            pltpu.SemaphoreType.DMA((CHUNKS,)),
        ],
        compiler_params=params(16),
        name="start",
    )(
        far(velocities),
        far(density.reshape(1, cells)),
        far(flow),
        far(thermal.reshape(1, cells)),
        far(deviation),
    )


def transport_kernel(first_row, stream_ref, f_ref, g_ref):
    rows, cells = g_ref.shape
    blocks = cells // LANES
    lane = lax.broadcasted_iota(jnp.int32, (8, LANES), 1)
    at_first, at_last = lane == 0, lane == LANES - 1
    lag = 4

    def row_step(row_tile, carry):
        source = pl.ds(pl.multiple_of(first_row + row_tile * 8, 8), 8)
        target = pl.ds(pl.multiple_of(row_tile * 8, 8), 8)
        stream = stream_ref[source, :]
        upward = stream > 0
        rate = KINETIC_STEP * jnp.abs(stream)
        half = jnp.where(upward, 0.5, -0.5)
        x, up, rise, down, face, face_up, face_down = {}, {}, {}, {}, {}, {}, {}

        def load(b):
            at = (b % blocks) * LANES
            x[b] = f_ref[source, at : at + LANES]
            up[b] = pltpu.roll(x[b], 1, 1)

        def slope_in(b):
            rise[b] = x[b] - jnp.where(at_first, up[b - 1], up[b])
            down[b] = pltpu.roll(rise[b], LANES - 1, 1)

        def reconstruct(b):
            ahead = jnp.where(at_last, down[b + 1], down[b])
            slope = jnp.maximum(jnp.minimum(rise[b], ahead), 0.0) + jnp.minimum(
                jnp.maximum(rise[b], ahead), 0.0
            )
            face[b] = x[b] + half * slope
            face_up[b] = pltpu.roll(face[b], 1, 1)
            face_down[b] = pltpu.roll(face[b], LANES - 1, 1)

        def store(b):
            other = jnp.where(
                upward,
                jnp.where(at_first, face_up[b - 1], face_up[b]),
                jnp.where(at_last, face_down[b + 1], face_down[b]),
            )
            g_ref[target, b * LANES : (b + 1) * LANES] = x[b] - rate * (face[b] - other)

        for k in range(-2, blocks + 3 * lag + 4):
            for act, behind, low, high in (
                (load, 0, -2, blocks + 1),
                (slope_in, lag, -1, blocks + 1),
                (reconstruct, 2 * lag + 1, -1, blocks),
                (store, 3 * lag + 2, 0, blocks - 1),
            ):
                if low <= k - behind <= high:
                    act(k - behind)
        return carry

    lax.fori_loop(0, rows // 8, row_step, 0)


def transport_call(stream, f, part):
    local, cells = f.shape
    rows = local // PARTS
    return pl.pallas_call(
        functools.partial(transport_kernel, part * rows),
        out_shape=pltpu.VMEM((rows, cells), jnp.float32),
        in_specs=[WHOLE, WHOLE],
        out_specs=WHOLE,
        compiler_params=params(4),
        name="transport",
    )(near(stream), near(f))


def fluid_kernel(moments_ref, coef_ref, macro_ref=None):
    blocks = moments_ref.shape[0] // SENT
    m = [moments_ref[row * blocks : (row + 1) * blocks, :] for row in range(13)]
    lane = lax.broadcasted_iota(jnp.int32, (blocks, LANES), 1)

    def following(x):
        turned = pltpu.roll(x, LANES - 1, 1)
        return jnp.where(lane == LANES - 1, pltpu.roll(turned, blocks - 1, 0), turned)

    def preceding(x):
        turned = pltpu.roll(x, 1, 1)
        return jnp.where(lane == 0, pltpu.roll(turned, 1, 0), turned)

    def power(x, exponent):
        return jnp.exp2(exponent * jnp.log2(x))

    def primitives(w):
        inverse = 1.0 / w[0]
        u = [w[1] * inverse, w[2] * inverse, w[3] * inverse]
        uu = u[0] * u[0] + u[1] * u[1] + u[2] * u[2]
        t = (2.0 * w[4] * inverse - uu) * (1.0 / 3.0)
        return u, uu, t

    n = m[0]
    w = [n, m[1], m[2], m[3], 0.5 * m[4]]
    u, uu, t = primitives(w)
    p = n * t
    second = [[m[5], m[6], m[7]], [m[6], m[8], m[9]], [m[7], m[9], m[4] - m[5] - m[8]]]
    stress = [m[5] - m[1] * u[0] - p, m[6] - m[1] * u[1], m[7] - m[1] * u[2]]
    q = []
    for i in range(3):
        along = second[i][0] * u[0] + second[i][1] * u[1] + second[i][2] * u[2]
        q.append(0.5 * (m[10 + i] - u[i] * m[4] - 2.0 * along + 2.0 * n * u[i] * uu))

    shear = SHEAR_REFERENCE * power(t, SHEAR_EXPONENT)
    high_order = [
        stress[i] + ((4.0 / 3.0 if i == 0 else 1.0) * 0.5) * shear * (following(u[i]) - preceding(u[i]))
        for i in range(3)
    ]
    high_order.append(q[0] + (3.75 * 0.5) * shear * (following(t) - preceding(t)))
    half_order = [0.5 * h for h in high_order]
    face_order = [h + following(h) for h in half_order]

    def sweep(w, u, t, shear):
        rates = jnp.abs(u[0]) + jnp.sqrt(ADIABATIC_INDEX * t)
        signal = jnp.max(jnp.max(rates, axis=0, keepdims=True), axis=1, keepdims=True)
        step = COURANT / signal
        p = w[0] * t
        euler = [w[1], w[1] * u[0] + p, w[1] * u[1], w[1] * u[2], (w[4] + p) * u[0]]
        next_u = [following(x) for x in u]
        half_shear = 0.5 * shear
        face_shear = half_shear + following(half_shear)
        sxx = face_order[0] - (4.0 / 3.0) * face_shear * (next_u[0] - u[0])
        sxy = face_order[1] - face_shear * (next_u[1] - u[1])
        sxz = face_order[2] - face_shear * (next_u[2] - u[2])
        heat = face_order[3] - 3.75 * face_shear * (following(t) - t)
        work = 0.5 * (
            sxx * (u[0] + next_u[0]) + sxy * (u[1] + next_u[1]) + sxz * (u[2] + next_u[2])
        )
        viscous = [None, sxx, sxy, sxz, work + heat]
        out = []
        for i in range(5):
            spread = signal * w[i]
            total = 0.5 * ((euler[i] + spread) + following(euler[i] - spread))
            if viscous[i] is not None:
                total = total + viscous[i]
            out.append(w[i] - step * (total - preceding(total)))
        return out

    w = sweep(w, u, t, shear)
    u, uu, t = primitives(w)
    w = sweep(w, u, t, SHEAR_REFERENCE * power(t, SHEAR_EXPONENT))
    u, uu, t = primitives(w)
    n = w[0]

    if macro_ref is not None:
        for row, field in enumerate([n, u[0], u[1], u[2], t, q[0], q[1], q[2]]):
            macro_ref[pl.ds(row, blocks, stride=8), :] = field

    inverse = 1.0 / t
    relax = n * power(t, 1.0 - SHEAR_EXPONENT)
    damp = 1.0 / (1.0 + relax)
    scale = n * inverse * lax.rsqrt(t) * relax * damp
    beta = scale * ((1.0 - CONDUCTIVE_SHARE) / 5.0) * inverse * inverse / n
    cubic = beta * inverse
    qu = q[0] * u[0] + q[1] * u[1] + q[2] * u[2]
    offset = beta * (uu * inverse - 5.0)
    twice = 2.0 * cubic
    zz = q[2] * u[2]
    polynomial = [
        scale - qu * offset,
        offset * q[0] + twice * qu * u[0],
        offset * q[1] + twice * qu * u[1],
        offset * q[2] + twice * qu * u[2],
        -cubic * (qu + 2.0 * zz),
        -twice * (q[0] * u[0] - zz),
        -twice * (q[0] * u[1] + q[1] * u[0]),
        -twice * (q[0] * u[2] + q[2] * u[0]),
        -twice * (q[1] * u[1] - zz),
        -twice * (q[1] * u[2] + q[2] * u[1]),
        cubic * q[0],
        cubic * q[1],
        cubic * q[2],
    ]
    zero = jnp.zeros_like(n)
    rate = (0.5 * LOG2E) * inverse
    exponent = [-rate * uu, 2.0 * rate * u[0], 2.0 * rate * u[1], 2.0 * rate * u[2], -rate]
    rows = polynomial + [damp, zero, zero] + exponent + [zero, zero, zero]
    for row, field in enumerate(rows):
        coef_ref[pl.ds(row, blocks, stride=COEF), :] = field


def fluid_call(moments, last):
    blocks = moments.shape[0] // SENT
    shapes = [pltpu.VMEM((blocks * COEF, LANES), jnp.float32)]
    if last:
        shapes.append(pltpu.VMEM((blocks * 8, LANES), jnp.float32))
    return pl.pallas_call(
        fluid_kernel,
        out_shape=shapes,
        in_specs=[WHOLE],
        out_specs=[WHOLE] * len(shapes),
        compiler_params=params(8),
        name="fluid",
    )(near(moments))


def relaxed(g, coef_ref, exponent_ref, polynomial_ref, tile):
    per_tile = TILE // LANES
    parts = [
        coef_ref[pl.ds((tile * per_tile + part) * COEF, COEF), :]
        for part in range(per_tile)
    ]
    coefficients = jnp.concatenate(parts, axis=1)
    polynomial = dot(polynomial_ref[...], expand_polynomial(coefficients[:BASIS]))
    exponent = dot(exponent_ref[...], expand_exponent(coefficients[BASIS:]))
    return g * coefficients[DAMP : DAMP + 1] + jnp.exp2(exponent) * polynomial


def gathered(g_refs, here):
    return jnp.concatenate([ref[:, here] for ref in g_refs], axis=0)


def update_kernel(*refs):
    g_refs = refs[:PARTS]
    coef_ref, exponent_ref, polynomial_ref, table_ref, f_ref, moments_ref = refs[PARTS:]
    cells = f_ref.shape[1]

    def front(tile):
        here = pl.ds(tile * TILE, TILE)
        return relaxed(gathered(g_refs, here), coef_ref, exponent_ref, polynomial_ref, tile)

    def back(tile, values):
        f_ref[:, tile * TILE : (tile + 1) * TILE] = values
        store_moments(moments_ref, table_ref[...], values, tile, cells // LANES)

    in_turn(front, back, cells // TILE)


def update_call(g, coefficients, tables, table):
    rows, cells = g[0].shape
    return pl.pallas_call(
        update_kernel,
        out_shape=(
            pltpu.VMEM((rows * PARTS, cells), jnp.float32),
            pltpu.VMEM((SENT * cells // LANES, LANES), jnp.float32),
        ),
        in_specs=[WHOLE] * (PARTS + 4),
        out_specs=(WHOLE, WHOLE),
        compiler_params=params(8),
        name="update",
    )(*map(near, g), near(coefficients), *map(near, tables), near(table))


def finish_kernel(*refs):
    g_refs = refs[:PARTS]
    coef_ref, macro_ref, exponent_ref, polynomial_ref, f_ref, fields_ref, held, sems = refs[PARTS:]
    cells = held.shape[1]
    width = cells // CHUNKS
    copies = []
    for chunk in range(CHUNKS):
        for local in range(width // TILE):
            tile = chunk * (width // TILE) + local
            here = pl.ds(tile * TILE, TILE)
            held[:, here] = relaxed(gathered(g_refs, here), coef_ref, exponent_ref, polynomial_ref, tile)
            for block in range(tile * TILE // LANES, (tile + 1) * TILE // LANES):
                fields_ref[:, pl.ds(block * LANES, LANES)] = macro_ref[pl.ds(block * 8, 8), :]
        there = pl.ds(chunk * width, width)
        copy = pltpu.make_async_copy(held.at[:, there], f_ref.at[:, there], sems.at[chunk])
        copy.start()
        copies.append(copy)
    for copy in copies:
        copy.wait()


def finish_call(g, coefficients, macro, tables):
    rows, cells = g[0].shape
    return pl.pallas_call(
        finish_kernel,
        out_shape=(
            jax.ShapeDtypeStruct((rows * PARTS, cells), jnp.float32),
            jax.ShapeDtypeStruct((8, cells), jnp.float32),
        ),
        in_specs=[WHOLE] * (PARTS + 4),
        out_specs=(OUTSIDE, WHOLE),
        scratch_shapes=[
            pltpu.VMEM((rows * PARTS, cells), jnp.float32),
            pltpu.SemaphoreType.DMA((CHUNKS,)),
        ],
        compiler_params=params(16),
        name="finish",
    )(*map(near, g), near(coefficients), near(macro), *map(near, tables))


def add_kernel(left_ref, right_ref, out_ref):
    out_ref[...] = left_ref[...] + right_ref[...]


def add_call(left, right):
    return pl.pallas_call(
        add_kernel,
        out_shape=pltpu.VMEM(left.shape, left.dtype),
        in_specs=[WHOLE, WHOLE],
        out_specs=WHOLE,
        compiler_params=params(1),
        name="add",
    )(near(left), near(right))


def plan(count):
    strides = [1 << bit for bit in range(count.bit_length() - 1)]
    return strides[:2], strides[2:]


def swap(values, count, stride):
    return lax.ppermute(values, "vel", [(device, device ^ stride) for device in range(count)])


def staged_sum(values, count, sides, f, tasks):
    splits, sums = plan(count)
    results, waiting, portions = [], list(tasks), list(BESIDE)

    def exchange(chunks, stride):
        got = [swap(chunk, count, stride) for chunk in chunks]
        portion = portions.pop(0) if portions else 0
        if portion:
            _, held = lax.optimization_barrier((chunks[-1], f))
            made = [task(held) for task in waiting[:portion]]
            del waiting[:portion]
            got[0], made = lax.optimization_barrier((got[0], made))
            results.extend(made)
        return got

    def split(chunks, stride, lower_side):
        kept, sent = [], []
        for chunk in chunks:
            half = chunk.shape[0] // 2
            first, second = chunk[:half], chunk[half:]
            kept.append(jnp.where(lower_side, first, second))
            sent.append(jnp.where(lower_side, second, first))
        sent = lax.optimization_barrier(sent)
        got = exchange(sent, stride)
        if len(chunks) == 1:
            return [kept[0] + got[0]]
        return [add_call(own, other) for own, other in zip(kept, got)]

    def join(chunks, stride, lower_side):
        out = []
        for own, got in zip(chunks, exchange(chunks, stride)):
            lower = jnp.where(lower_side, own, got)
            upper = jnp.where(lower_side, got, own)
            out.append((lower, upper))
        return out

    (block,) = split([values], splits[0], sides[0])
    half = block.shape[0] // 2
    chunks = [block[:half], block[half:]]
    for stride, lower_side in zip(splits[1:], sides[1:]):
        chunks = split(chunks, stride, lower_side)
    for stride in sums:
        chunks = [add_call(own, got) for own, got in zip(chunks, exchange(chunks, stride))]
    for stride, lower_side in reversed(list(zip(splits[1:], sides[1:]))):
        chunks = [jnp.concatenate(both, axis=0) for both in join(chunks, stride, lower_side)]
    lowers, uppers = zip(*join(chunks, splits[0], sides[0]))
    results.extend(task(f) for task in waiting)
    return jnp.concatenate(lowers + uppers, axis=0), results


def on_device(velocities, density, flow, thermal, deviation):
    count = lax.axis_size("vel")
    place = lax.axis_index("vel")
    sides = [place & stride == 0 for stride in plan(count)[0]]
    velocities, sides = lax.optimization_barrier((velocities, sides))
    f, moments, *tables, table, stream = start_call(
        velocities, density, flow, thermal, deviation, velocities.shape[1] * count
    )
    for iteration in range(ITERS):
        tasks = [
            functools.partial(lambda held, part: transport_call(stream, held, part), part=part)
            for part in range(PARTS)
        ]
        summed, g = staged_sum(moments, count, sides, f, tasks)
        last = iteration == ITERS - 1
        coefficients, *macro = fluid_call(summed, last)
        if not last:
            f, moments = update_call(g, coefficients, tables, table)
    return finish_call(g, coefficients, macro[0], tables)


def solution(mesh):
    return jax.shard_map(
        on_device,
        mesh=mesh,
        in_specs=(P(None, "vel"), P("grp"), P(None, "grp"), P("grp"), P("vel", "grp")),
        out_specs=(P("vel", "grp"), P(None, "grp")),
        check_vma=False,
    )
```

```python
import functools

import jax
import jax.numpy as jnp
from jax import lax
from jax.experimental import pallas as pl
from jax.experimental.pallas import tpu as pltpu
from jax.sharding import PartitionSpec as P

ITERS = 2

ADIABATIC_INDEX = 5.0 / 3.0
CONDUCTIVE_SHARE = 2.0 / 3.0
SHEAR_EXPONENT = 0.81
SHEAR_REFERENCE = 0.05
KINETIC_STEP = 0.05
COURANT = 0.4
SPREAD_SCALE = 1.5

LOG2E = 1.4426950408889634
LANES = 128
TILE = 256
BASIS = 16
SENT = 13
COEF = 24
DAMP = 13
ROWS = 64
CHUNKS = 8
PARTS = 8
BESIDE = (1, 2, 1, 1, 2, 1)
MIB = 1024 * 1024

WHOLE = pl.BlockSpec(memory_space=pltpu.VMEM)
OUTSIDE = pl.BlockSpec(memory_space=pltpu.HBM)


def params(mebibytes):
    return pltpu.CompilerParams(vmem_limit_bytes=mebibytes * MIB)


def near(values):
    return pltpu.with_memory_space_constraint(values, pltpu.VMEM)


def far(values):
    return pltpu.with_memory_space_constraint(values, pltpu.HBM)


def dot(left, right):
    return jnp.dot(left, right, preferred_element_type=jnp.float32)


def rounded(values):
    return values.astype(jnp.bfloat16).astype(jnp.float32)


def phi_rows(velocities):
    vx, vy, vz = velocities[0:1], velocities[1:2], velocities[2:3]
    sq = vx * vx + vy * vy + vz * vz
    zero = jnp.zeros_like(vx)
    rows = [
        jnp.ones_like(vx), vx, vy, vz, sq, vx * vx, vx * vy, vx * vz, vy * vy, vy * vz,
        vx * sq, vy * sq, vz * sq, zero, zero, zero,
    ]
    return jnp.concatenate(rows, axis=0), sq


def parts_of(values):
    high = rounded(values)
    middle = rounded(values - high)
    return high, middle, values - high - middle


def make_tables(velocities, total_count):
    phi, sq = phi_rows(velocities)
    high, middle, low = parts_of(phi)
    three = [high[:8], high[:8], high[:8], middle[:8], middle[:8], low[:8]]
    wide = jnp.zeros((128 - 6 * 8, phi.shape[1]), jnp.float32)
    exponent = jnp.concatenate(three + [wide], axis=0).T[:, : 6 * 8].astype(jnp.bfloat16)
    two = [high, high, middle]
    polynomial = jnp.concatenate(two + [wide], axis=0).T[:, : 3 * BASIS].astype(jnp.bfloat16)
    weighted = phi * (SPREAD_SCALE**3 * jnp.exp(sq / (2.0 * SPREAD_SCALE**2)) / total_count)
    top = rounded(weighted)
    rest = weighted - top
    moments = jnp.concatenate(
        [
            jnp.concatenate([top, top], axis=1),
            jnp.concatenate([rest, jnp.zeros_like(rest)], axis=1),
        ],
        axis=0,
    ).astype(jnp.bfloat16)
    return exponent, polynomial, moments


def expand_exponent(rows):
    high, middle, low = parts_of(rows)
    return jnp.concatenate([high, middle, low, high, middle, high], axis=0).astype(jnp.bfloat16)


def expand_polynomial(rows):
    high = rows.astype(jnp.bfloat16)
    middle = (rows - high.astype(jnp.float32)).astype(jnp.bfloat16)
    return jnp.concatenate([high, middle, high], axis=0)


def store_moments(moments_ref, table, split, tile, blocks):
    both = dot(table, split)
    sums = both[:BASIS] + both[BASIS:]
    per_tile = TILE // LANES
    for part in range(per_tile):
        block = tile * per_tile + part
        moments_ref[pl.ds(block, SENT, stride=blocks), :] = sums[
            :SENT, part * LANES : (part + 1) * LANES
        ]


def store_tile(f_ref, here, rows, values_of):
    high, low = [], []
    for first in range(0, rows, ROWS):
        some = pl.ds(first, ROWS)
        values = values_of(some)
        f_ref[some, here] = values
        high.append(values.astype(jnp.bfloat16))
        low.append((values - high[-1].astype(jnp.float32)).astype(jnp.bfloat16))
    return jnp.concatenate(high + low, axis=0)


def in_turn(front, back, tiles):
    made = front(0)
    for tile in range(1, tiles):
        upcoming = front(tile)
        back(tile - 1, made)
        made = upcoming
    back(tiles - 1, made)


def start_kernel(
    total_count,
    vel_hbm, density_hbm, flow_hbm, thermal_hbm, deviation_hbm,
    f_ref, moments_ref, exponent_ref, polynomial_ref, table_ref, stream_ref,
    vel_ref, density_ref, flow_ref, thermal_ref, deviation_ref, small_sems, sems,
):
    cells = f_ref.shape[1]
    width = cells // CHUNKS
    small = [
        pltpu.make_async_copy(source, target, small_sems.at[number])
        for number, (source, target) in enumerate(
            [
                (vel_hbm, vel_ref),
                (density_hbm, density_ref),
                (flow_hbm, flow_ref),
                (thermal_hbm, thermal_ref),
            ]
        )
    ]
    for copy in small:
        copy.start()
    copies = [
        pltpu.make_async_copy(
            deviation_hbm.at[:, pl.ds(chunk * width, width)],
            deviation_ref.at[:, pl.ds(chunk * width, width)],
            sems.at[chunk],
        )
        for chunk in range(CHUNKS)
    ]
    for copy in copies:
        copy.start()
    small[0].wait()
    exponent_table, polynomial_table, table = make_tables(vel_ref[...], total_count)
    exponent_ref[...] = exponent_table
    polynomial_ref[...] = polynomial_table
    table_ref[...] = table
    stream_ref[...] = jnp.broadcast_to(vel_ref[0:1, :], (LANES, vel_ref.shape[1])).T
    for copy in small[1:]:
        copy.wait()
    def front(tile):
        here = pl.ds(tile * TILE, TILE)
        density, flow, thermal = density_ref[:, here], flow_ref[:, here], thermal_ref[:, here]
        rate = (0.5 * LOG2E) / thermal
        speed_sq = flow[0:1] * flow[0:1] + flow[1:2] * flow[1:2] + flow[2:3] * flow[2:3]
        rows = [-rate * speed_sq, 2.0 * rate * flow, -rate, jnp.zeros((3, TILE), jnp.float32)]
        spread = expand_exponent(jnp.concatenate(rows, axis=0))
        scale = density / (thermal * jnp.sqrt(thermal))

        def values_of(some):
            exponent = dot(exponent_ref[some, :], spread)
            return jnp.exp2(exponent) * (scale * (1.0 + deviation_ref[some, here]))

        return store_tile(f_ref, here, f_ref.shape[0], values_of)

    def back(tile, split):
        store_moments(moments_ref, table, split, tile, cells // LANES)

    def front_when_here(tile):
        if tile * TILE % width == 0:
            copies[tile * TILE // width].wait()
        return front(tile)

    in_turn(front_when_here, back, cells // TILE)


def start_call(velocities, density, flow, thermal, deviation, total_count):
    local, cells = deviation.shape
    return pl.pallas_call(
        functools.partial(start_kernel, total_count),
        out_shape=(
            pltpu.VMEM((local, cells), jnp.float32),
            pltpu.VMEM((SENT * cells // LANES, LANES), jnp.float32),
            pltpu.VMEM((local, 6 * 8), jnp.bfloat16),
            pltpu.VMEM((local, 3 * BASIS), jnp.bfloat16),
            pltpu.VMEM((2 * BASIS, 2 * local), jnp.bfloat16),
            pltpu.VMEM((local, LANES), jnp.float32),
        ),
        in_specs=[OUTSIDE] * 5,
        out_specs=(WHOLE,) * 6,
        scratch_shapes=[
            pltpu.VMEM((3, local), jnp.float32),
            pltpu.VMEM((1, cells), jnp.float32),
            pltpu.VMEM((3, cells), jnp.float32),
            pltpu.VMEM((1, cells), jnp.float32),
            pltpu.VMEM((local, cells), jnp.float32),
            pltpu.SemaphoreType.DMA((4,)),
            pltpu.SemaphoreType.DMA((CHUNKS,)),
        ],
        compiler_params=params(16),
        name="start",
    )(
        far(velocities),
        far(density.reshape(1, cells)),
        far(flow),
        far(thermal.reshape(1, cells)),
        far(deviation),
    )


def transport_kernel(first_row, stream_ref, f_ref, g_ref):
    rows, cells = g_ref.shape
    blocks = cells // LANES
    lane = lax.broadcasted_iota(jnp.int32, (8, LANES), 1)
    at_first, at_last = lane == 0, lane == LANES - 1
    lag = 4

    def row_step(row_tile, carry):
        source = pl.ds(pl.multiple_of(first_row + row_tile * 8, 8), 8)
        target = pl.ds(pl.multiple_of(row_tile * 8, 8), 8)
        stream = stream_ref[source, :]
        upward = stream > 0
        rate = KINETIC_STEP * jnp.abs(stream)
        half = jnp.where(upward, 0.5, -0.5)
        x, up, rise, down, face, face_up, face_down = {}, {}, {}, {}, {}, {}, {}

        def load(b):
            at = (b % blocks) * LANES
            x[b] = f_ref[source, at : at + LANES]
            up[b] = pltpu.roll(x[b], 1, 1)

        def slope_in(b):
            rise[b] = x[b] - jnp.where(at_first, up[b - 1], up[b])
            down[b] = pltpu.roll(rise[b], LANES - 1, 1)

        def reconstruct(b):
            ahead = jnp.where(at_last, down[b + 1], down[b])
            slope = jnp.maximum(jnp.minimum(rise[b], ahead), 0.0) + jnp.minimum(
                jnp.maximum(rise[b], ahead), 0.0
            )
            face[b] = x[b] + half * slope
            face_up[b] = pltpu.roll(face[b], 1, 1)
            face_down[b] = pltpu.roll(face[b], LANES - 1, 1)

        def store(b):
            other = jnp.where(
                upward,
                jnp.where(at_first, face_up[b - 1], face_up[b]),
                jnp.where(at_last, face_down[b + 1], face_down[b]),
            )
            g_ref[target, b * LANES : (b + 1) * LANES] = x[b] - rate * (face[b] - other)

        for k in range(-2, blocks + 3 * lag + 4):
            for act, behind, low, high in (
                (load, 0, -2, blocks + 1),
                (slope_in, lag, -1, blocks + 1),
                (reconstruct, 2 * lag + 1, -1, blocks),
                (store, 3 * lag + 2, 0, blocks - 1),
            ):
                if low <= k - behind <= high:
                    act(k - behind)
        return carry

    lax.fori_loop(0, rows // 8, row_step, 0)


def transport_call(stream, f, part):
    local, cells = f.shape
    rows = local // PARTS
    return pl.pallas_call(
        functools.partial(transport_kernel, part * rows),
        out_shape=pltpu.VMEM((rows, cells), jnp.float32),
        in_specs=[WHOLE, WHOLE],
        out_specs=WHOLE,
        compiler_params=params(4),
        name="transport",
    )(near(stream), near(f))


def fluid_kernel(moments_ref, coef_ref, macro_ref=None):
    blocks = moments_ref.shape[0] // SENT
    m = [moments_ref[row * blocks : (row + 1) * blocks, :] for row in range(13)]
    lane = lax.broadcasted_iota(jnp.int32, (blocks, LANES), 1)

    def following(x):
        turned = pltpu.roll(x, LANES - 1, 1)
        return jnp.where(lane == LANES - 1, pltpu.roll(turned, blocks - 1, 0), turned)

    def preceding(x):
        turned = pltpu.roll(x, 1, 1)
        return jnp.where(lane == 0, pltpu.roll(turned, 1, 0), turned)

    def power(x, exponent):
        return jnp.exp2(exponent * jnp.log2(x))

    def primitives(w):
        inverse = 1.0 / w[0]
        u = [w[1] * inverse, w[2] * inverse, w[3] * inverse]
        uu = u[0] * u[0] + u[1] * u[1] + u[2] * u[2]
        t = (2.0 * w[4] * inverse - uu) * (1.0 / 3.0)
        return u, uu, t

    n = m[0]
    w = [n, m[1], m[2], m[3], 0.5 * m[4]]
    u, uu, t = primitives(w)
    p = n * t
    second = [[m[5], m[6], m[7]], [m[6], m[8], m[9]], [m[7], m[9], m[4] - m[5] - m[8]]]
    stress = [m[5] - m[1] * u[0] - p, m[6] - m[1] * u[1], m[7] - m[1] * u[2]]
    q = []
    for i in range(3):
        along = second[i][0] * u[0] + second[i][1] * u[1] + second[i][2] * u[2]
        q.append(0.5 * (m[10 + i] - u[i] * m[4] - 2.0 * along + 2.0 * n * u[i] * uu))

    shear = SHEAR_REFERENCE * power(t, SHEAR_EXPONENT)
    high_order = [
        stress[i] + ((4.0 / 3.0 if i == 0 else 1.0) * 0.5) * shear * (following(u[i]) - preceding(u[i]))
        for i in range(3)
    ]
    high_order.append(q[0] + (3.75 * 0.5) * shear * (following(t) - preceding(t)))
    half_order = [0.5 * h for h in high_order]
    face_order = [h + following(h) for h in half_order]

    def sweep(w, u, t, shear):
        rates = jnp.abs(u[0]) + jnp.sqrt(ADIABATIC_INDEX * t)
        signal = jnp.max(jnp.max(rates, axis=0, keepdims=True), axis=1, keepdims=True)
        step = COURANT / signal
        p = w[0] * t
        euler = [w[1], w[1] * u[0] + p, w[1] * u[1], w[1] * u[2], (w[4] + p) * u[0]]
        next_u = [following(x) for x in u]
        half_shear = 0.5 * shear
        face_shear = half_shear + following(half_shear)
        sxx = face_order[0] - (4.0 / 3.0) * face_shear * (next_u[0] - u[0])
        sxy = face_order[1] - face_shear * (next_u[1] - u[1])
        sxz = face_order[2] - face_shear * (next_u[2] - u[2])
        heat = face_order[3] - 3.75 * face_shear * (following(t) - t)
        work = 0.5 * (
            sxx * (u[0] + next_u[0]) + sxy * (u[1] + next_u[1]) + sxz * (u[2] + next_u[2])
        )
        viscous = [None, sxx, sxy, sxz, work + heat]
        out = []
        for i in range(5):
            spread = signal * w[i]
            total = 0.5 * ((euler[i] + spread) + following(euler[i] - spread))
            if viscous[i] is not None:
                total = total + viscous[i]
            out.append(w[i] - step * (total - preceding(total)))
        return out

    w = sweep(w, u, t, shear)
    u, uu, t = primitives(w)
    w = sweep(w, u, t, SHEAR_REFERENCE * power(t, SHEAR_EXPONENT))
    u, uu, t = primitives(w)
    n = w[0]

    if macro_ref is not None:
        for row, field in enumerate([n, u[0], u[1], u[2], t, q[0], q[1], q[2]]):
            macro_ref[pl.ds(row, blocks, stride=8), :] = field

    inverse = 1.0 / t
    relax = n * power(t, 1.0 - SHEAR_EXPONENT)
    damp = 1.0 / (1.0 + relax)
    scale = n * inverse * lax.rsqrt(t) * relax * damp
    beta = scale * ((1.0 - CONDUCTIVE_SHARE) / 5.0) * inverse * inverse / n
    cubic = beta * inverse
    qu = q[0] * u[0] + q[1] * u[1] + q[2] * u[2]
    offset = beta * (uu * inverse - 5.0)
    twice = 2.0 * cubic
    zz = q[2] * u[2]
    polynomial = [
        scale - qu * offset,
        offset * q[0] + twice * qu * u[0],
        offset * q[1] + twice * qu * u[1],
        offset * q[2] + twice * qu * u[2],
        -cubic * (qu + 2.0 * zz),
        -twice * (q[0] * u[0] - zz),
        -twice * (q[0] * u[1] + q[1] * u[0]),
        -twice * (q[0] * u[2] + q[2] * u[0]),
        -twice * (q[1] * u[1] - zz),
        -twice * (q[1] * u[2] + q[2] * u[1]),
        cubic * q[0],
        cubic * q[1],
        cubic * q[2],
    ]
    zero = jnp.zeros_like(n)
    rate = (0.5 * LOG2E) * inverse
    exponent = [-rate * uu, 2.0 * rate * u[0], 2.0 * rate * u[1], 2.0 * rate * u[2], -rate]
    rows = polynomial + [damp, zero, zero] + exponent + [zero, zero, zero]
    for row, field in enumerate(rows):
        coef_ref[pl.ds(row, blocks, stride=COEF), :] = field


def fluid_call(moments, last):
    blocks = moments.shape[0] // SENT
    shapes = [pltpu.VMEM((blocks * COEF, LANES), jnp.float32)]
    if last:
        shapes.append(pltpu.VMEM((blocks * 8, LANES), jnp.float32))
    return pl.pallas_call(
        fluid_kernel,
        out_shape=shapes,
        in_specs=[WHOLE],
        out_specs=[WHOLE] * len(shapes),
        compiler_params=params(8),
        name="fluid",
    )(near(moments))


def relaxed(g_refs, here, coef_ref, exponent_ref, polynomial_ref, tile):
    per_tile = TILE // LANES
    parts = [
        coef_ref[pl.ds((tile * per_tile + part) * COEF, COEF), :]
        for part in range(per_tile)
    ]
    coefficients = jnp.concatenate(parts, axis=1)
    cubic = expand_polynomial(coefficients[:BASIS])
    spread = expand_exponent(coefficients[BASIS:])
    rows = g_refs[0].shape[0]

    def values_of(some):
        polynomial = dot(polynomial_ref[some, :], cubic)
        exponent = dot(exponent_ref[some, :], spread)
        refs = g_refs[some.start // rows : (some.start + some.size) // rows]
        g = jnp.concatenate([ref[:, here] for ref in refs], axis=0)
        return g * coefficients[DAMP : DAMP + 1] + jnp.exp2(exponent) * polynomial

    return values_of


def update_kernel(*refs):
    g_refs = refs[:PARTS]
    coef_ref, exponent_ref, polynomial_ref, table_ref, f_ref, moments_ref = refs[PARTS:]
    cells = f_ref.shape[1]

    def front(tile):
        here = pl.ds(tile * TILE, TILE)
        values_of = relaxed(g_refs, here, coef_ref, exponent_ref, polynomial_ref, tile)
        return store_tile(f_ref, here, f_ref.shape[0], values_of)

    def back(tile, split):
        store_moments(moments_ref, table_ref[...], split, tile, cells // LANES)

    in_turn(front, back, cells // TILE)


def update_call(g, coefficients, tables, table):
    rows, cells = g[0].shape
    return pl.pallas_call(
        update_kernel,
        out_shape=(
            pltpu.VMEM((rows * PARTS, cells), jnp.float32),
            pltpu.VMEM((SENT * cells // LANES, LANES), jnp.float32),
        ),
        in_specs=[WHOLE] * (PARTS + 4),
        out_specs=(WHOLE, WHOLE),
        compiler_params=params(8),
        name="update",
    )(*map(near, g), near(coefficients), *map(near, tables), near(table))


def finish_kernel(*refs):
    g_refs = refs[:PARTS]
    coef_ref, macro_ref, exponent_ref, polynomial_ref, f_ref, fields_ref, held, sems = refs[PARTS:]
    cells = held.shape[1]
    width = cells // CHUNKS
    copies = []
    for chunk in range(CHUNKS):
        for local in range(width // TILE):
            tile = chunk * (width // TILE) + local
            here = pl.ds(tile * TILE, TILE)
            values_of = relaxed(g_refs, here, coef_ref, exponent_ref, polynomial_ref, tile)
            for first in range(0, held.shape[0], ROWS):
                held[pl.ds(first, ROWS), here] = values_of(pl.ds(first, ROWS))
            for block in range(tile * TILE // LANES, (tile + 1) * TILE // LANES):
                fields_ref[:, pl.ds(block * LANES, LANES)] = macro_ref[pl.ds(block * 8, 8), :]
        there = pl.ds(chunk * width, width)
        copy = pltpu.make_async_copy(held.at[:, there], f_ref.at[:, there], sems.at[chunk])
        copy.start()
        copies.append(copy)
    for copy in copies:
        copy.wait()


def finish_call(g, coefficients, macro, tables):
    rows, cells = g[0].shape
    return pl.pallas_call(
        finish_kernel,
        out_shape=(
            jax.ShapeDtypeStruct((rows * PARTS, cells), jnp.float32),
            jax.ShapeDtypeStruct((8, cells), jnp.float32),
        ),
        in_specs=[WHOLE] * (PARTS + 4),
        out_specs=(OUTSIDE, WHOLE),
        scratch_shapes=[
            pltpu.VMEM((rows * PARTS, cells), jnp.float32),
            pltpu.SemaphoreType.DMA((CHUNKS,)),
        ],
        compiler_params=params(16),
        name="finish",
    )(*map(near, g), near(coefficients), near(macro), *map(near, tables))


def add_kernel(left_ref, right_ref, out_ref):
    out_ref[...] = left_ref[...] + right_ref[...]


def add_call(left, right):
    return pl.pallas_call(
        add_kernel,
        out_shape=pltpu.VMEM(left.shape, left.dtype),
        in_specs=[WHOLE, WHOLE],
        out_specs=WHOLE,
        compiler_params=params(1),
        name="add",
    )(near(left), near(right))


def plan(count):
    strides = [1 << bit for bit in range(count.bit_length() - 1)]
    return strides[:2], strides[2:]


def swap(values, count, stride):
    return lax.ppermute(values, "vel", [(device, device ^ stride) for device in range(count)])


def staged_sum(values, count, sides, f, tasks):
    splits, sums = plan(count)
    results, waiting, portions = [], list(tasks), list(BESIDE)

    def exchange(chunks, stride):
        got = [swap(chunk, count, stride) for chunk in chunks]
        portion = portions.pop(0) if portions else 0
        if portion:
            _, held = lax.optimization_barrier((chunks[-1], f))
            made = [task(held) for task in waiting[:portion]]
            del waiting[:portion]
            got[0], made = lax.optimization_barrier((got[0], made))
            results.extend(made)
        return got

    def split(chunks, stride, lower_side):
        kept, sent = [], []
        for chunk in chunks:
            half = chunk.shape[0] // 2
            first, second = chunk[:half], chunk[half:]
            kept.append(jnp.where(lower_side, first, second))
            sent.append(jnp.where(lower_side, second, first))
        sent = lax.optimization_barrier(sent)
        got = exchange(sent, stride)
        if len(chunks) == 1:
            return [kept[0] + got[0]]
        return [add_call(own, other) for own, other in zip(kept, got)]

    def join(chunks, stride, lower_side):
        out = []
        for own, got in zip(chunks, exchange(chunks, stride)):
            lower = jnp.where(lower_side, own, got)
            upper = jnp.where(lower_side, got, own)
            out.append((lower, upper))
        return out

    (block,) = split([values], splits[0], sides[0])
    half = block.shape[0] // 2
    chunks = [block[:half], block[half:]]
    for stride, lower_side in zip(splits[1:], sides[1:]):
        chunks = split(chunks, stride, lower_side)
    for stride in sums:
        chunks = [add_call(own, got) for own, got in zip(chunks, exchange(chunks, stride))]
    for stride, lower_side in reversed(list(zip(splits[1:], sides[1:]))):
        chunks = [jnp.concatenate(both, axis=0) for both in join(chunks, stride, lower_side)]
    lowers, uppers = zip(*join(chunks, splits[0], sides[0]))
    results.extend(task(f) for task in waiting)
    return jnp.concatenate(lowers + uppers, axis=0), results


def on_device(velocities, density, flow, thermal, deviation):
    count = lax.axis_size("vel")
    place = lax.axis_index("vel")
    sides = [place & stride == 0 for stride in plan(count)[0]]
    velocities, sides = lax.optimization_barrier((velocities, sides))
    f, moments, *tables, table, stream = start_call(
        velocities, density, flow, thermal, deviation, velocities.shape[1] * count
    )
    for iteration in range(ITERS):
        tasks = [
            functools.partial(lambda held, part: transport_call(stream, held, part), part=part)
            for part in range(PARTS)
        ]
        summed, g = staged_sum(moments, count, sides, f, tasks)
        last = iteration == ITERS - 1
        coefficients, *macro = fluid_call(summed, last)
        if not last:
            f, moments = update_call(g, coefficients, tables, table)
    return finish_call(g, coefficients, macro[0], tables)


def solution(mesh):
    return jax.shard_map(
        on_device,
        mesh=mesh,
        in_specs=(P(None, "vel"), P("grp"), P(None, "grp"), P("grp"), P("vel", "grp")),
        out_specs=(P("vel", "grp"), P(None, "grp")),
        check_vma=False,
    )
```

```python
import functools

import jax
import jax.numpy as jnp
from jax import lax
from jax.experimental import pallas as pl
from jax.experimental.pallas import tpu as pltpu
from jax.sharding import PartitionSpec as P

ITERS = 2

ADIABATIC_INDEX = 5.0 / 3.0
CONDUCTIVE_SHARE = 2.0 / 3.0
SHEAR_EXPONENT = 0.81
SHEAR_REFERENCE = 0.05
KINETIC_STEP = 0.05
COURANT = 0.4
SPREAD_SCALE = 1.5

LOG2E = 1.4426950408889634
LANES = 128
TILE = 256
BASIS = 16
SENT = 13
COEF = 24
DAMP = 13
ROWS = 64
CHUNKS = 8
PARTS = 8
BESIDE = (1, 2, 1, 1, 2, 1)
MIB = 1024 * 1024

WHOLE = pl.BlockSpec(memory_space=pltpu.VMEM)
OUTSIDE = pl.BlockSpec(memory_space=pltpu.HBM)


def params(mebibytes):
    return pltpu.CompilerParams(vmem_limit_bytes=mebibytes * MIB)


def near(values):
    return pltpu.with_memory_space_constraint(values, pltpu.VMEM)


def far(values):
    return pltpu.with_memory_space_constraint(values, pltpu.HBM)


def dot(left, right):
    return jnp.dot(left, right, preferred_element_type=jnp.float32)


def rounded(values):
    return values.astype(jnp.bfloat16).astype(jnp.float32)


def phi_rows(velocities):
    vx, vy, vz = velocities[0:1], velocities[1:2], velocities[2:3]
    sq = vx * vx + vy * vy + vz * vz
    zero = jnp.zeros_like(vx)
    rows = [
        jnp.ones_like(vx), vx, vy, vz, sq, vx * vx, vx * vy, vx * vz, vy * vy, vy * vz,
        vx * sq, vy * sq, vz * sq, zero, zero, zero,
    ]
    return jnp.concatenate(rows, axis=0), sq


def parts_of(values):
    high = rounded(values)
    middle = rounded(values - high)
    return high, middle, values - high - middle


def make_tables(velocities, total_count):
    phi, sq = phi_rows(velocities)
    high, middle, low = parts_of(phi)
    three = [high[:8], high[:8], high[:8], middle[:8], middle[:8], low[:8]]
    wide = jnp.zeros((128 - 6 * 8, phi.shape[1]), jnp.float32)
    exponent = jnp.concatenate(three + [wide], axis=0).T[:, : 6 * 8].astype(jnp.bfloat16)
    two = [high, high, middle]
    polynomial = jnp.concatenate(two + [wide], axis=0).T[:, : 3 * BASIS].astype(jnp.bfloat16)
    weighted = phi * (SPREAD_SCALE**3 * jnp.exp(sq / (2.0 * SPREAD_SCALE**2)) / total_count)
    top = rounded(weighted)
    rest = weighted - top
    moments = jnp.concatenate(
        [
            jnp.concatenate([top, top], axis=1),
            jnp.concatenate([rest, jnp.zeros_like(rest)], axis=1),
        ],
        axis=0,
    ).astype(jnp.bfloat16)
    return exponent, polynomial, moments


def expand_exponent(rows):
    high, middle, low = parts_of(rows)
    return jnp.concatenate([high, middle, low, high, middle, high], axis=0).astype(jnp.bfloat16)


def expand_polynomial(rows):
    high = rows.astype(jnp.bfloat16)
    middle = (rows - high.astype(jnp.float32)).astype(jnp.bfloat16)
    return jnp.concatenate([high, middle, high], axis=0)


def store_moments(moments_ref, table, split, tile, blocks):
    both = dot(table, split)
    sums = both[:BASIS] + both[BASIS:]
    per_tile = TILE // LANES
    for part in range(per_tile):
        block = tile * per_tile + part
        moments_ref[pl.ds(block, SENT, stride=blocks), :] = sums[
            :SENT, part * LANES : (part + 1) * LANES
        ]


def store_tile(f_ref, here, rows, values_of):
    high, low = [], []
    for first in range(0, rows, ROWS):
        some = pl.ds(first, ROWS)
        values = values_of(some)
        f_ref[some, here] = values
        high.append(values.astype(jnp.bfloat16))
        low.append((values - high[-1].astype(jnp.float32)).astype(jnp.bfloat16))
    return jnp.concatenate(high + low, axis=0)


def tile_cells(tile):
    return pl.ds(pl.multiple_of(tile * TILE, TILE), TILE)


def in_turn(front, back, first, tiles):
    made = front(first)
    for tile in range(1, tiles):
        upcoming = front(first + tile)
        back(first + tile - 1, made)
        made = upcoming
    back(first + tiles - 1, made)


def start_kernel(
    total_count,
    vel_hbm, density_hbm, flow_hbm, thermal_hbm, deviation_hbm,
    f_ref, moments_ref, exponent_ref, polynomial_ref, table_ref, stream_ref,
    vel_ref, density_ref, flow_ref, thermal_ref, deviation_ref, small_sems, sems,
):
    cells = f_ref.shape[1]
    width = cells // CHUNKS
    small = [
        pltpu.make_async_copy(source, target, small_sems.at[number])
        for number, (source, target) in enumerate(
            [
                (vel_hbm, vel_ref),
                (density_hbm, density_ref),
                (flow_hbm, flow_ref),
                (thermal_hbm, thermal_ref),
            ]
        )
    ]
    for copy in small:
        copy.start()

    def arrival(chunk):
        there = pl.ds(pl.multiple_of(chunk * width, width), width)
        return pltpu.make_async_copy(
            deviation_hbm.at[:, there], deviation_ref.at[:, there], sems.at[chunk]
        )

    for chunk in range(CHUNKS):
        arrival(chunk).start()
    small[0].wait()
    exponent_table, polynomial_table, table = make_tables(vel_ref[...], total_count)
    exponent_ref[...] = exponent_table
    polynomial_ref[...] = polynomial_table
    table_ref[...] = table
    stream_ref[...] = jnp.broadcast_to(vel_ref[0:1, :], (LANES, vel_ref.shape[1])).T
    for copy in small[1:]:
        copy.wait()
    def front(tile):
        here = tile_cells(tile)
        density, flow, thermal = density_ref[:, here], flow_ref[:, here], thermal_ref[:, here]
        rate = (0.5 * LOG2E) / thermal
        speed_sq = flow[0:1] * flow[0:1] + flow[1:2] * flow[1:2] + flow[2:3] * flow[2:3]
        rows = [-rate * speed_sq, 2.0 * rate * flow, -rate, jnp.zeros((3, TILE), jnp.float32)]
        spread = expand_exponent(jnp.concatenate(rows, axis=0))
        scale = density / (thermal * jnp.sqrt(thermal))

        def values_of(some):
            exponent = dot(exponent_ref[some, :], spread)
            return jnp.exp2(exponent) * (scale * (1.0 + deviation_ref[some, here]))

        return store_tile(f_ref, here, f_ref.shape[0], values_of)

    def back(tile, split):
        store_moments(moments_ref, table_ref[...], split, tile, cells // LANES)

    def step(chunk, carry):
        arrival(chunk).wait()
        in_turn(front, back, chunk * (width // TILE), width // TILE)
        return carry

    lax.fori_loop(0, CHUNKS, step, 0)


def start_call(velocities, density, flow, thermal, deviation, total_count):
    local, cells = deviation.shape
    return pl.pallas_call(
        functools.partial(start_kernel, total_count),
        out_shape=(
            pltpu.VMEM((local, cells), jnp.float32),
            pltpu.VMEM((SENT * cells // LANES, LANES), jnp.float32),
            pltpu.VMEM((local, 6 * 8), jnp.bfloat16),
            pltpu.VMEM((local, 3 * BASIS), jnp.bfloat16),
            pltpu.VMEM((2 * BASIS, 2 * local), jnp.bfloat16),
            pltpu.VMEM((local, LANES), jnp.float32),
        ),
        in_specs=[OUTSIDE] * 5,
        out_specs=(WHOLE,) * 6,
        scratch_shapes=[
            pltpu.VMEM((3, local), jnp.float32),
            pltpu.VMEM((1, cells), jnp.float32),
            pltpu.VMEM((3, cells), jnp.float32),
            pltpu.VMEM((1, cells), jnp.float32),
            pltpu.VMEM((local, cells), jnp.float32),
            pltpu.SemaphoreType.DMA((4,)),
            pltpu.SemaphoreType.DMA((CHUNKS,)),
        ],
        compiler_params=params(16),
        name="start",
    )(
        far(velocities),
        far(density.reshape(1, cells)),
        far(flow),
        far(thermal.reshape(1, cells)),
        far(deviation),
    )


def transport_kernel(first_row, stream_ref, f_ref, g_ref):
    rows, cells = g_ref.shape
    blocks = cells // LANES
    lane = lax.broadcasted_iota(jnp.int32, (8, LANES), 1)
    at_first, at_last = lane == 0, lane == LANES - 1
    lag = 4

    def row_step(row_tile, carry):
        source = pl.ds(pl.multiple_of(first_row + row_tile * 8, 8), 8)
        target = pl.ds(pl.multiple_of(row_tile * 8, 8), 8)
        stream = stream_ref[source, :]
        upward = stream > 0
        rate = KINETIC_STEP * jnp.abs(stream)
        half = jnp.where(upward, 0.5, -0.5)
        x, up, rise, down, face, face_up, face_down = {}, {}, {}, {}, {}, {}, {}

        def load(b):
            at = (b % blocks) * LANES
            x[b] = f_ref[source, at : at + LANES]
            up[b] = pltpu.roll(x[b], 1, 1)

        def slope_in(b):
            rise[b] = x[b] - jnp.where(at_first, up[b - 1], up[b])
            down[b] = pltpu.roll(rise[b], LANES - 1, 1)

        def reconstruct(b):
            ahead = jnp.where(at_last, down[b + 1], down[b])
            slope = jnp.maximum(jnp.minimum(rise[b], ahead), 0.0) + jnp.minimum(
                jnp.maximum(rise[b], ahead), 0.0
            )
            face[b] = x[b] + half * slope
            face_up[b] = pltpu.roll(face[b], 1, 1)
            face_down[b] = pltpu.roll(face[b], LANES - 1, 1)

        def store(b):
            other = jnp.where(
                upward,
                jnp.where(at_first, face_up[b - 1], face_up[b]),
                jnp.where(at_last, face_down[b + 1], face_down[b]),
            )
            g_ref[target, b * LANES : (b + 1) * LANES] = x[b] - rate * (face[b] - other)

        for k in range(-2, blocks + 3 * lag + 4):
            for act, behind, low, high in (
                (load, 0, -2, blocks + 1),
                (slope_in, lag, -1, blocks + 1),
                (reconstruct, 2 * lag + 1, -1, blocks),
                (store, 3 * lag + 2, 0, blocks - 1),
            ):
                if low <= k - behind <= high:
                    act(k - behind)
        return carry

    lax.fori_loop(0, rows // 8, row_step, 0)


def transport_call(stream, f, part):
    local, cells = f.shape
    rows = local // PARTS
    return pl.pallas_call(
        functools.partial(transport_kernel, part * rows),
        out_shape=pltpu.VMEM((rows, cells), jnp.float32),
        in_specs=[WHOLE, WHOLE],
        out_specs=WHOLE,
        compiler_params=params(4),
        name="transport",
    )(near(stream), near(f))


def fluid_kernel(moments_ref, coef_ref, macro_ref=None):
    blocks = moments_ref.shape[0] // SENT
    m = [moments_ref[row * blocks : (row + 1) * blocks, :] for row in range(13)]
    lane = lax.broadcasted_iota(jnp.int32, (blocks, LANES), 1)

    def following(x):
        turned = pltpu.roll(x, LANES - 1, 1)
        return jnp.where(lane == LANES - 1, pltpu.roll(turned, blocks - 1, 0), turned)

    def preceding(x):
        turned = pltpu.roll(x, 1, 1)
        return jnp.where(lane == 0, pltpu.roll(turned, 1, 0), turned)

    def power(x, exponent):
        return jnp.exp2(exponent * jnp.log2(x))

    def primitives(w):
        inverse = 1.0 / w[0]
        u = [w[1] * inverse, w[2] * inverse, w[3] * inverse]
        uu = u[0] * u[0] + u[1] * u[1] + u[2] * u[2]
        t = (2.0 * w[4] * inverse - uu) * (1.0 / 3.0)
        return u, uu, t

    n = m[0]
    w = [n, m[1], m[2], m[3], 0.5 * m[4]]
    u, uu, t = primitives(w)
    p = n * t
    second = [[m[5], m[6], m[7]], [m[6], m[8], m[9]], [m[7], m[9], m[4] - m[5] - m[8]]]
    stress = [m[5] - m[1] * u[0] - p, m[6] - m[1] * u[1], m[7] - m[1] * u[2]]
    q = []
    for i in range(3):
        along = second[i][0] * u[0] + second[i][1] * u[1] + second[i][2] * u[2]
        q.append(0.5 * (m[10 + i] - u[i] * m[4] - 2.0 * along + 2.0 * n * u[i] * uu))

    shear = SHEAR_REFERENCE * power(t, SHEAR_EXPONENT)
    high_order = [
        stress[i] + ((4.0 / 3.0 if i == 0 else 1.0) * 0.5) * shear * (following(u[i]) - preceding(u[i]))
        for i in range(3)
    ]
    high_order.append(q[0] + (3.75 * 0.5) * shear * (following(t) - preceding(t)))
    half_order = [0.5 * h for h in high_order]
    face_order = [h + following(h) for h in half_order]

    def sweep(w, u, t, shear):
        rates = jnp.abs(u[0]) + jnp.sqrt(ADIABATIC_INDEX * t)
        signal = jnp.max(jnp.max(rates, axis=0, keepdims=True), axis=1, keepdims=True)
        step = COURANT / signal
        p = w[0] * t
        euler = [w[1], w[1] * u[0] + p, w[1] * u[1], w[1] * u[2], (w[4] + p) * u[0]]
        next_u = [following(x) for x in u]
        half_shear = 0.5 * shear
        face_shear = half_shear + following(half_shear)
        sxx = face_order[0] - (4.0 / 3.0) * face_shear * (next_u[0] - u[0])
        sxy = face_order[1] - face_shear * (next_u[1] - u[1])
        sxz = face_order[2] - face_shear * (next_u[2] - u[2])
        heat = face_order[3] - 3.75 * face_shear * (following(t) - t)
        work = 0.5 * (
            sxx * (u[0] + next_u[0]) + sxy * (u[1] + next_u[1]) + sxz * (u[2] + next_u[2])
        )
        viscous = [None, sxx, sxy, sxz, work + heat]
        out = []
        for i in range(5):
            spread = signal * w[i]
            total = 0.5 * ((euler[i] + spread) + following(euler[i] - spread))
            if viscous[i] is not None:
                total = total + viscous[i]
            out.append(w[i] - step * (total - preceding(total)))
        return out

    w = sweep(w, u, t, shear)
    u, uu, t = primitives(w)
    w = sweep(w, u, t, SHEAR_REFERENCE * power(t, SHEAR_EXPONENT))
    u, uu, t = primitives(w)
    n = w[0]

    if macro_ref is not None:
        for row, field in enumerate([n, u[0], u[1], u[2], t, q[0], q[1], q[2]]):
            macro_ref[pl.ds(row, blocks, stride=8), :] = field

    inverse = 1.0 / t
    relax = n * power(t, 1.0 - SHEAR_EXPONENT)
    damp = 1.0 / (1.0 + relax)
    scale = n * inverse * lax.rsqrt(t) * relax * damp
    beta = scale * ((1.0 - CONDUCTIVE_SHARE) / 5.0) * inverse * inverse / n
    cubic = beta * inverse
    qu = q[0] * u[0] + q[1] * u[1] + q[2] * u[2]
    offset = beta * (uu * inverse - 5.0)
    twice = 2.0 * cubic
    zz = q[2] * u[2]
    polynomial = [
        scale - qu * offset,
        offset * q[0] + twice * qu * u[0],
        offset * q[1] + twice * qu * u[1],
        offset * q[2] + twice * qu * u[2],
        -cubic * (qu + 2.0 * zz),
        -twice * (q[0] * u[0] - zz),
        -twice * (q[0] * u[1] + q[1] * u[0]),
        -twice * (q[0] * u[2] + q[2] * u[0]),
        -twice * (q[1] * u[1] - zz),
        -twice * (q[1] * u[2] + q[2] * u[1]),
        cubic * q[0],
        cubic * q[1],
        cubic * q[2],
    ]
    zero = jnp.zeros_like(n)
    rate = (0.5 * LOG2E) * inverse
    exponent = [-rate * uu, 2.0 * rate * u[0], 2.0 * rate * u[1], 2.0 * rate * u[2], -rate]
    rows = polynomial + [damp, zero, zero] + exponent + [zero, zero, zero]
    for row, field in enumerate(rows):
        coef_ref[pl.ds(row, blocks, stride=COEF), :] = field


def fluid_call(moments, last):
    blocks = moments.shape[0] // SENT
    shapes = [pltpu.VMEM((blocks * COEF, LANES), jnp.float32)]
    if last:
        shapes.append(pltpu.VMEM((blocks * 8, LANES), jnp.float32))
    return pl.pallas_call(
        fluid_kernel,
        out_shape=shapes,
        in_specs=[WHOLE],
        out_specs=[WHOLE] * len(shapes),
        compiler_params=params(8),
        name="fluid",
    )(near(moments))


def relaxed(g_refs, here, coef_ref, exponent_ref, polynomial_ref, tile):
    per_tile = TILE // LANES
    parts = [
        coef_ref[pl.ds(pl.multiple_of((tile * per_tile + part) * COEF, 8), COEF), :]
        for part in range(per_tile)
    ]
    coefficients = jnp.concatenate(parts, axis=1)
    cubic = expand_polynomial(coefficients[:BASIS])
    spread = expand_exponent(coefficients[BASIS:])
    rows = g_refs[0].shape[0]

    def values_of(some):
        polynomial = dot(polynomial_ref[some, :], cubic)
        exponent = dot(exponent_ref[some, :], spread)
        refs = g_refs[some.start // rows : (some.start + some.size) // rows]
        g = jnp.concatenate([ref[:, here] for ref in refs], axis=0)
        return g * coefficients[DAMP : DAMP + 1] + jnp.exp2(exponent) * polynomial

    return values_of


def update_kernel(*refs):
    g_refs = refs[:PARTS]
    coef_ref, exponent_ref, polynomial_ref, table_ref, f_ref, moments_ref = refs[PARTS:]
    cells = f_ref.shape[1]

    def front(tile):
        here = tile_cells(tile)
        values_of = relaxed(g_refs, here, coef_ref, exponent_ref, polynomial_ref, tile)
        return store_tile(f_ref, here, f_ref.shape[0], values_of)

    def back(tile, split):
        store_moments(moments_ref, table_ref[...], split, tile, cells // LANES)

    def step(chunk, carry):
        in_turn(front, back, chunk * (cells // CHUNKS // TILE), cells // CHUNKS // TILE)
        return carry

    lax.fori_loop(0, CHUNKS, step, 0)


def update_call(g, coefficients, tables, table):
    rows, cells = g[0].shape
    return pl.pallas_call(
        update_kernel,
        out_shape=(
            pltpu.VMEM((rows * PARTS, cells), jnp.float32),
            pltpu.VMEM((SENT * cells // LANES, LANES), jnp.float32),
        ),
        in_specs=[WHOLE] * (PARTS + 4),
        out_specs=(WHOLE, WHOLE),
        compiler_params=params(8),
        name="update",
    )(*map(near, g), near(coefficients), *map(near, tables), near(table))


def finish_kernel(*refs):
    g_refs = refs[:PARTS]
    coef_ref, macro_ref, exponent_ref, polynomial_ref, f_ref, fields_ref, held, sems = refs[PARTS:]
    cells = held.shape[1]
    width = cells // CHUNKS

    def departure(chunk):
        there = pl.ds(pl.multiple_of(chunk * width, width), width)
        return pltpu.make_async_copy(held.at[:, there], f_ref.at[:, there], sems.at[chunk])

    def step(chunk, carry):
        for local in range(width // TILE):
            tile = chunk * (width // TILE) + local
            here = tile_cells(tile)
            values_of = relaxed(g_refs, here, coef_ref, exponent_ref, polynomial_ref, tile)
            for first in range(0, held.shape[0], ROWS):
                held[pl.ds(first, ROWS), here] = values_of(pl.ds(first, ROWS))
            for part in range(TILE // LANES):
                block = tile * (TILE // LANES) + part
                fields_ref[:, pl.ds(pl.multiple_of(block * LANES, LANES), LANES)] = macro_ref[
                    pl.ds(pl.multiple_of(block * 8, 8), 8), :
                ]
        departure(chunk).start()
        return carry

    lax.fori_loop(0, CHUNKS, step, 0)
    for chunk in range(CHUNKS):
        departure(chunk).wait()


def finish_call(g, coefficients, macro, tables):
    rows, cells = g[0].shape
    return pl.pallas_call(
        finish_kernel,
        out_shape=(
            jax.ShapeDtypeStruct((rows * PARTS, cells), jnp.float32),
            jax.ShapeDtypeStruct((8, cells), jnp.float32),
        ),
        in_specs=[WHOLE] * (PARTS + 4),
        out_specs=(OUTSIDE, WHOLE),
        scratch_shapes=[
            pltpu.VMEM((rows * PARTS, cells), jnp.float32),
            pltpu.SemaphoreType.DMA((CHUNKS,)),
        ],
        compiler_params=params(16),
        name="finish",
    )(*map(near, g), near(coefficients), near(macro), *map(near, tables))


def add_kernel(left_ref, right_ref, out_ref):
    out_ref[...] = left_ref[...] + right_ref[...]


def add_call(left, right):
    return pl.pallas_call(
        add_kernel,
        out_shape=pltpu.VMEM(left.shape, left.dtype),
        in_specs=[WHOLE, WHOLE],
        out_specs=WHOLE,
        compiler_params=params(1),
        name="add",
    )(near(left), near(right))


def plan(count):
    strides = [1 << bit for bit in range(count.bit_length() - 1)]
    return strides[:2], strides[2:]


def swap(values, count, stride):
    return lax.ppermute(values, "vel", [(device, device ^ stride) for device in range(count)])


def staged_sum(values, count, sides, f, tasks):
    splits, sums = plan(count)
    results, waiting, portions = [], list(tasks), list(BESIDE)

    def exchange(chunks, stride):
        got = [swap(chunk, count, stride) for chunk in chunks]
        portion = portions.pop(0) if portions else 0
        if portion:
            _, held = lax.optimization_barrier((chunks[-1], f))
            made = [task(held) for task in waiting[:portion]]
            del waiting[:portion]
            got[0], made = lax.optimization_barrier((got[0], made))
            results.extend(made)
        return got

    def split(chunks, stride, lower_side):
        kept, sent = [], []
        for chunk in chunks:
            half = chunk.shape[0] // 2
            first, second = chunk[:half], chunk[half:]
            kept.append(jnp.where(lower_side, first, second))
            sent.append(jnp.where(lower_side, second, first))
        sent = lax.optimization_barrier(sent)
        got = exchange(sent, stride)
        if len(chunks) == 1:
            return [kept[0] + got[0]]
        return [add_call(own, other) for own, other in zip(kept, got)]

    def join(chunks, stride, lower_side):
        out = []
        for own, got in zip(chunks, exchange(chunks, stride)):
            lower = jnp.where(lower_side, own, got)
            upper = jnp.where(lower_side, got, own)
            out.append((lower, upper))
        return out

    (block,) = split([values], splits[0], sides[0])
    half = block.shape[0] // 2
    chunks = [block[:half], block[half:]]
    for stride, lower_side in zip(splits[1:], sides[1:]):
        chunks = split(chunks, stride, lower_side)
    for stride in sums:
        chunks = [add_call(own, got) for own, got in zip(chunks, exchange(chunks, stride))]
    for stride, lower_side in reversed(list(zip(splits[1:], sides[1:]))):
        chunks = [jnp.concatenate(both, axis=0) for both in join(chunks, stride, lower_side)]
    lowers, uppers = zip(*join(chunks, splits[0], sides[0]))
    results.extend(task(f) for task in waiting)
    return jnp.concatenate(lowers + uppers, axis=0), results


def on_device(velocities, density, flow, thermal, deviation):
    count = lax.axis_size("vel")
    place = lax.axis_index("vel")
    sides = [place & stride == 0 for stride in plan(count)[0]]
    velocities, sides = lax.optimization_barrier((velocities, sides))
    f, moments, *tables, table, stream = start_call(
        velocities, density, flow, thermal, deviation, velocities.shape[1] * count
    )
    for iteration in range(ITERS):
        tasks = [
            functools.partial(lambda held, part: transport_call(stream, held, part), part=part)
            for part in range(PARTS)
        ]
        summed, g = staged_sum(moments, count, sides, f, tasks)
        last = iteration == ITERS - 1
        coefficients, *macro = fluid_call(summed, last)
        if not last:
            f, moments = update_call(g, coefficients, tables, table)
    return finish_call(g, coefficients, macro[0], tables)


def solution(mesh):
    return jax.shard_map(
        on_device,
        mesh=mesh,
        in_specs=(P(None, "vel"), P("grp"), P(None, "grp"), P("grp"), P("vel", "grp")),
        out_specs=(P("vel", "grp"), P(None, "grp")),
        check_vma=False,
    )
```

```python
import functools

import jax
import jax.numpy as jnp
from jax import lax
from jax.experimental import pallas as pl
from jax.experimental.pallas import tpu as pltpu
from jax.sharding import PartitionSpec as P

ITERS = 2

ADIABATIC_INDEX = 5.0 / 3.0
CONDUCTIVE_SHARE = 2.0 / 3.0
SHEAR_EXPONENT = 0.81
SHEAR_REFERENCE = 0.05
KINETIC_STEP = 0.05
COURANT = 0.4
SPREAD_SCALE = 1.5

LOG2E = 1.4426950408889634
LANES = 128
TILE = 256
BASIS = 16
SENT = 13
COEF = 24
DAMP = 13
ROWS = 64
CHUNKS = 8
PARTS = 8
BESIDE = (1, 2, 2, 2, 1)
MIB = 1024 * 1024

WHOLE = pl.BlockSpec(memory_space=pltpu.VMEM)
OUTSIDE = pl.BlockSpec(memory_space=pltpu.HBM)


def params(mebibytes):
    return pltpu.CompilerParams(vmem_limit_bytes=mebibytes * MIB)


def near(values):
    return pltpu.with_memory_space_constraint(values, pltpu.VMEM)


def far(values):
    return pltpu.with_memory_space_constraint(values, pltpu.HBM)


def dot(left, right):
    return jnp.dot(left, right, preferred_element_type=jnp.float32)


def rounded(values):
    return values.astype(jnp.bfloat16).astype(jnp.float32)


def phi_rows(velocities):
    vx, vy, vz = velocities[0:1], velocities[1:2], velocities[2:3]
    sq = vx * vx + vy * vy + vz * vz
    zero = jnp.zeros_like(vx)
    rows = [
        jnp.ones_like(vx), vx, vy, vz, sq, vx * vx, vx * vy, vx * vz, vy * vy, vy * vz,
        vx * sq, vy * sq, vz * sq, zero, zero, zero,
    ]
    return jnp.concatenate(rows, axis=0), sq


def parts_of(values):
    high = rounded(values)
    middle = rounded(values - high)
    return high, middle, values - high - middle


def make_tables(velocities, total_count):
    phi, sq = phi_rows(velocities)
    high, middle, low = parts_of(phi)
    three = [high[:8], high[:8], high[:8], middle[:8], middle[:8], low[:8]]
    wide = jnp.zeros((128 - 6 * 8, phi.shape[1]), jnp.float32)
    exponent = jnp.concatenate(three + [wide], axis=0).T[:, : 6 * 8].astype(jnp.bfloat16)
    two = [high, high, middle]
    polynomial = jnp.concatenate(two + [wide], axis=0).T[:, : 3 * BASIS].astype(jnp.bfloat16)
    weighted = phi * (SPREAD_SCALE**3 * jnp.exp(sq / (2.0 * SPREAD_SCALE**2)) / total_count)
    top = rounded(weighted)
    rest = weighted - top
    moments = jnp.concatenate(
        [
            jnp.concatenate([top, top], axis=1),
            jnp.concatenate([rest, jnp.zeros_like(rest)], axis=1),
        ],
        axis=0,
    ).astype(jnp.bfloat16)
    return exponent, polynomial, moments


def expand_exponent(rows):
    high, middle, low = parts_of(rows)
    return jnp.concatenate([high, middle, low, high, middle, high], axis=0).astype(jnp.bfloat16)


def expand_polynomial(rows):
    high = rows.astype(jnp.bfloat16)
    middle = (rows - high.astype(jnp.float32)).astype(jnp.bfloat16)
    return jnp.concatenate([high, middle, high], axis=0)


def store_moments(moments_ref, table, split, tile, blocks):
    both = dot(table, split)
    sums = both[:BASIS] + both[BASIS:]
    per_tile = TILE // LANES
    for part in range(per_tile):
        block = tile * per_tile + part
        moments_ref[pl.ds(block, SENT, stride=blocks), :] = sums[
            :SENT, part * LANES : (part + 1) * LANES
        ]


def store_tile(f_ref, here, rows, values_of):
    high, low = [], []
    for first in range(0, rows, ROWS):
        some = pl.ds(first, ROWS)
        values = values_of(some)
        f_ref[some, here] = values
        high.append(values.astype(jnp.bfloat16))
        low.append((values - high[-1].astype(jnp.float32)).astype(jnp.bfloat16))
    return jnp.concatenate(high + low, axis=0)


def in_turn(front, back, tiles):
    made = front(0)
    for tile in range(1, tiles):
        upcoming = front(tile)
        back(tile - 1, made)
        made = upcoming
    back(tiles - 1, made)


def start_kernel(
    total_count,
    vel_hbm, density_hbm, flow_hbm, thermal_hbm, deviation_hbm,
    f_ref, moments_ref, exponent_ref, polynomial_ref, table_ref, stream_ref,
    vel_ref, density_ref, flow_ref, thermal_ref, deviation_ref, small_sems, sems,
):
    cells = f_ref.shape[1]
    width = cells // CHUNKS
    small = [
        pltpu.make_async_copy(source, target, small_sems.at[number])
        for number, (source, target) in enumerate(
            [
                (vel_hbm, vel_ref),
                (density_hbm, density_ref),
                (flow_hbm, flow_ref),
                (thermal_hbm, thermal_ref),
            ]
        )
    ]
    for copy in small:
        copy.start()
    copies = [
        pltpu.make_async_copy(
            deviation_hbm.at[:, pl.ds(chunk * width, width)],
            deviation_ref.at[:, pl.ds(chunk * width, width)],
            sems.at[chunk],
        )
        for chunk in range(CHUNKS)
    ]
    for copy in copies:
        copy.start()
    small[0].wait()
    exponent_table, polynomial_table, table = make_tables(vel_ref[...], total_count)
    exponent_ref[...] = exponent_table
    polynomial_ref[...] = polynomial_table
    table_ref[...] = table
    stream_ref[...] = jnp.broadcast_to(vel_ref[0:1, :], (LANES, vel_ref.shape[1])).T
    for copy in small[1:]:
        copy.wait()
    def front(tile):
        here = pl.ds(tile * TILE, TILE)
        density, flow, thermal = density_ref[:, here], flow_ref[:, here], thermal_ref[:, here]
        rate = (0.5 * LOG2E) / thermal
        speed_sq = flow[0:1] * flow[0:1] + flow[1:2] * flow[1:2] + flow[2:3] * flow[2:3]
        rows = [-rate * speed_sq, 2.0 * rate * flow, -rate, jnp.zeros((3, TILE), jnp.float32)]
        spread = expand_exponent(jnp.concatenate(rows, axis=0))
        scale = density / (thermal * jnp.sqrt(thermal))

        def values_of(some):
            exponent = dot(exponent_ref[some, :], spread)
            return jnp.exp2(exponent) * (scale * (1.0 + deviation_ref[some, here]))

        return store_tile(f_ref, here, f_ref.shape[0], values_of)

    def back(tile, split):
        store_moments(moments_ref, table, split, tile, cells // LANES)

    def front_when_here(tile):
        if tile * TILE % width == 0:
            copies[tile * TILE // width].wait()
        return front(tile)

    in_turn(front_when_here, back, cells // TILE)


def start_call(velocities, density, flow, thermal, deviation, total_count):
    local, cells = deviation.shape
    return pl.pallas_call(
        functools.partial(start_kernel, total_count),
        out_shape=(
            pltpu.VMEM((local, cells), jnp.float32),
            pltpu.VMEM((SENT * cells // LANES, LANES), jnp.float32),
            pltpu.VMEM((local, 6 * 8), jnp.bfloat16),
            pltpu.VMEM((local, 3 * BASIS), jnp.bfloat16),
            pltpu.VMEM((2 * BASIS, 2 * local), jnp.bfloat16),
            pltpu.VMEM((local, LANES), jnp.float32),
        ),
        in_specs=[OUTSIDE] * 5,
        out_specs=(WHOLE,) * 6,
        scratch_shapes=[
            pltpu.VMEM((3, local), jnp.float32),
            pltpu.VMEM((1, cells), jnp.float32),
            pltpu.VMEM((3, cells), jnp.float32),
            pltpu.VMEM((1, cells), jnp.float32),
            pltpu.VMEM((local, cells), jnp.float32),
            pltpu.SemaphoreType.DMA((4,)),
            pltpu.SemaphoreType.DMA((CHUNKS,)),
        ],
        compiler_params=params(16),
        name="start",
    )(
        far(velocities),
        far(density.reshape(1, cells)),
        far(flow),
        far(thermal.reshape(1, cells)),
        far(deviation),
    )


def transport_kernel(first_row, stream_ref, f_ref, g_ref):
    rows, cells = g_ref.shape
    blocks = cells // LANES
    lane = lax.broadcasted_iota(jnp.int32, (8, LANES), 1)
    at_first, at_last = lane == 0, lane == LANES - 1
    lag = 4

    def row_step(row_tile, carry):
        source = pl.ds(pl.multiple_of(first_row + row_tile * 8, 8), 8)
        target = pl.ds(pl.multiple_of(row_tile * 8, 8), 8)
        stream = stream_ref[source, :]
        upward = stream > 0
        rate = KINETIC_STEP * jnp.abs(stream)
        half = jnp.where(upward, 0.5, -0.5)
        x, up, rise, down, face, face_up, face_down = {}, {}, {}, {}, {}, {}, {}

        def load(b):
            at = (b % blocks) * LANES
            x[b] = f_ref[source, at : at + LANES]
            up[b] = pltpu.roll(x[b], 1, 1)

        def slope_in(b):
            rise[b] = x[b] - jnp.where(at_first, up[b - 1], up[b])
            down[b] = pltpu.roll(rise[b], LANES - 1, 1)

        def reconstruct(b):
            ahead = jnp.where(at_last, down[b + 1], down[b])
            slope = jnp.maximum(jnp.minimum(rise[b], ahead), 0.0) + jnp.minimum(
                jnp.maximum(rise[b], ahead), 0.0
            )
            face[b] = x[b] + half * slope
            face_up[b] = pltpu.roll(face[b], 1, 1)
            face_down[b] = pltpu.roll(face[b], LANES - 1, 1)

        def store(b):
            other = jnp.where(
                upward,
                jnp.where(at_first, face_up[b - 1], face_up[b]),
                jnp.where(at_last, face_down[b + 1], face_down[b]),
            )
            g_ref[target, b * LANES : (b + 1) * LANES] = x[b] - rate * (face[b] - other)

        for k in range(-2, blocks + 3 * lag + 4):
            for act, behind, low, high in (
                (load, 0, -2, blocks + 1),
                (slope_in, lag, -1, blocks + 1),
                (reconstruct, 2 * lag + 1, -1, blocks),
                (store, 3 * lag + 2, 0, blocks - 1),
            ):
                if low <= k - behind <= high:
                    act(k - behind)
        return carry

    lax.fori_loop(0, rows // 8, row_step, 0)


def transport_call(stream, f, part):
    local, cells = f.shape
    rows = local // PARTS
    return pl.pallas_call(
        functools.partial(transport_kernel, part * rows),
        out_shape=pltpu.VMEM((rows, cells), jnp.float32),
        in_specs=[WHOLE, WHOLE],
        out_specs=WHOLE,
        compiler_params=params(4),
        name="transport",
    )(near(stream), near(f))


def fluid_kernel(moments_ref, coef_ref, macro_ref=None):
    blocks = moments_ref.shape[0] // SENT
    m = [moments_ref[row * blocks : (row + 1) * blocks, :] for row in range(13)]
    lane = lax.broadcasted_iota(jnp.int32, (blocks, LANES), 1)

    def following(x):
        turned = pltpu.roll(x, LANES - 1, 1)
        return jnp.where(lane == LANES - 1, pltpu.roll(turned, blocks - 1, 0), turned)

    def preceding(x):
        turned = pltpu.roll(x, 1, 1)
        return jnp.where(lane == 0, pltpu.roll(turned, 1, 0), turned)

    def power(x, exponent):
        return jnp.exp2(exponent * jnp.log2(x))

    def primitives(w):
        inverse = 1.0 / w[0]
        u = [w[1] * inverse, w[2] * inverse, w[3] * inverse]
        uu = u[0] * u[0] + u[1] * u[1] + u[2] * u[2]
        t = (2.0 * w[4] * inverse - uu) * (1.0 / 3.0)
        return u, uu, t

    n = m[0]
    w = [n, m[1], m[2], m[3], 0.5 * m[4]]
    u, uu, t = primitives(w)
    p = n * t
    second = [[m[5], m[6], m[7]], [m[6], m[8], m[9]], [m[7], m[9], m[4] - m[5] - m[8]]]
    stress = [m[5] - m[1] * u[0] - p, m[6] - m[1] * u[1], m[7] - m[1] * u[2]]
    q = []
    for i in range(3):
        along = second[i][0] * u[0] + second[i][1] * u[1] + second[i][2] * u[2]
        q.append(0.5 * (m[10 + i] - u[i] * m[4] - 2.0 * along + 2.0 * n * u[i] * uu))

    shear = SHEAR_REFERENCE * power(t, SHEAR_EXPONENT)
    high_order = [
        stress[i] + ((4.0 / 3.0 if i == 0 else 1.0) * 0.5) * shear * (following(u[i]) - preceding(u[i]))
        for i in range(3)
    ]
    high_order.append(q[0] + (3.75 * 0.5) * shear * (following(t) - preceding(t)))
    half_order = [0.5 * h for h in high_order]
    face_order = [h + following(h) for h in half_order]

    def sweep(w, u, t, shear):
        rates = jnp.abs(u[0]) + jnp.sqrt(ADIABATIC_INDEX * t)
        signal = jnp.max(jnp.max(rates, axis=0, keepdims=True), axis=1, keepdims=True)
        step = COURANT / signal
        p = w[0] * t
        euler = [w[1], w[1] * u[0] + p, w[1] * u[1], w[1] * u[2], (w[4] + p) * u[0]]
        next_u = [following(x) for x in u]
        half_shear = 0.5 * shear
        face_shear = half_shear + following(half_shear)
        sxx = face_order[0] - (4.0 / 3.0) * face_shear * (next_u[0] - u[0])
        sxy = face_order[1] - face_shear * (next_u[1] - u[1])
        sxz = face_order[2] - face_shear * (next_u[2] - u[2])
        heat = face_order[3] - 3.75 * face_shear * (following(t) - t)
        work = 0.5 * (
            sxx * (u[0] + next_u[0]) + sxy * (u[1] + next_u[1]) + sxz * (u[2] + next_u[2])
        )
        viscous = [None, sxx, sxy, sxz, work + heat]
        out = []
        for i in range(5):
            spread = signal * w[i]
            total = 0.5 * ((euler[i] + spread) + following(euler[i] - spread))
            if viscous[i] is not None:
                total = total + viscous[i]
            out.append(w[i] - step * (total - preceding(total)))
        return out

    w = sweep(w, u, t, shear)
    u, uu, t = primitives(w)
    w = sweep(w, u, t, SHEAR_REFERENCE * power(t, SHEAR_EXPONENT))
    u, uu, t = primitives(w)
    n = w[0]

    if macro_ref is not None:
        for row, field in enumerate([n, u[0], u[1], u[2], t, q[0], q[1], q[2]]):
            macro_ref[pl.ds(row, blocks, stride=8), :] = field

    inverse = 1.0 / t
    relax = n * power(t, 1.0 - SHEAR_EXPONENT)
    damp = 1.0 / (1.0 + relax)
    scale = n * inverse * lax.rsqrt(t) * relax * damp
    beta = scale * ((1.0 - CONDUCTIVE_SHARE) / 5.0) * inverse * inverse / n
    cubic = beta * inverse
    qu = q[0] * u[0] + q[1] * u[1] + q[2] * u[2]
    offset = beta * (uu * inverse - 5.0)
    twice = 2.0 * cubic
    zz = q[2] * u[2]
    polynomial = [
        scale - qu * offset,
        offset * q[0] + twice * qu * u[0],
        offset * q[1] + twice * qu * u[1],
        offset * q[2] + twice * qu * u[2],
        -cubic * (qu + 2.0 * zz),
        -twice * (q[0] * u[0] - zz),
        -twice * (q[0] * u[1] + q[1] * u[0]),
        -twice * (q[0] * u[2] + q[2] * u[0]),
        -twice * (q[1] * u[1] - zz),
        -twice * (q[1] * u[2] + q[2] * u[1]),
        cubic * q[0],
        cubic * q[1],
        cubic * q[2],
    ]
    zero = jnp.zeros_like(n)
    rate = (0.5 * LOG2E) * inverse
    exponent = [-rate * uu, 2.0 * rate * u[0], 2.0 * rate * u[1], 2.0 * rate * u[2], -rate]
    rows = polynomial + [damp, zero, zero] + exponent + [zero, zero, zero]
    for row, field in enumerate(rows):
        coef_ref[pl.ds(row, blocks, stride=COEF), :] = field


def fluid_call(moments, last):
    blocks = moments.shape[0] // SENT
    shapes = [pltpu.VMEM((blocks * COEF, LANES), jnp.float32)]
    if last:
        shapes.append(pltpu.VMEM((blocks * 8, LANES), jnp.float32))
    return pl.pallas_call(
        fluid_kernel,
        out_shape=shapes,
        in_specs=[WHOLE],
        out_specs=[WHOLE] * len(shapes),
        compiler_params=params(8),
        name="fluid",
    )(near(moments))


def relaxed(g_refs, here, coef_ref, exponent_ref, polynomial_ref, tile):
    per_tile = TILE // LANES
    parts = [
        coef_ref[pl.ds((tile * per_tile + part) * COEF, COEF), :]
        for part in range(per_tile)
    ]
    coefficients = jnp.concatenate(parts, axis=1)
    cubic = expand_polynomial(coefficients[:BASIS])
    spread = expand_exponent(coefficients[BASIS:])
    rows = g_refs[0].shape[0]

    def values_of(some):
        polynomial = dot(polynomial_ref[some, :], cubic)
        exponent = dot(exponent_ref[some, :], spread)
        refs = g_refs[some.start // rows : (some.start + some.size) // rows]
        g = jnp.concatenate([ref[:, here] for ref in refs], axis=0)
        return g * coefficients[DAMP : DAMP + 1] + jnp.exp2(exponent) * polynomial

    return values_of


def update_kernel(*refs):
    g_refs = refs[:PARTS]
    coef_ref, exponent_ref, polynomial_ref, table_ref, f_ref, moments_ref = refs[PARTS:]
    cells = f_ref.shape[1]

    def front(tile):
        here = pl.ds(tile * TILE, TILE)
        values_of = relaxed(g_refs, here, coef_ref, exponent_ref, polynomial_ref, tile)
        return store_tile(f_ref, here, f_ref.shape[0], values_of)

    def back(tile, split):
        store_moments(moments_ref, table_ref[...], split, tile, cells // LANES)

    in_turn(front, back, cells // TILE)


def update_call(g, coefficients, tables, table):
    rows, cells = g[0].shape
    return pl.pallas_call(
        update_kernel,
        out_shape=(
            pltpu.VMEM((rows * PARTS, cells), jnp.float32),
            pltpu.VMEM((SENT * cells // LANES, LANES), jnp.float32),
        ),
        in_specs=[WHOLE] * (PARTS + 4),
        out_specs=(WHOLE, WHOLE),
        compiler_params=params(8),
        name="update",
    )(*map(near, g), near(coefficients), *map(near, tables), near(table))


def finish_kernel(*refs):
    g_refs = refs[:PARTS]
    coef_ref, macro_ref, exponent_ref, polynomial_ref, f_ref, fields_ref, held, sems = refs[PARTS:]
    cells = held.shape[1]
    width = cells // CHUNKS
    copies = []
    for chunk in range(CHUNKS):
        for local in range(width // TILE):
            tile = chunk * (width // TILE) + local
            here = pl.ds(tile * TILE, TILE)
            values_of = relaxed(g_refs, here, coef_ref, exponent_ref, polynomial_ref, tile)
            for first in range(0, held.shape[0], ROWS):
                held[pl.ds(first, ROWS), here] = values_of(pl.ds(first, ROWS))
            for block in range(tile * TILE // LANES, (tile + 1) * TILE // LANES):
                fields_ref[:, pl.ds(block * LANES, LANES)] = macro_ref[pl.ds(block * 8, 8), :]
        there = pl.ds(chunk * width, width)
        copy = pltpu.make_async_copy(held.at[:, there], f_ref.at[:, there], sems.at[chunk])
        copy.start()
        copies.append(copy)
    for copy in copies:
        copy.wait()


def finish_call(g, coefficients, macro, tables):
    rows, cells = g[0].shape
    return pl.pallas_call(
        finish_kernel,
        out_shape=(
            jax.ShapeDtypeStruct((rows * PARTS, cells), jnp.float32),
            jax.ShapeDtypeStruct((8, cells), jnp.float32),
        ),
        in_specs=[WHOLE] * (PARTS + 4),
        out_specs=(OUTSIDE, WHOLE),
        scratch_shapes=[
            pltpu.VMEM((rows * PARTS, cells), jnp.float32),
            pltpu.SemaphoreType.DMA((CHUNKS,)),
        ],
        compiler_params=params(16),
        name="finish",
    )(*map(near, g), near(coefficients), near(macro), *map(near, tables))


def add_kernel(left_ref, right_ref, out_ref):
    out_ref[...] = left_ref[...] + right_ref[...]


def add_call(left, right):
    return pl.pallas_call(
        add_kernel,
        out_shape=pltpu.VMEM(left.shape, left.dtype),
        in_specs=[WHOLE, WHOLE],
        out_specs=WHOLE,
        compiler_params=params(1),
        name="add",
    )(near(left), near(right))


def swap(values, count, stride):
    return lax.ppermute(values, "vel", [(device, device ^ stride) for device in range(count)])


def staged_sum(values, count, even, f, tasks):
    strides = [1 << bit for bit in range(1, count.bit_length() - 1)]
    orders = (strides, strides[1:] + strides[:1])
    results, waiting, portions = [], list(tasks), list(BESIDE)

    def exchange(chunks, chosen):
        got = [swap(chunk, count, stride) for chunk, stride in zip(chunks, chosen)]
        portion = portions.pop(0) if portions else 0
        if portion:
            _, held = lax.optimization_barrier((chunks[-1], f))
            made = [task(held) for task in waiting[:portion]]
            del waiting[:portion]
            got[0], made = lax.optimization_barrier((got[0], made))
            results.extend(made)
        return got

    half = values.shape[0] // 2
    first, second = values[:half], values[half:]
    kept, sent = jnp.where(even, first, second), jnp.where(even, second, first)
    (got,) = exchange([sent], [1])
    block = kept + got
    chunks = lax.optimization_barrier([block[: half // 2], block[half // 2 :]])
    for chosen in zip(*orders):
        chunks = [add_call(own, got) for own, got in zip(chunks, exchange(chunks, chosen))]
    got = exchange(chunks, [1, 1])
    results.extend(task(f) for task in waiting)
    lower = [jnp.where(even, own, other) for own, other in zip(chunks, got)]
    upper = [jnp.where(even, other, own) for own, other in zip(chunks, got)]
    return jnp.concatenate(lower + upper, axis=0), results


def on_device(velocities, density, flow, thermal, deviation):
    count = lax.axis_size("vel")
    velocities, even = lax.optimization_barrier((velocities, lax.axis_index("vel") & 1 == 0))
    f, moments, *tables, table, stream = start_call(
        velocities, density, flow, thermal, deviation, velocities.shape[1] * count
    )
    for iteration in range(ITERS):
        tasks = [
            functools.partial(lambda held, part: transport_call(stream, held, part), part=part)
            for part in range(PARTS)
        ]
        summed, g = staged_sum(moments, count, even, f, tasks)
        last = iteration == ITERS - 1
        coefficients, *macro = fluid_call(summed, last)
        if not last:
            f, moments = update_call(g, coefficients, tables, table)
    return finish_call(g, coefficients, macro[0], tables)


def solution(mesh):
    return jax.shard_map(
        on_device,
        mesh=mesh,
        in_specs=(P(None, "vel"), P("grp"), P(None, "grp"), P("grp"), P("vel", "grp")),
        out_specs=(P("vel", "grp"), P(None, "grp")),
        check_vma=False,
    )
```

```python
import functools

import jax
import jax.numpy as jnp
from jax import lax
from jax.experimental import pallas as pl
from jax.experimental.pallas import tpu as pltpu
from jax.sharding import PartitionSpec as P

ITERS = 2

ADIABATIC_INDEX = 5.0 / 3.0
CONDUCTIVE_SHARE = 2.0 / 3.0
SHEAR_EXPONENT = 0.81
SHEAR_REFERENCE = 0.05
KINETIC_STEP = 0.05
COURANT = 0.4
SPREAD_SCALE = 1.5

LOG2E = 1.4426950408889634
LANES = 128
TILE = 256
BASIS = 16
SENT = 13
COEF = 24
DAMP = 13
ROWS = 64
CHUNKS = 8
DEPARTURES = 16
PARTS = 8
BESIDE = (1, 2, 1, 1, 2, 1)
MIB = 1024 * 1024

WHOLE = pl.BlockSpec(memory_space=pltpu.VMEM)
OUTSIDE = pl.BlockSpec(memory_space=pltpu.HBM)


def params(mebibytes):
    return pltpu.CompilerParams(vmem_limit_bytes=mebibytes * MIB)


def near(values):
    return pltpu.with_memory_space_constraint(values, pltpu.VMEM)


def far(values):
    return pltpu.with_memory_space_constraint(values, pltpu.HBM)


def dot(left, right):
    return jnp.dot(left, right, preferred_element_type=jnp.float32)


def rounded(values):
    return values.astype(jnp.bfloat16).astype(jnp.float32)


def phi_rows(velocities):
    vx, vy, vz = velocities[0:1], velocities[1:2], velocities[2:3]
    sq = vx * vx + vy * vy + vz * vz
    zero = jnp.zeros_like(vx)
    rows = [
        jnp.ones_like(vx), vx, vy, vz, sq, vx * vx, vx * vy, vx * vz, vy * vy, vy * vz,
        vx * sq, vy * sq, vz * sq, zero, zero, zero,
    ]
    return jnp.concatenate(rows, axis=0), sq


def parts_of(values):
    high = rounded(values)
    middle = rounded(values - high)
    return high, middle, values - high - middle


def make_tables(velocities, total_count):
    phi, sq = phi_rows(velocities)
    high, middle, low = parts_of(phi)
    three = [high[:8], high[:8], high[:8], middle[:8], middle[:8], low[:8]]
    wide = jnp.zeros((128 - 6 * 8, phi.shape[1]), jnp.float32)
    exponent = jnp.concatenate(three + [wide], axis=0).T[:, : 6 * 8].astype(jnp.bfloat16)
    two = [high, high, middle]
    polynomial = jnp.concatenate(two + [wide], axis=0).T[:, : 3 * BASIS].astype(jnp.bfloat16)
    weighted = phi * (SPREAD_SCALE**3 * jnp.exp(sq / (2.0 * SPREAD_SCALE**2)) / total_count)
    top = rounded(weighted)
    rest = weighted - top
    moments = jnp.concatenate(
        [
            jnp.concatenate([top, top], axis=1),
            jnp.concatenate([rest, jnp.zeros_like(rest)], axis=1),
        ],
        axis=0,
    ).astype(jnp.bfloat16)
    return exponent, polynomial, moments


def expand_exponent(rows):
    high, middle, low = parts_of(rows)
    return jnp.concatenate([high, middle, low, high, middle, high], axis=0).astype(jnp.bfloat16)


def expand_polynomial(rows):
    high = rows.astype(jnp.bfloat16)
    middle = (rows - high.astype(jnp.float32)).astype(jnp.bfloat16)
    return jnp.concatenate([high, middle, high], axis=0)


def store_moments(moments_ref, table, split, tile, blocks):
    both = dot(table, split)
    sums = both[:BASIS] + both[BASIS:]
    per_tile = TILE // LANES
    for part in range(per_tile):
        block = tile * per_tile + part
        moments_ref[pl.ds(block, SENT, stride=blocks), :] = sums[
            :SENT, part * LANES : (part + 1) * LANES
        ]


def store_tile(f_ref, here, rows, values_of):
    high, low = [], []
    for first in range(0, rows, ROWS):
        some = pl.ds(first, ROWS)
        values = values_of(some)
        f_ref[some, here] = values
        high.append(values.astype(jnp.bfloat16))
        low.append((values - high[-1].astype(jnp.float32)).astype(jnp.bfloat16))
    return jnp.concatenate(high + low, axis=0)


def in_turn(front, back, tiles):
    made = front(0)
    for tile in range(1, tiles):
        upcoming = front(tile)
        back(tile - 1, made)
        made = upcoming
    back(tiles - 1, made)


def start_kernel(
    total_count,
    vel_hbm, density_hbm, flow_hbm, thermal_hbm, deviation_hbm,
    f_ref, moments_ref, exponent_ref, polynomial_ref, table_ref, stream_ref,
    vel_ref, density_ref, flow_ref, thermal_ref, deviation_ref, small_sems, sems,
):
    cells = f_ref.shape[1]
    width = cells // CHUNKS
    small = [
        pltpu.make_async_copy(source, target, small_sems.at[number])
        for number, (source, target) in enumerate(
            [
                (vel_hbm, vel_ref),
                (density_hbm, density_ref),
                (flow_hbm, flow_ref),
                (thermal_hbm, thermal_ref),
            ]
        )
    ]
    for copy in small:
        copy.start()
    copies = [
        pltpu.make_async_copy(
            deviation_hbm.at[:, pl.ds(chunk * width, width)],
            deviation_ref.at[:, pl.ds(chunk * width, width)],
            sems.at[chunk],
        )
        for chunk in range(CHUNKS)
    ]
    for copy in copies:
        copy.start()
    small[0].wait()
    exponent_table, polynomial_table, table = make_tables(vel_ref[...], total_count)
    exponent_ref[...] = exponent_table
    polynomial_ref[...] = polynomial_table
    table_ref[...] = table
    stream_ref[...] = jnp.broadcast_to(vel_ref[0:1, :], (LANES, vel_ref.shape[1])).T
    for copy in small[1:]:
        copy.wait()
    def front(tile):
        here = pl.ds(tile * TILE, TILE)
        density, flow, thermal = density_ref[:, here], flow_ref[:, here], thermal_ref[:, here]
        rate = (0.5 * LOG2E) / thermal
        speed_sq = flow[0:1] * flow[0:1] + flow[1:2] * flow[1:2] + flow[2:3] * flow[2:3]
        rows = [-rate * speed_sq, 2.0 * rate * flow, -rate, jnp.zeros((3, TILE), jnp.float32)]
        spread = expand_exponent(jnp.concatenate(rows, axis=0))
        scale = density / (thermal * jnp.sqrt(thermal))

        def values_of(some):
            exponent = dot(exponent_ref[some, :], spread)
            return jnp.exp2(exponent) * (scale * (1.0 + deviation_ref[some, here]))

        return store_tile(f_ref, here, f_ref.shape[0], values_of)

    def back(tile, split):
        store_moments(moments_ref, table, split, tile, cells // LANES)

    def front_when_here(tile):
        if tile * TILE % width == 0:
            copies[tile * TILE // width].wait()
        return front(tile)

    in_turn(front_when_here, back, cells // TILE)


def start_call(velocities, density, flow, thermal, deviation, total_count):
    local, cells = deviation.shape
    return pl.pallas_call(
        functools.partial(start_kernel, total_count),
        out_shape=(
            pltpu.VMEM((local, cells), jnp.float32),
            pltpu.VMEM((SENT * cells // LANES, LANES), jnp.float32),
            pltpu.VMEM((local, 6 * 8), jnp.bfloat16),
            pltpu.VMEM((local, 3 * BASIS), jnp.bfloat16),
            pltpu.VMEM((2 * BASIS, 2 * local), jnp.bfloat16),
            pltpu.VMEM((local, LANES), jnp.float32),
        ),
        in_specs=[OUTSIDE] * 5,
        out_specs=(WHOLE,) * 6,
        scratch_shapes=[
            pltpu.VMEM((3, local), jnp.float32),
            pltpu.VMEM((1, cells), jnp.float32),
            pltpu.VMEM((3, cells), jnp.float32),
            pltpu.VMEM((1, cells), jnp.float32),
            pltpu.VMEM((local, cells), jnp.float32),
            pltpu.SemaphoreType.DMA((4,)),
            pltpu.SemaphoreType.DMA((CHUNKS,)),
        ],
        compiler_params=params(16),
        name="start",
    )(
        far(velocities),
        far(density.reshape(1, cells)),
        far(flow),
        far(thermal.reshape(1, cells)),
        far(deviation),
    )


def transport_kernel(first_row, stream_ref, f_ref, g_ref):
    rows, cells = g_ref.shape
    blocks = cells // LANES
    lane = lax.broadcasted_iota(jnp.int32, (8, LANES), 1)
    at_first, at_last = lane == 0, lane == LANES - 1
    lag = 4

    def row_step(row_tile, carry):
        source = pl.ds(pl.multiple_of(first_row + row_tile * 8, 8), 8)
        target = pl.ds(pl.multiple_of(row_tile * 8, 8), 8)
        stream = stream_ref[source, :]
        upward = stream > 0
        rate = KINETIC_STEP * jnp.abs(stream)
        half = jnp.where(upward, 0.5, -0.5)
        x, up, rise, down, face, face_up, face_down = {}, {}, {}, {}, {}, {}, {}

        def load(b):
            at = (b % blocks) * LANES
            x[b] = f_ref[source, at : at + LANES]
            up[b] = pltpu.roll(x[b], 1, 1)

        def slope_in(b):
            rise[b] = x[b] - jnp.where(at_first, up[b - 1], up[b])
            down[b] = pltpu.roll(rise[b], LANES - 1, 1)

        def reconstruct(b):
            ahead = jnp.where(at_last, down[b + 1], down[b])
            slope = jnp.maximum(jnp.minimum(rise[b], ahead), 0.0) + jnp.minimum(
                jnp.maximum(rise[b], ahead), 0.0
            )
            face[b] = x[b] + half * slope
            face_up[b] = pltpu.roll(face[b], 1, 1)
            face_down[b] = pltpu.roll(face[b], LANES - 1, 1)

        def store(b):
            other = jnp.where(
                upward,
                jnp.where(at_first, face_up[b - 1], face_up[b]),
                jnp.where(at_last, face_down[b + 1], face_down[b]),
            )
            g_ref[target, b * LANES : (b + 1) * LANES] = x[b] - rate * (face[b] - other)

        for k in range(-2, blocks + 3 * lag + 4):
            for act, behind, low, high in (
                (load, 0, -2, blocks + 1),
                (slope_in, lag, -1, blocks + 1),
                (reconstruct, 2 * lag + 1, -1, blocks),
                (store, 3 * lag + 2, 0, blocks - 1),
            ):
                if low <= k - behind <= high:
                    act(k - behind)
        return carry

    lax.fori_loop(0, rows // 8, row_step, 0)


def transport_call(stream, f, part):
    local, cells = f.shape
    rows = local // PARTS
    return pl.pallas_call(
        functools.partial(transport_kernel, part * rows),
        out_shape=pltpu.VMEM((rows, cells), jnp.float32),
        in_specs=[WHOLE, WHOLE],
        out_specs=WHOLE,
        compiler_params=params(4),
        name="transport",
    )(near(stream), near(f))


def fluid_kernel(moments_ref, coef_ref, macro_ref=None):
    blocks = moments_ref.shape[0] // SENT
    m = [moments_ref[row * blocks : (row + 1) * blocks, :] for row in range(13)]
    lane = lax.broadcasted_iota(jnp.int32, (blocks, LANES), 1)

    def following(x):
        turned = pltpu.roll(x, LANES - 1, 1)
        return jnp.where(lane == LANES - 1, pltpu.roll(turned, blocks - 1, 0), turned)

    def preceding(x):
        turned = pltpu.roll(x, 1, 1)
        return jnp.where(lane == 0, pltpu.roll(turned, 1, 0), turned)

    def power(x, exponent):
        return jnp.exp2(exponent * jnp.log2(x))

    def primitives(w):
        inverse = 1.0 / w[0]
        u = [w[1] * inverse, w[2] * inverse, w[3] * inverse]
        uu = u[0] * u[0] + u[1] * u[1] + u[2] * u[2]
        t = (2.0 * w[4] * inverse - uu) * (1.0 / 3.0)
        return u, uu, t

    n = m[0]
    w = [n, m[1], m[2], m[3], 0.5 * m[4]]
    u, uu, t = primitives(w)
    p = n * t
    second = [[m[5], m[6], m[7]], [m[6], m[8], m[9]], [m[7], m[9], m[4] - m[5] - m[8]]]
    stress = [m[5] - m[1] * u[0] - p, m[6] - m[1] * u[1], m[7] - m[1] * u[2]]
    q = []
    for i in range(3):
        along = second[i][0] * u[0] + second[i][1] * u[1] + second[i][2] * u[2]
        q.append(0.5 * (m[10 + i] - u[i] * m[4] - 2.0 * along + 2.0 * n * u[i] * uu))

    shear = SHEAR_REFERENCE * power(t, SHEAR_EXPONENT)
    high_order = [
        stress[i] + ((4.0 / 3.0 if i == 0 else 1.0) * 0.5) * shear * (following(u[i]) - preceding(u[i]))
        for i in range(3)
    ]
    high_order.append(q[0] + (3.75 * 0.5) * shear * (following(t) - preceding(t)))
    half_order = [0.5 * h for h in high_order]
    face_order = [h + following(h) for h in half_order]

    def sweep(w, u, t, shear):
        rates = jnp.abs(u[0]) + jnp.sqrt(ADIABATIC_INDEX * t)
        signal = jnp.max(jnp.max(rates, axis=0, keepdims=True), axis=1, keepdims=True)
        step = COURANT / signal
        p = w[0] * t
        euler = [w[1], w[1] * u[0] + p, w[1] * u[1], w[1] * u[2], (w[4] + p) * u[0]]
        next_u = [following(x) for x in u]
        half_shear = 0.5 * shear
        face_shear = half_shear + following(half_shear)
        sxx = face_order[0] - (4.0 / 3.0) * face_shear * (next_u[0] - u[0])
        sxy = face_order[1] - face_shear * (next_u[1] - u[1])
        sxz = face_order[2] - face_shear * (next_u[2] - u[2])
        heat = face_order[3] - 3.75 * face_shear * (following(t) - t)
        work = 0.5 * (
            sxx * (u[0] + next_u[0]) + sxy * (u[1] + next_u[1]) + sxz * (u[2] + next_u[2])
        )
        viscous = [None, sxx, sxy, sxz, work + heat]
        out = []
        for i in range(5):
            spread = signal * w[i]
            total = 0.5 * ((euler[i] + spread) + following(euler[i] - spread))
            if viscous[i] is not None:
                total = total + viscous[i]
            out.append(w[i] - step * (total - preceding(total)))
        return out

    w = sweep(w, u, t, shear)
    u, uu, t = primitives(w)
    w = sweep(w, u, t, SHEAR_REFERENCE * power(t, SHEAR_EXPONENT))
    u, uu, t = primitives(w)
    n = w[0]

    if macro_ref is not None:
        for row, field in enumerate([n, u[0], u[1], u[2], t, q[0], q[1], q[2]]):
            macro_ref[pl.ds(row, blocks, stride=8), :] = field

    inverse = 1.0 / t
    relax = n * power(t, 1.0 - SHEAR_EXPONENT)
    damp = 1.0 / (1.0 + relax)
    scale = n * inverse * lax.rsqrt(t) * relax * damp
    beta = scale * ((1.0 - CONDUCTIVE_SHARE) / 5.0) * inverse * inverse / n
    cubic = beta * inverse
    qu = q[0] * u[0] + q[1] * u[1] + q[2] * u[2]
    offset = beta * (uu * inverse - 5.0)
    twice = 2.0 * cubic
    zz = q[2] * u[2]
    polynomial = [
        scale - qu * offset,
        offset * q[0] + twice * qu * u[0],
        offset * q[1] + twice * qu * u[1],
        offset * q[2] + twice * qu * u[2],
        -cubic * (qu + 2.0 * zz),
        -twice * (q[0] * u[0] - zz),
        -twice * (q[0] * u[1] + q[1] * u[0]),
        -twice * (q[0] * u[2] + q[2] * u[0]),
        -twice * (q[1] * u[1] - zz),
        -twice * (q[1] * u[2] + q[2] * u[1]),
        cubic * q[0],
        cubic * q[1],
        cubic * q[2],
    ]
    zero = jnp.zeros_like(n)
    rate = (0.5 * LOG2E) * inverse
    exponent = [-rate * uu, 2.0 * rate * u[0], 2.0 * rate * u[1], 2.0 * rate * u[2], -rate]
    rows = polynomial + [damp, zero, zero] + exponent + [zero, zero, zero]
    for row, field in enumerate(rows):
        coef_ref[pl.ds(row, blocks, stride=COEF), :] = field


def fluid_call(moments, last):
    blocks = moments.shape[0] // SENT
    shapes = [pltpu.VMEM((blocks * COEF, LANES), jnp.float32)]
    if last:
        shapes.append(pltpu.VMEM((blocks * 8, LANES), jnp.float32))
    return pl.pallas_call(
        fluid_kernel,
        out_shape=shapes,
        in_specs=[WHOLE],
        out_specs=[WHOLE] * len(shapes),
        compiler_params=params(8),
        name="fluid",
    )(near(moments))


def relaxed(g_refs, here, coef_ref, exponent_ref, polynomial_ref, tile):
    per_tile = TILE // LANES
    parts = [
        coef_ref[pl.ds((tile * per_tile + part) * COEF, COEF), :]
        for part in range(per_tile)
    ]
    coefficients = jnp.concatenate(parts, axis=1)
    cubic = expand_polynomial(coefficients[:BASIS])
    spread = expand_exponent(coefficients[BASIS:])
    rows = g_refs[0].shape[0]

    def values_of(some):
        polynomial = dot(polynomial_ref[some, :], cubic)
        exponent = dot(exponent_ref[some, :], spread)
        refs = g_refs[some.start // rows : (some.start + some.size) // rows]
        g = jnp.concatenate([ref[:, here] for ref in refs], axis=0)
        return g * coefficients[DAMP : DAMP + 1] + jnp.exp2(exponent) * polynomial

    return values_of


def update_kernel(*refs):
    g_refs = refs[:PARTS]
    coef_ref, exponent_ref, polynomial_ref, table_ref, f_ref, moments_ref = refs[PARTS:]
    cells = f_ref.shape[1]

    def front(tile):
        here = pl.ds(tile * TILE, TILE)
        values_of = relaxed(g_refs, here, coef_ref, exponent_ref, polynomial_ref, tile)
        return store_tile(f_ref, here, f_ref.shape[0], values_of)

    def back(tile, split):
        store_moments(moments_ref, table_ref[...], split, tile, cells // LANES)

    in_turn(front, back, cells // TILE)


def update_call(g, coefficients, tables, table):
    rows, cells = g[0].shape
    return pl.pallas_call(
        update_kernel,
        out_shape=(
            pltpu.VMEM((rows * PARTS, cells), jnp.float32),
            pltpu.VMEM((SENT * cells // LANES, LANES), jnp.float32),
        ),
        in_specs=[WHOLE] * (PARTS + 4),
        out_specs=(WHOLE, WHOLE),
        compiler_params=params(8),
        name="update",
    )(*map(near, g), near(coefficients), *map(near, tables), near(table))


def finish_kernel(*refs):
    g_refs = refs[:PARTS]
    coef_ref, macro_ref, exponent_ref, polynomial_ref, f_hbm, fields_hbm = refs[PARTS : PARTS + 6]
    held, fields, sems = refs[PARTS + 6 :]
    cells = held.shape[1]
    width = cells // DEPARTURES
    for block in range(cells // LANES):
        fields[:, block * LANES : (block + 1) * LANES] = macro_ref[block * 8 : (block + 1) * 8, :]
    copies = [pltpu.make_async_copy(fields, fields_hbm, sems.at[DEPARTURES])]
    copies[0].start()
    for chunk in range(DEPARTURES):
        for local in range(width // TILE):
            tile = chunk * (width // TILE) + local
            here = pl.ds(tile * TILE, TILE)
            values_of = relaxed(g_refs, here, coef_ref, exponent_ref, polynomial_ref, tile)
            for first in range(0, held.shape[0], ROWS):
                held[pl.ds(first, ROWS), here] = values_of(pl.ds(first, ROWS))
        there = pl.ds(chunk * width, width)
        copy = pltpu.make_async_copy(held.at[:, there], f_hbm.at[:, there], sems.at[chunk])
        copy.start()
        copies.append(copy)
    for copy in copies:
        copy.wait()


def finish_call(g, coefficients, macro, tables):
    rows, cells = g[0].shape
    return pl.pallas_call(
        finish_kernel,
        out_shape=(
            jax.ShapeDtypeStruct((rows * PARTS, cells), jnp.float32),
            jax.ShapeDtypeStruct((8, cells), jnp.float32),
        ),
        in_specs=[WHOLE] * (PARTS + 4),
        out_specs=(OUTSIDE, OUTSIDE),
        scratch_shapes=[
            pltpu.VMEM((rows * PARTS, cells), jnp.float32),
            pltpu.VMEM((8, cells), jnp.float32),
            pltpu.SemaphoreType.DMA((DEPARTURES + 1,)),
        ],
        compiler_params=params(16),
        name="finish",
    )(*map(near, g), near(coefficients), near(macro), *map(near, tables))


def add_kernel(left_ref, right_ref, out_ref):
    out_ref[...] = left_ref[...] + right_ref[...]


def add_call(left, right):
    return pl.pallas_call(
        add_kernel,
        out_shape=pltpu.VMEM(left.shape, left.dtype),
        in_specs=[WHOLE, WHOLE],
        out_specs=WHOLE,
        compiler_params=params(1),
        name="add",
    )(near(left), near(right))


def plan(count):
    strides = [1 << bit for bit in range(count.bit_length() - 1)]
    return strides[:2], strides[2:]


def swap(values, count, stride):
    return lax.ppermute(values, "vel", [(device, device ^ stride) for device in range(count)])


def staged_sum(values, count, sides, f, tasks):
    splits, sums = plan(count)
    results, waiting, portions = [], list(tasks), list(BESIDE)

    def exchange(chunks, stride):
        got = [swap(chunk, count, stride) for chunk in chunks]
        portion = portions.pop(0) if portions else 0
        if portion:
            _, held = lax.optimization_barrier((chunks[-1], f))
            made = [task(held) for task in waiting[:portion]]
            del waiting[:portion]
            got[0], made = lax.optimization_barrier((got[0], made))
            results.extend(made)
        return got

    def split(chunks, stride, lower_side):
        kept, sent = [], []
        for chunk in chunks:
            half = chunk.shape[0] // 2
            first, second = chunk[:half], chunk[half:]
            kept.append(jnp.where(lower_side, first, second))
            sent.append(jnp.where(lower_side, second, first))
        sent = lax.optimization_barrier(sent)
        got = exchange(sent, stride)
        if len(chunks) == 1:
            return [kept[0] + got[0]]
        return [add_call(own, other) for own, other in zip(kept, got)]

    def join(chunks, stride, lower_side):
        out = []
        for own, got in zip(chunks, exchange(chunks, stride)):
            lower = jnp.where(lower_side, own, got)
            upper = jnp.where(lower_side, got, own)
            out.append((lower, upper))
        return out

    (block,) = split([values], splits[0], sides[0])
    half = block.shape[0] // 2
    chunks = [block[:half], block[half:]]
    for stride, lower_side in zip(splits[1:], sides[1:]):
        chunks = split(chunks, stride, lower_side)
    for stride in sums:
        chunks = [add_call(own, got) for own, got in zip(chunks, exchange(chunks, stride))]
    for stride, lower_side in reversed(list(zip(splits[1:], sides[1:]))):
        chunks = [jnp.concatenate(both, axis=0) for both in join(chunks, stride, lower_side)]
    lowers, uppers = zip(*join(chunks, splits[0], sides[0]))
    results.extend(task(f) for task in waiting)
    return jnp.concatenate(lowers + uppers, axis=0), results


def on_device(velocities, density, flow, thermal, deviation):
    count = lax.axis_size("vel")
    place = lax.axis_index("vel")
    sides = [place & stride == 0 for stride in plan(count)[0]]
    velocities, sides = lax.optimization_barrier((velocities, sides))
    f, moments, *tables, table, stream = start_call(
        velocities, density, flow, thermal, deviation, velocities.shape[1] * count
    )
    for iteration in range(ITERS):
        tasks = [
            functools.partial(lambda held, part: transport_call(stream, held, part), part=part)
            for part in range(PARTS)
        ]
        summed, g = staged_sum(moments, count, sides, f, tasks)
        last = iteration == ITERS - 1
        coefficients, *macro = fluid_call(summed, last)
        if not last:
            f, moments = update_call(g, coefficients, tables, table)
    return finish_call(g, coefficients, macro[0], tables)


def solution(mesh):
    return jax.shard_map(
        on_device,
        mesh=mesh,
        in_specs=(P(None, "vel"), P("grp"), P(None, "grp"), P("grp"), P("vel", "grp")),
        out_specs=(P("vel", "grp"), P(None, "grp")),
        check_vma=False,
    )
```

```python
import functools

import jax
import jax.numpy as jnp
from jax import lax
from jax.experimental import pallas as pl
from jax.experimental.pallas import tpu as pltpu
from jax.sharding import PartitionSpec as P

ITERS = 2

ADIABATIC_INDEX = 5.0 / 3.0
CONDUCTIVE_SHARE = 2.0 / 3.0
SHEAR_EXPONENT = 0.81
SHEAR_REFERENCE = 0.05
KINETIC_STEP = 0.05
COURANT = 0.4
SPREAD_SCALE = 1.5

LOG2E = 1.4426950408889634
LANES = 128
TILE = 256
BASIS = 16
SENT = 13
COEF = 24
DAMP = 13
ROWS = 64
CHUNKS = 8
DEPARTURES = 16
PARTS = 8
BESIDE = (1, 2, 1, 1, 2, 1)
BESIDE_ROUNDS = (1, 2, 2, 2, 1)
MIB = 1024 * 1024

WHOLE = pl.BlockSpec(memory_space=pltpu.VMEM)
OUTSIDE = pl.BlockSpec(memory_space=pltpu.HBM)


def params(mebibytes):
    return pltpu.CompilerParams(vmem_limit_bytes=mebibytes * MIB)


def near(values):
    return pltpu.with_memory_space_constraint(values, pltpu.VMEM)


def far(values):
    return pltpu.with_memory_space_constraint(values, pltpu.HBM)


def dot(left, right):
    return jnp.dot(left, right, preferred_element_type=jnp.float32)


def rounded(values):
    return values.astype(jnp.bfloat16).astype(jnp.float32)


def phi_rows(velocities):
    vx, vy, vz = velocities[0:1], velocities[1:2], velocities[2:3]
    sq = vx * vx + vy * vy + vz * vz
    zero = jnp.zeros_like(vx)
    rows = [
        jnp.ones_like(vx), vx, vy, vz, sq, vx * vx, vx * vy, vx * vz, vy * vy, vy * vz,
        vx * sq, vy * sq, vz * sq, zero, zero, zero,
    ]
    return jnp.concatenate(rows, axis=0), sq


def parts_of(values):
    high = rounded(values)
    middle = rounded(values - high)
    return high, middle, values - high - middle


def polynomial_table_of(velocities):
    high, middle, _ = parts_of(phi_rows(velocities)[0])
    wide = jnp.zeros((128 - 3 * BASIS, velocities.shape[1]), jnp.float32)
    rows = jnp.concatenate([high, high, middle, wide], axis=0)
    return rows.T[:, : 3 * BASIS].astype(jnp.bfloat16)


def make_tables(velocities, total_count):
    phi, sq = phi_rows(velocities)
    high, middle, low = parts_of(phi)
    three = [high[:8], high[:8], high[:8], middle[:8], middle[:8], low[:8]]
    wide = jnp.zeros((128 - 6 * 8, phi.shape[1]), jnp.float32)
    exponent = jnp.concatenate(three + [wide], axis=0).T[:, : 6 * 8].astype(jnp.bfloat16)
    weighted = phi * (SPREAD_SCALE**3 * jnp.exp(sq / (2.0 * SPREAD_SCALE**2)) / total_count)
    top = rounded(weighted)
    rest = weighted - top
    moments = jnp.concatenate(
        [
            jnp.concatenate([top, top], axis=1),
            jnp.concatenate([rest, jnp.zeros_like(rest)], axis=1),
        ],
        axis=0,
    ).astype(jnp.bfloat16)
    return exponent, moments


def expand_exponent(rows):
    high, middle, low = parts_of(rows)
    return jnp.concatenate([high, middle, low, high, middle, high], axis=0).astype(jnp.bfloat16)


def expand_polynomial(rows):
    high = rows.astype(jnp.bfloat16)
    middle = (rows - high.astype(jnp.float32)).astype(jnp.bfloat16)
    return jnp.concatenate([high, middle, high], axis=0)


def store_moments(moments_ref, table, split, tile, blocks):
    both = dot(table, split)
    sums = both[:BASIS] + both[BASIS:]
    per_tile = TILE // LANES
    for part in range(per_tile):
        block = tile * per_tile + part
        moments_ref[pl.ds(block, SENT, stride=blocks), :] = sums[
            :SENT, part * LANES : (part + 1) * LANES
        ]


def store_tile(f_ref, here, rows, values_of):
    high, low = [], []
    for first in range(0, rows, ROWS):
        some = pl.ds(first, ROWS)
        values = values_of(some)
        f_ref[some, here] = values
        high.append(values.astype(jnp.bfloat16))
        low.append((values - high[-1].astype(jnp.float32)).astype(jnp.bfloat16))
    return jnp.concatenate(high + low, axis=0)


def in_turn(front, back, tiles):
    made = front(0)
    for tile in range(1, tiles):
        upcoming = front(tile)
        back(tile - 1, made)
        made = upcoming
    back(tiles - 1, made)


def start_kernel(
    total_count,
    vel_hbm, density_hbm, flow_hbm, thermal_hbm, deviation_hbm,
    f_ref, moments_ref, exponent_ref, polynomial_ref, table_ref, stream_ref,
    vel_ref, density_ref, flow_ref, thermal_ref, deviation_ref, small_sems, sems,
):
    cells = f_ref.shape[1]
    width = cells // CHUNKS
    small = [
        pltpu.make_async_copy(source, target, small_sems.at[number])
        for number, (source, target) in enumerate(
            [
                (vel_hbm, vel_ref),
                (density_hbm, density_ref),
                (flow_hbm, flow_ref),
                (thermal_hbm, thermal_ref),
            ]
        )
    ]
    for copy in small:
        copy.start()
    copies = [
        pltpu.make_async_copy(
            deviation_hbm.at[:, pl.ds(chunk * width, width)],
            deviation_ref.at[:, pl.ds(chunk * width, width)],
            sems.at[chunk],
        )
        for chunk in range(CHUNKS)
    ]
    for copy in copies:
        copy.start()
    small[0].wait()
    exponent_table, table = make_tables(vel_ref[...], total_count)
    exponent_ref[...] = exponent_table
    table_ref[...] = table
    for copy in small[1:]:
        copy.wait()
    def front(tile):
        here = pl.ds(tile * TILE, TILE)
        density, flow, thermal = density_ref[:, here], flow_ref[:, here], thermal_ref[:, here]
        rate = (0.5 * LOG2E) / thermal
        speed_sq = flow[0:1] * flow[0:1] + flow[1:2] * flow[1:2] + flow[2:3] * flow[2:3]
        rows = [-rate * speed_sq, 2.0 * rate * flow, -rate, jnp.zeros((3, TILE), jnp.float32)]
        spread = expand_exponent(jnp.concatenate(rows, axis=0))
        scale = density / (thermal * jnp.sqrt(thermal))

        def values_of(some):
            exponent = dot(exponent_ref[some, :], spread)
            return jnp.exp2(exponent) * (scale * (1.0 + deviation_ref[some, here]))

        return store_tile(f_ref, here, f_ref.shape[0], values_of)

    def back(tile, split):
        store_moments(moments_ref, table, split, tile, cells // LANES)
        if tile == 1:
            polynomial_ref[...] = polynomial_table_of(vel_ref[...])
            stream_ref[...] = jnp.broadcast_to(vel_ref[0:1, :], (LANES, vel_ref.shape[1])).T

    def front_when_here(tile):
        if tile * TILE % width == 0:
            copies[tile * TILE // width].wait()
        return front(tile)

    in_turn(front_when_here, back, cells // TILE)


def start_call(velocities, density, flow, thermal, deviation, total_count):
    local, cells = deviation.shape
    return pl.pallas_call(
        functools.partial(start_kernel, total_count),
        out_shape=(
            pltpu.VMEM((local, cells), jnp.float32),
            pltpu.VMEM((SENT * cells // LANES, LANES), jnp.float32),
            pltpu.VMEM((local, 6 * 8), jnp.bfloat16),
            pltpu.VMEM((local, 3 * BASIS), jnp.bfloat16),
            pltpu.VMEM((2 * BASIS, 2 * local), jnp.bfloat16),
            pltpu.VMEM((local, LANES), jnp.float32),
        ),
        in_specs=[OUTSIDE] * 5,
        out_specs=(WHOLE,) * 6,
        scratch_shapes=[
            pltpu.VMEM((3, local), jnp.float32),
            pltpu.VMEM((1, cells), jnp.float32),
            pltpu.VMEM((3, cells), jnp.float32),
            pltpu.VMEM((1, cells), jnp.float32),
            pltpu.VMEM((local, cells), jnp.float32),
            pltpu.SemaphoreType.DMA((4,)),
            pltpu.SemaphoreType.DMA((CHUNKS,)),
        ],
        compiler_params=params(16),
        name="start",
    )(
        far(velocities),
        far(density.reshape(1, cells)),
        far(flow),
        far(thermal.reshape(1, cells)),
        far(deviation),
    )


def transport_kernel(first_row, stream_ref, f_ref, g_ref):
    rows, cells = g_ref.shape
    blocks = cells // LANES
    lane = lax.broadcasted_iota(jnp.int32, (8, LANES), 1)
    at_first, at_last = lane == 0, lane == LANES - 1
    lag = 4

    def row_step(row_tile, carry):
        source = pl.ds(pl.multiple_of(first_row + row_tile * 8, 8), 8)
        target = pl.ds(pl.multiple_of(row_tile * 8, 8), 8)
        stream = stream_ref[source, :]
        upward = stream > 0
        rate = KINETIC_STEP * jnp.abs(stream)
        half = jnp.where(upward, 0.5, -0.5)
        x, up, rise, down, face, face_up, face_down = {}, {}, {}, {}, {}, {}, {}

        def load(b):
            at = (b % blocks) * LANES
            x[b] = f_ref[source, at : at + LANES]
            up[b] = pltpu.roll(x[b], 1, 1)

        def slope_in(b):
            rise[b] = x[b] - jnp.where(at_first, up[b - 1], up[b])
            down[b] = pltpu.roll(rise[b], LANES - 1, 1)

        def reconstruct(b):
            ahead = jnp.where(at_last, down[b + 1], down[b])
            slope = jnp.maximum(jnp.minimum(rise[b], ahead), 0.0) + jnp.minimum(
                jnp.maximum(rise[b], ahead), 0.0
            )
            face[b] = x[b] + half * slope
            face_up[b] = pltpu.roll(face[b], 1, 1)
            face_down[b] = pltpu.roll(face[b], LANES - 1, 1)

        def store(b):
            other = jnp.where(
                upward,
                jnp.where(at_first, face_up[b - 1], face_up[b]),
                jnp.where(at_last, face_down[b + 1], face_down[b]),
            )
            g_ref[target, b * LANES : (b + 1) * LANES] = x[b] - rate * (face[b] - other)

        for k in range(-2, blocks + 3 * lag + 4):
            for act, behind, low, high in (
                (load, 0, -2, blocks + 1),
                (slope_in, lag, -1, blocks + 1),
                (reconstruct, 2 * lag + 1, -1, blocks),
                (store, 3 * lag + 2, 0, blocks - 1),
            ):
                if low <= k - behind <= high:
                    act(k - behind)
        return carry

    lax.fori_loop(0, rows // 8, row_step, 0)


def transport_call(stream, f, part):
    local, cells = f.shape
    rows = local // PARTS
    return pl.pallas_call(
        functools.partial(transport_kernel, part * rows),
        out_shape=pltpu.VMEM((rows, cells), jnp.float32),
        in_specs=[WHOLE, WHOLE],
        out_specs=WHOLE,
        compiler_params=params(4),
        name="transport",
    )(near(stream), near(f))


def fluid_kernel(moments_ref, coef_ref, macro_ref=None):
    blocks = moments_ref.shape[0] // SENT
    m = [moments_ref[row * blocks : (row + 1) * blocks, :] for row in range(13)]
    lane = lax.broadcasted_iota(jnp.int32, (blocks, LANES), 1)

    def following(x):
        turned = pltpu.roll(x, LANES - 1, 1)
        return jnp.where(lane == LANES - 1, pltpu.roll(turned, blocks - 1, 0), turned)

    def preceding(x):
        turned = pltpu.roll(x, 1, 1)
        return jnp.where(lane == 0, pltpu.roll(turned, 1, 0), turned)

    def power(x, exponent):
        return jnp.exp2(exponent * jnp.log2(x))

    def primitives(w):
        inverse = 1.0 / w[0]
        u = [w[1] * inverse, w[2] * inverse, w[3] * inverse]
        uu = u[0] * u[0] + u[1] * u[1] + u[2] * u[2]
        t = (2.0 * w[4] * inverse - uu) * (1.0 / 3.0)
        return u, uu, t

    n = m[0]
    w = [n, m[1], m[2], m[3], 0.5 * m[4]]
    u, uu, t = primitives(w)
    p = n * t
    second = [[m[5], m[6], m[7]], [m[6], m[8], m[9]], [m[7], m[9], m[4] - m[5] - m[8]]]
    stress = [m[5] - m[1] * u[0] - p, m[6] - m[1] * u[1], m[7] - m[1] * u[2]]
    q = []
    for i in range(3):
        along = second[i][0] * u[0] + second[i][1] * u[1] + second[i][2] * u[2]
        q.append(0.5 * (m[10 + i] - u[i] * m[4] - 2.0 * along + 2.0 * n * u[i] * uu))

    shear = SHEAR_REFERENCE * power(t, SHEAR_EXPONENT)
    high_order = [
        stress[i] + ((4.0 / 3.0 if i == 0 else 1.0) * 0.5) * shear * (following(u[i]) - preceding(u[i]))
        for i in range(3)
    ]
    high_order.append(q[0] + (3.75 * 0.5) * shear * (following(t) - preceding(t)))
    half_order = [0.5 * h for h in high_order]
    face_order = [h + following(h) for h in half_order]

    def sweep(w, u, t, shear):
        rates = jnp.abs(u[0]) + jnp.sqrt(ADIABATIC_INDEX * t)
        signal = jnp.max(jnp.max(rates, axis=0, keepdims=True), axis=1, keepdims=True)
        step = COURANT / signal
        p = w[0] * t
        euler = [w[1], w[1] * u[0] + p, w[1] * u[1], w[1] * u[2], (w[4] + p) * u[0]]
        next_u = [following(x) for x in u]
        half_shear = 0.5 * shear
        face_shear = half_shear + following(half_shear)
        sxx = face_order[0] - (4.0 / 3.0) * face_shear * (next_u[0] - u[0])
        sxy = face_order[1] - face_shear * (next_u[1] - u[1])
        sxz = face_order[2] - face_shear * (next_u[2] - u[2])
        heat = face_order[3] - 3.75 * face_shear * (following(t) - t)
        work = 0.5 * (
            sxx * (u[0] + next_u[0]) + sxy * (u[1] + next_u[1]) + sxz * (u[2] + next_u[2])
        )
        viscous = [None, sxx, sxy, sxz, work + heat]
        out = []
        for i in range(5):
            spread = signal * w[i]
            total = 0.5 * ((euler[i] + spread) + following(euler[i] - spread))
            if viscous[i] is not None:
                total = total + viscous[i]
            out.append(w[i] - step * (total - preceding(total)))
        return out

    w = sweep(w, u, t, shear)
    u, uu, t = primitives(w)
    w = sweep(w, u, t, SHEAR_REFERENCE * power(t, SHEAR_EXPONENT))
    u, uu, t = primitives(w)
    n = w[0]

    if macro_ref is not None:
        for row, field in enumerate([n, u[0], u[1], u[2], t, q[0], q[1], q[2]]):
            macro_ref[pl.ds(row, blocks, stride=8), :] = field

    inverse = 1.0 / t
    relax = n * power(t, 1.0 - SHEAR_EXPONENT)
    damp = 1.0 / (1.0 + relax)
    scale = n * inverse * lax.rsqrt(t) * relax * damp
    beta = scale * ((1.0 - CONDUCTIVE_SHARE) / 5.0) * inverse * inverse / n
    cubic = beta * inverse
    qu = q[0] * u[0] + q[1] * u[1] + q[2] * u[2]
    offset = beta * (uu * inverse - 5.0)
    twice = 2.0 * cubic
    zz = q[2] * u[2]
    polynomial = [
        scale - qu * offset,
        offset * q[0] + twice * qu * u[0],
        offset * q[1] + twice * qu * u[1],
        offset * q[2] + twice * qu * u[2],
        -cubic * (qu + 2.0 * zz),
        -twice * (q[0] * u[0] - zz),
        -twice * (q[0] * u[1] + q[1] * u[0]),
        -twice * (q[0] * u[2] + q[2] * u[0]),
        -twice * (q[1] * u[1] - zz),
        -twice * (q[1] * u[2] + q[2] * u[1]),
        cubic * q[0],
        cubic * q[1],
        cubic * q[2],
    ]
    zero = jnp.zeros_like(n)
    rate = (0.5 * LOG2E) * inverse
    exponent = [-rate * uu, 2.0 * rate * u[0], 2.0 * rate * u[1], 2.0 * rate * u[2], -rate]
    rows = polynomial + [damp, zero, zero] + exponent + [zero, zero, zero]
    for row, field in enumerate(rows):
        coef_ref[pl.ds(row, blocks, stride=COEF), :] = field


def fluid_call(moments, last):
    blocks = moments.shape[0] // SENT
    shapes = [pltpu.VMEM((blocks * COEF, LANES), jnp.float32)]
    if last:
        shapes.append(pltpu.VMEM((blocks * 8, LANES), jnp.float32))
    return pl.pallas_call(
        fluid_kernel,
        out_shape=shapes,
        in_specs=[WHOLE],
        out_specs=[WHOLE] * len(shapes),
        compiler_params=params(8),
        name="fluid",
    )(near(moments))


def relaxed(g_refs, here, coef_ref, exponent_ref, polynomial_ref, tile):
    per_tile = TILE // LANES
    parts = [
        coef_ref[pl.ds((tile * per_tile + part) * COEF, COEF), :]
        for part in range(per_tile)
    ]
    coefficients = jnp.concatenate(parts, axis=1)
    cubic = expand_polynomial(coefficients[:BASIS])
    spread = expand_exponent(coefficients[BASIS:])
    rows = g_refs[0].shape[0]

    def values_of(some):
        polynomial = dot(polynomial_ref[some, :], cubic)
        exponent = dot(exponent_ref[some, :], spread)
        refs = g_refs[some.start // rows : (some.start + some.size) // rows]
        g = jnp.concatenate([ref[:, here] for ref in refs], axis=0)
        return g * coefficients[DAMP : DAMP + 1] + jnp.exp2(exponent) * polynomial

    return values_of


def update_kernel(*refs):
    g_refs = refs[:PARTS]
    coef_ref, exponent_ref, polynomial_ref, table_ref, f_ref, moments_ref = refs[PARTS:]
    cells = f_ref.shape[1]

    def front(tile):
        here = pl.ds(tile * TILE, TILE)
        values_of = relaxed(g_refs, here, coef_ref, exponent_ref, polynomial_ref, tile)
        return store_tile(f_ref, here, f_ref.shape[0], values_of)

    def back(tile, split):
        store_moments(moments_ref, table_ref[...], split, tile, cells // LANES)

    in_turn(front, back, cells // TILE)


def update_call(g, coefficients, tables, table):
    rows, cells = g[0].shape
    return pl.pallas_call(
        update_kernel,
        out_shape=(
            pltpu.VMEM((rows * PARTS, cells), jnp.float32),
            pltpu.VMEM((SENT * cells // LANES, LANES), jnp.float32),
        ),
        in_specs=[WHOLE] * (PARTS + 4),
        out_specs=(WHOLE, WHOLE),
        compiler_params=params(8),
        name="update",
    )(*map(near, g), near(coefficients), *map(near, tables), near(table))


def finish_kernel(*refs):
    g_refs = refs[:PARTS]
    coef_ref, macro_ref, exponent_ref, polynomial_ref, f_hbm, fields_hbm = refs[PARTS : PARTS + 6]
    held, fields, sems = refs[PARTS + 6 :]
    cells = held.shape[1]
    width = cells // DEPARTURES
    for block in range(cells // LANES):
        fields[:, block * LANES : (block + 1) * LANES] = macro_ref[block * 8 : (block + 1) * 8, :]
    copies = [pltpu.make_async_copy(fields, fields_hbm, sems.at[DEPARTURES])]
    copies[0].start()
    for chunk in range(DEPARTURES):
        for local in range(width // TILE):
            tile = chunk * (width // TILE) + local
            here = pl.ds(tile * TILE, TILE)
            values_of = relaxed(g_refs, here, coef_ref, exponent_ref, polynomial_ref, tile)
            for first in range(0, held.shape[0], ROWS):
                held[pl.ds(first, ROWS), here] = values_of(pl.ds(first, ROWS))
        there = pl.ds(chunk * width, width)
        copy = pltpu.make_async_copy(held.at[:, there], f_hbm.at[:, there], sems.at[chunk])
        copy.start()
        copies.append(copy)
    for copy in copies:
        copy.wait()


def finish_call(g, coefficients, macro, tables):
    rows, cells = g[0].shape
    return pl.pallas_call(
        finish_kernel,
        out_shape=(
            jax.ShapeDtypeStruct((rows * PARTS, cells), jnp.float32),
            jax.ShapeDtypeStruct((8, cells), jnp.float32),
        ),
        in_specs=[WHOLE] * (PARTS + 4),
        out_specs=(OUTSIDE, OUTSIDE),
        scratch_shapes=[
            pltpu.VMEM((rows * PARTS, cells), jnp.float32),
            pltpu.VMEM((8, cells), jnp.float32),
            pltpu.SemaphoreType.DMA((DEPARTURES + 1,)),
        ],
        compiler_params=params(16),
        name="finish",
    )(*map(near, g), near(coefficients), near(macro), *map(near, tables))


def add_kernel(left_ref, right_ref, out_ref):
    out_ref[...] = left_ref[...] + right_ref[...]


def add_call(left, right):
    return pl.pallas_call(
        add_kernel,
        out_shape=pltpu.VMEM(left.shape, left.dtype),
        in_specs=[WHOLE, WHOLE],
        out_specs=WHOLE,
        compiler_params=params(1),
        name="add",
    )(near(left), near(right))


def plan(count):
    strides = [1 << bit for bit in range(count.bit_length() - 1)]
    return strides[:2], strides[2:]


def swap(values, count, stride):
    return lax.ppermute(values, "vel", [(device, device ^ stride) for device in range(count)])


def staged_sum(values, count, sides, f, tasks):
    splits, sums = plan(count)
    results, waiting, portions = [], list(tasks), list(BESIDE)

    def exchange(chunks, stride):
        got = [swap(chunk, count, stride) for chunk in chunks]
        portion = portions.pop(0) if portions else 0
        if portion:
            _, held = lax.optimization_barrier((chunks[-1], f))
            made = [task(held) for task in waiting[:portion]]
            del waiting[:portion]
            got[0], made = lax.optimization_barrier((got[0], made))
            results.extend(made)
        return got

    def split(chunks, stride, lower_side):
        kept, sent = [], []
        for chunk in chunks:
            half = chunk.shape[0] // 2
            first, second = chunk[:half], chunk[half:]
            kept.append(jnp.where(lower_side, first, second))
            sent.append(jnp.where(lower_side, second, first))
        sent = lax.optimization_barrier(sent)
        got = exchange(sent, stride)
        if len(chunks) == 1:
            return [kept[0] + got[0]]
        return [add_call(own, other) for own, other in zip(kept, got)]

    def join(chunks, stride, lower_side):
        out = []
        for own, got in zip(chunks, exchange(chunks, stride)):
            lower = jnp.where(lower_side, own, got)
            upper = jnp.where(lower_side, got, own)
            out.append((lower, upper))
        return out

    (block,) = split([values], splits[0], sides[0])
    half = block.shape[0] // 2
    chunks = [block[:half], block[half:]]
    for stride, lower_side in zip(splits[1:], sides[1:]):
        chunks = split(chunks, stride, lower_side)
    for stride in sums:
        chunks = [add_call(own, got) for own, got in zip(chunks, exchange(chunks, stride))]
    for stride, lower_side in reversed(list(zip(splits[1:], sides[1:]))):
        chunks = [jnp.concatenate(both, axis=0) for both in join(chunks, stride, lower_side)]
    lowers, uppers = zip(*join(chunks, splits[0], sides[0]))
    results.extend(task(f) for task in waiting)
    return jnp.concatenate(lowers + uppers, axis=0), results


def rounds_sum(values, count, even, f, tasks):
    strides = [1 << bit for bit in range(1, count.bit_length() - 1)]
    orders = (strides, strides[1:] + strides[:1])
    results, waiting, portions = [], list(tasks), list(BESIDE_ROUNDS)

    def exchange(chunks, chosen):
        got = [swap(chunk, count, stride) for chunk, stride in zip(chunks, chosen)]
        portion = portions.pop(0) if portions else 0
        if portion:
            _, held = lax.optimization_barrier((chunks[-1], f))
            made = [task(held) for task in waiting[:portion]]
            del waiting[:portion]
            got[0], made = lax.optimization_barrier((got[0], made))
            results.extend(made)
        return got

    half = values.shape[0] // 2
    first, second = values[:half], values[half:]
    kept, sent = jnp.where(even, first, second), jnp.where(even, second, first)
    (got,) = exchange([sent], [1])
    block = kept + got
    chunks = lax.optimization_barrier([block[: half // 2], block[half // 2 :]])
    for chosen in zip(*orders):
        chunks = [add_call(own, got) for own, got in zip(chunks, exchange(chunks, chosen))]
    got = exchange(chunks, [1, 1])
    results.extend(task(f) for task in waiting)
    lower = [jnp.where(even, own, other) for own, other in zip(chunks, got)]
    upper = [jnp.where(even, other, own) for own, other in zip(chunks, got)]
    return jnp.concatenate(lower + upper, axis=0), results


def on_device(velocities, density, flow, thermal, deviation):
    count = lax.axis_size("vel")
    place = lax.axis_index("vel")
    sides = [place & stride == 0 for stride in plan(count)[0]]
    velocities, sides = lax.optimization_barrier((velocities, sides))
    f, moments, *tables, table, stream = start_call(
        velocities, density, flow, thermal, deviation, velocities.shape[1] * count
    )
    for iteration in range(ITERS):
        tasks = [
            functools.partial(lambda held, part: transport_call(stream, held, part), part=part)
            for part in range(PARTS)
        ]
        if iteration == 0:
            summed, g = rounds_sum(moments, count, sides[0], f, tasks)
        else:
            summed, g = staged_sum(moments, count, sides, f, tasks)
        last = iteration == ITERS - 1
        coefficients, *macro = fluid_call(summed, last)
        if not last:
            f, moments = update_call(g, coefficients, tables, table)
    return finish_call(g, coefficients, macro[0], tables)


def solution(mesh):
    return jax.shard_map(
        on_device,
        mesh=mesh,
        in_specs=(P(None, "vel"), P("grp"), P(None, "grp"), P("grp"), P("vel", "grp")),
        out_specs=(P("vel", "grp"), P(None, "grp")),
        check_vma=False,
    )
```

```python
import functools

import jax
import jax.numpy as jnp
from jax import lax
from jax.experimental import pallas as pl
from jax.experimental.pallas import tpu as pltpu
from jax.sharding import PartitionSpec as P

ITERS = 2

ADIABATIC_INDEX = 5.0 / 3.0
CONDUCTIVE_SHARE = 2.0 / 3.0
SHEAR_EXPONENT = 0.81
SHEAR_REFERENCE = 0.05
KINETIC_STEP = 0.05
COURANT = 0.4
SPREAD_SCALE = 1.5

LOG2E = 1.4426950408889634
LANES = 128
TILE = 512
BASIS = 16
SENT = 13
COEF = 24
DAMP = 13
ROWS = 32
CHUNKS = 8
DEPARTURES = 16
PARTS = 8
BESIDE = (1, 2, 1, 1, 2, 1)
MIB = 1024 * 1024

WHOLE = pl.BlockSpec(memory_space=pltpu.VMEM)
OUTSIDE = pl.BlockSpec(memory_space=pltpu.HBM)


def params(mebibytes):
    return pltpu.CompilerParams(vmem_limit_bytes=mebibytes * MIB)


def near(values):
    return pltpu.with_memory_space_constraint(values, pltpu.VMEM)


def far(values):
    return pltpu.with_memory_space_constraint(values, pltpu.HBM)


def dot(left, right):
    return jnp.dot(left, right, preferred_element_type=jnp.float32)


def rounded(values):
    return values.astype(jnp.bfloat16).astype(jnp.float32)


def phi_rows(velocities):
    vx, vy, vz = velocities[0:1], velocities[1:2], velocities[2:3]
    sq = vx * vx + vy * vy + vz * vz
    zero = jnp.zeros_like(vx)
    rows = [
        jnp.ones_like(vx), vx, vy, vz, sq, vx * vx, vx * vy, vx * vz, vy * vy, vy * vz,
        vx * sq, vy * sq, vz * sq, zero, zero, zero,
    ]
    return jnp.concatenate(rows, axis=0), sq


def parts_of(values):
    high = rounded(values)
    middle = rounded(values - high)
    return high, middle, values - high - middle


def make_tables(velocities, total_count):
    phi, sq = phi_rows(velocities)
    high, middle, low = parts_of(phi)
    three = [high[:8], high[:8], high[:8], middle[:8], middle[:8], low[:8]]
    wide = jnp.zeros((128 - 6 * 8, phi.shape[1]), jnp.float32)
    exponent = jnp.concatenate(three + [wide], axis=0).T[:, : 6 * 8].astype(jnp.bfloat16)
    two = [high, high, middle]
    polynomial = jnp.concatenate(two + [wide], axis=0).T[:, : 3 * BASIS].astype(jnp.bfloat16)
    weighted = phi * (SPREAD_SCALE**3 * jnp.exp(sq / (2.0 * SPREAD_SCALE**2)) / total_count)
    top = rounded(weighted)
    rest = weighted - top
    moments = jnp.concatenate(
        [
            jnp.concatenate([top, top], axis=1),
            jnp.concatenate([rest, jnp.zeros_like(rest)], axis=1),
        ],
        axis=0,
    ).astype(jnp.bfloat16)
    return exponent, polynomial, moments


def expand_exponent(rows):
    high, middle, low = parts_of(rows)
    return jnp.concatenate([high, middle, low, high, middle, high], axis=0).astype(jnp.bfloat16)


def expand_polynomial(rows):
    high = rows.astype(jnp.bfloat16)
    middle = (rows - high.astype(jnp.float32)).astype(jnp.bfloat16)
    return jnp.concatenate([high, middle, high], axis=0)


def store_moments(moments_ref, table, split, tile, blocks):
    both = dot(table, split)
    sums = both[:BASIS] + both[BASIS:]
    per_tile = TILE // LANES
    for part in range(per_tile):
        block = tile * per_tile + part
        moments_ref[pl.ds(block, SENT, stride=blocks), :] = sums[
            :SENT, part * LANES : (part + 1) * LANES
        ]


def store_tile(f_ref, here, rows, values_of):
    high, low = [], []
    for first in range(0, rows, ROWS):
        some = pl.ds(first, ROWS)
        values = values_of(some)
        f_ref[some, here] = values
        high.append(values.astype(jnp.bfloat16))
        low.append((values - high[-1].astype(jnp.float32)).astype(jnp.bfloat16))
    return jnp.concatenate(high + low, axis=0)


def in_turn(front, back, tiles):
    made = front(0)
    for tile in range(1, tiles):
        upcoming = front(tile)
        back(tile - 1, made)
        made = upcoming
    back(tiles - 1, made)


def start_kernel(
    total_count,
    vel_hbm, density_hbm, flow_hbm, thermal_hbm, deviation_hbm,
    f_ref, moments_ref, exponent_ref, polynomial_ref, table_ref, stream_ref,
    vel_ref, density_ref, flow_ref, thermal_ref, deviation_ref, small_sems, sems,
):
    cells = f_ref.shape[1]
    width = cells // CHUNKS
    small = [
        pltpu.make_async_copy(source, target, small_sems.at[number])
        for number, (source, target) in enumerate(
            [
                (vel_hbm, vel_ref),
                (density_hbm, density_ref),
                (flow_hbm, flow_ref),
                (thermal_hbm, thermal_ref),
            ]
        )
    ]
    for copy in small:
        copy.start()
    copies = [
        pltpu.make_async_copy(
            deviation_hbm.at[:, pl.ds(chunk * width, width)],
            deviation_ref.at[:, pl.ds(chunk * width, width)],
            sems.at[chunk],
        )
        for chunk in range(CHUNKS)
    ]
    for copy in copies:
        copy.start()
    small[0].wait()
    exponent_table, polynomial_table, table = make_tables(vel_ref[...], total_count)
    exponent_ref[...] = exponent_table
    polynomial_ref[...] = polynomial_table
    table_ref[...] = table
    stream_ref[...] = jnp.broadcast_to(vel_ref[0:1, :], (LANES, vel_ref.shape[1])).T
    for copy in small[1:]:
        copy.wait()
    def front(tile):
        here = pl.ds(tile * TILE, TILE)
        density, flow, thermal = density_ref[:, here], flow_ref[:, here], thermal_ref[:, here]
        rate = (0.5 * LOG2E) / thermal
        speed_sq = flow[0:1] * flow[0:1] + flow[1:2] * flow[1:2] + flow[2:3] * flow[2:3]
        rows = [-rate * speed_sq, 2.0 * rate * flow, -rate, jnp.zeros((3, TILE), jnp.float32)]
        spread = expand_exponent(jnp.concatenate(rows, axis=0))
        scale = density / (thermal * jnp.sqrt(thermal))

        def values_of(some):
            exponent = dot(exponent_ref[some, :], spread)
            return jnp.exp2(exponent) * (scale * (1.0 + deviation_ref[some, here]))

        return store_tile(f_ref, here, f_ref.shape[0], values_of)

    def back(tile, split):
        store_moments(moments_ref, table, split, tile, cells // LANES)

    def front_when_here(tile):
        if tile * TILE % width == 0:
            copies[tile * TILE // width].wait()
        return front(tile)

    in_turn(front_when_here, back, cells // TILE)


def start_call(velocities, density, flow, thermal, deviation, total_count):
    local, cells = deviation.shape
    return pl.pallas_call(
        functools.partial(start_kernel, total_count),
        out_shape=(
            pltpu.VMEM((local, cells), jnp.float32),
            pltpu.VMEM((SENT * cells // LANES, LANES), jnp.float32),
            pltpu.VMEM((local, 6 * 8), jnp.bfloat16),
            pltpu.VMEM((local, 3 * BASIS), jnp.bfloat16),
            pltpu.VMEM((2 * BASIS, 2 * local), jnp.bfloat16),
            pltpu.VMEM((local, LANES), jnp.float32),
        ),
        in_specs=[OUTSIDE] * 5,
        out_specs=(WHOLE,) * 6,
        scratch_shapes=[
            pltpu.VMEM((3, local), jnp.float32),
            pltpu.VMEM((1, cells), jnp.float32),
            pltpu.VMEM((3, cells), jnp.float32),
            pltpu.VMEM((1, cells), jnp.float32),
            pltpu.VMEM((local, cells), jnp.float32),
            pltpu.SemaphoreType.DMA((4,)),
            pltpu.SemaphoreType.DMA((CHUNKS,)),
        ],
        compiler_params=params(16),
        name="start",
    )(
        far(velocities),
        far(density.reshape(1, cells)),
        far(flow),
        far(thermal.reshape(1, cells)),
        far(deviation),
    )


def transport_kernel(first_row, stream_ref, f_ref, g_ref):
    rows, cells = g_ref.shape
    blocks = cells // LANES
    lane = lax.broadcasted_iota(jnp.int32, (8, LANES), 1)
    at_first, at_last = lane == 0, lane == LANES - 1
    lag = 4

    def row_step(row_tile, carry):
        source = pl.ds(pl.multiple_of(first_row + row_tile * 8, 8), 8)
        target = pl.ds(pl.multiple_of(row_tile * 8, 8), 8)
        stream = stream_ref[source, :]
        upward = stream > 0
        rate = KINETIC_STEP * jnp.abs(stream)
        half = jnp.where(upward, 0.5, -0.5)
        x, up, rise, down, face, face_up, face_down = {}, {}, {}, {}, {}, {}, {}

        def load(b):
            at = (b % blocks) * LANES
            x[b] = f_ref[source, at : at + LANES]
            up[b] = pltpu.roll(x[b], 1, 1)

        def slope_in(b):
            rise[b] = x[b] - jnp.where(at_first, up[b - 1], up[b])
            down[b] = pltpu.roll(rise[b], LANES - 1, 1)

        def reconstruct(b):
            ahead = jnp.where(at_last, down[b + 1], down[b])
            slope = jnp.maximum(jnp.minimum(rise[b], ahead), 0.0) + jnp.minimum(
                jnp.maximum(rise[b], ahead), 0.0
            )
            face[b] = x[b] + half * slope
            face_up[b] = pltpu.roll(face[b], 1, 1)
            face_down[b] = pltpu.roll(face[b], LANES - 1, 1)

        def store(b):
            other = jnp.where(
                upward,
                jnp.where(at_first, face_up[b - 1], face_up[b]),
                jnp.where(at_last, face_down[b + 1], face_down[b]),
            )
            g_ref[target, b * LANES : (b + 1) * LANES] = x[b] - rate * (face[b] - other)

        for k in range(-2, blocks + 3 * lag + 4):
            for act, behind, low, high in (
                (load, 0, -2, blocks + 1),
                (slope_in, lag, -1, blocks + 1),
                (reconstruct, 2 * lag + 1, -1, blocks),
                (store, 3 * lag + 2, 0, blocks - 1),
            ):
                if low <= k - behind <= high:
                    act(k - behind)
        return carry

    lax.fori_loop(0, rows // 8, row_step, 0)


def transport_call(stream, f, part):
    local, cells = f.shape
    rows = local // PARTS
    return pl.pallas_call(
        functools.partial(transport_kernel, part * rows),
        out_shape=pltpu.VMEM((rows, cells), jnp.float32),
        in_specs=[WHOLE, WHOLE],
        out_specs=WHOLE,
        compiler_params=params(4),
        name="transport",
    )(near(stream), near(f))


def fluid_kernel(moments_ref, coef_ref, macro_ref=None):
    blocks = moments_ref.shape[0] // SENT
    m = [moments_ref[row * blocks : (row + 1) * blocks, :] for row in range(13)]
    lane = lax.broadcasted_iota(jnp.int32, (blocks, LANES), 1)

    def following(x):
        turned = pltpu.roll(x, LANES - 1, 1)
        return jnp.where(lane == LANES - 1, pltpu.roll(turned, blocks - 1, 0), turned)

    def preceding(x):
        turned = pltpu.roll(x, 1, 1)
        return jnp.where(lane == 0, pltpu.roll(turned, 1, 0), turned)

    def power(x, exponent):
        return jnp.exp2(exponent * jnp.log2(x))

    def primitives(w):
        inverse = 1.0 / w[0]
        u = [w[1] * inverse, w[2] * inverse, w[3] * inverse]
        uu = u[0] * u[0] + u[1] * u[1] + u[2] * u[2]
        t = (2.0 * w[4] * inverse - uu) * (1.0 / 3.0)
        return u, uu, t

    n = m[0]
    w = [n, m[1], m[2], m[3], 0.5 * m[4]]
    u, uu, t = primitives(w)
    p = n * t
    second = [[m[5], m[6], m[7]], [m[6], m[8], m[9]], [m[7], m[9], m[4] - m[5] - m[8]]]
    stress = [m[5] - m[1] * u[0] - p, m[6] - m[1] * u[1], m[7] - m[1] * u[2]]
    q = []
    for i in range(3):
        along = second[i][0] * u[0] + second[i][1] * u[1] + second[i][2] * u[2]
        q.append(0.5 * (m[10 + i] - u[i] * m[4] - 2.0 * along + 2.0 * n * u[i] * uu))

    shear = SHEAR_REFERENCE * power(t, SHEAR_EXPONENT)
    high_order = [
        stress[i] + ((4.0 / 3.0 if i == 0 else 1.0) * 0.5) * shear * (following(u[i]) - preceding(u[i]))
        for i in range(3)
    ]
    high_order.append(q[0] + (3.75 * 0.5) * shear * (following(t) - preceding(t)))
    half_order = [0.5 * h for h in high_order]
    face_order = [h + following(h) for h in half_order]

    def sweep(w, u, t, shear):
        rates = jnp.abs(u[0]) + jnp.sqrt(ADIABATIC_INDEX * t)
        signal = jnp.max(jnp.max(rates, axis=0, keepdims=True), axis=1, keepdims=True)
        step = COURANT / signal
        p = w[0] * t
        euler = [w[1], w[1] * u[0] + p, w[1] * u[1], w[1] * u[2], (w[4] + p) * u[0]]
        next_u = [following(x) for x in u]
        half_shear = 0.5 * shear
        face_shear = half_shear + following(half_shear)
        sxx = face_order[0] - (4.0 / 3.0) * face_shear * (next_u[0] - u[0])
        sxy = face_order[1] - face_shear * (next_u[1] - u[1])
        sxz = face_order[2] - face_shear * (next_u[2] - u[2])
        heat = face_order[3] - 3.75 * face_shear * (following(t) - t)
        work = 0.5 * (
            sxx * (u[0] + next_u[0]) + sxy * (u[1] + next_u[1]) + sxz * (u[2] + next_u[2])
        )
        viscous = [None, sxx, sxy, sxz, work + heat]
        out = []
        for i in range(5):
            spread = signal * w[i]
            total = 0.5 * ((euler[i] + spread) + following(euler[i] - spread))
            if viscous[i] is not None:
                total = total + viscous[i]
            out.append(w[i] - step * (total - preceding(total)))
        return out

    w = sweep(w, u, t, shear)
    u, uu, t = primitives(w)
    w = sweep(w, u, t, SHEAR_REFERENCE * power(t, SHEAR_EXPONENT))
    u, uu, t = primitives(w)
    n = w[0]

    if macro_ref is not None:
        for row, field in enumerate([n, u[0], u[1], u[2], t, q[0], q[1], q[2]]):
            macro_ref[pl.ds(row, blocks, stride=8), :] = field

    inverse = 1.0 / t
    relax = n * power(t, 1.0 - SHEAR_EXPONENT)
    damp = 1.0 / (1.0 + relax)
    scale = n * inverse * lax.rsqrt(t) * relax * damp
    beta = scale * ((1.0 - CONDUCTIVE_SHARE) / 5.0) * inverse * inverse / n
    cubic = beta * inverse
    qu = q[0] * u[0] + q[1] * u[1] + q[2] * u[2]
    offset = beta * (uu * inverse - 5.0)
    twice = 2.0 * cubic
    zz = q[2] * u[2]
    polynomial = [
        scale - qu * offset,
        offset * q[0] + twice * qu * u[0],
        offset * q[1] + twice * qu * u[1],
        offset * q[2] + twice * qu * u[2],
        -cubic * (qu + 2.0 * zz),
        -twice * (q[0] * u[0] - zz),
        -twice * (q[0] * u[1] + q[1] * u[0]),
        -twice * (q[0] * u[2] + q[2] * u[0]),
        -twice * (q[1] * u[1] - zz),
        -twice * (q[1] * u[2] + q[2] * u[1]),
        cubic * q[0],
        cubic * q[1],
        cubic * q[2],
    ]
    zero = jnp.zeros_like(n)
    rate = (0.5 * LOG2E) * inverse
    exponent = [-rate * uu, 2.0 * rate * u[0], 2.0 * rate * u[1], 2.0 * rate * u[2], -rate]
    rows = polynomial + [damp, zero, zero] + exponent + [zero, zero, zero]
    for row, field in enumerate(rows):
        coef_ref[pl.ds(row, blocks, stride=COEF), :] = field


def fluid_call(moments, last):
    blocks = moments.shape[0] // SENT
    shapes = [pltpu.VMEM((blocks * COEF, LANES), jnp.float32)]
    if last:
        shapes.append(pltpu.VMEM((blocks * 8, LANES), jnp.float32))
    return pl.pallas_call(
        fluid_kernel,
        out_shape=shapes,
        in_specs=[WHOLE],
        out_specs=[WHOLE] * len(shapes),
        compiler_params=params(8),
        name="fluid",
    )(near(moments))


def relaxed(g_refs, here, coef_ref, exponent_ref, polynomial_ref, tile):
    per_tile = TILE // LANES
    parts = [
        coef_ref[pl.ds((tile * per_tile + part) * COEF, COEF), :]
        for part in range(per_tile)
    ]
    coefficients = jnp.concatenate(parts, axis=1)
    cubic = expand_polynomial(coefficients[:BASIS])
    spread = expand_exponent(coefficients[BASIS:])
    rows = g_refs[0].shape[0]

    def values_of(some):
        polynomial = dot(polynomial_ref[some, :], cubic)
        exponent = dot(exponent_ref[some, :], spread)
        refs = g_refs[some.start // rows : (some.start + some.size) // rows]
        g = jnp.concatenate([ref[:, here] for ref in refs], axis=0)
        return g * coefficients[DAMP : DAMP + 1] + jnp.exp2(exponent) * polynomial

    return values_of


def update_kernel(*refs):
    g_refs = refs[:PARTS]
    coef_ref, exponent_ref, polynomial_ref, table_ref, f_ref, moments_ref = refs[PARTS:]
    cells = f_ref.shape[1]

    def front(tile):
        here = pl.ds(tile * TILE, TILE)
        values_of = relaxed(g_refs, here, coef_ref, exponent_ref, polynomial_ref, tile)
        return store_tile(f_ref, here, f_ref.shape[0], values_of)

    def back(tile, split):
        store_moments(moments_ref, table_ref[...], split, tile, cells // LANES)

    in_turn(front, back, cells // TILE)


def update_call(g, coefficients, tables, table):
    rows, cells = g[0].shape
    return pl.pallas_call(
        update_kernel,
        out_shape=(
            pltpu.VMEM((rows * PARTS, cells), jnp.float32),
            pltpu.VMEM((SENT * cells // LANES, LANES), jnp.float32),
        ),
        in_specs=[WHOLE] * (PARTS + 4),
        out_specs=(WHOLE, WHOLE),
        compiler_params=params(8),
        name="update",
    )(*map(near, g), near(coefficients), *map(near, tables), near(table))


def finish_kernel(*refs):
    g_refs = refs[:PARTS]
    coef_ref, macro_ref, exponent_ref, polynomial_ref, f_hbm, fields_hbm = refs[PARTS : PARTS + 6]
    held, fields, sems = refs[PARTS + 6 :]
    cells = held.shape[1]
    width = cells // DEPARTURES
    for block in range(cells // LANES):
        fields[:, block * LANES : (block + 1) * LANES] = macro_ref[block * 8 : (block + 1) * 8, :]
    copies = [pltpu.make_async_copy(fields, fields_hbm, sems.at[DEPARTURES])]
    copies[0].start()
    for chunk in range(DEPARTURES):
        for local in range(width // TILE):
            tile = chunk * (width // TILE) + local
            here = pl.ds(tile * TILE, TILE)
            values_of = relaxed(g_refs, here, coef_ref, exponent_ref, polynomial_ref, tile)
            for first in range(0, held.shape[0], ROWS):
                held[pl.ds(first, ROWS), here] = values_of(pl.ds(first, ROWS))
        there = pl.ds(chunk * width, width)
        copy = pltpu.make_async_copy(held.at[:, there], f_hbm.at[:, there], sems.at[chunk])
        copy.start()
        copies.append(copy)
    for copy in copies:
        copy.wait()


def finish_call(g, coefficients, macro, tables):
    rows, cells = g[0].shape
    return pl.pallas_call(
        finish_kernel,
        out_shape=(
            jax.ShapeDtypeStruct((rows * PARTS, cells), jnp.float32),
            jax.ShapeDtypeStruct((8, cells), jnp.float32),
        ),
        in_specs=[WHOLE] * (PARTS + 4),
        out_specs=(OUTSIDE, OUTSIDE),
        scratch_shapes=[
            pltpu.VMEM((rows * PARTS, cells), jnp.float32),
            pltpu.VMEM((8, cells), jnp.float32),
            pltpu.SemaphoreType.DMA((DEPARTURES + 1,)),
        ],
        compiler_params=params(16),
        name="finish",
    )(*map(near, g), near(coefficients), near(macro), *map(near, tables))


def add_kernel(left_ref, right_ref, out_ref):
    out_ref[...] = left_ref[...] + right_ref[...]


def add_call(left, right):
    return pl.pallas_call(
        add_kernel,
        out_shape=pltpu.VMEM(left.shape, left.dtype),
        in_specs=[WHOLE, WHOLE],
        out_specs=WHOLE,
        compiler_params=params(1),
        name="add",
    )(near(left), near(right))


def plan(count):
    strides = [1 << bit for bit in range(count.bit_length() - 1)]
    return strides[:2], strides[2:]


def swap(values, count, stride):
    return lax.ppermute(values, "vel", [(device, device ^ stride) for device in range(count)])


def staged_sum(values, count, sides, f, tasks):
    splits, sums = plan(count)
    results, waiting, portions = [], list(tasks), list(BESIDE)

    def exchange(chunks, stride):
        got = [swap(chunk, count, stride) for chunk in chunks]
        portion = portions.pop(0) if portions else 0
        if portion:
            _, held = lax.optimization_barrier((chunks[-1], f))
            made = [task(held) for task in waiting[:portion]]
            del waiting[:portion]
            got[0], made = lax.optimization_barrier((got[0], made))
            results.extend(made)
        return got

    def split(chunks, stride, lower_side):
        kept, sent = [], []
        for chunk in chunks:
            half = chunk.shape[0] // 2
            first, second = chunk[:half], chunk[half:]
            kept.append(jnp.where(lower_side, first, second))
            sent.append(jnp.where(lower_side, second, first))
        sent = lax.optimization_barrier(sent)
        got = exchange(sent, stride)
        if len(chunks) == 1:
            return [kept[0] + got[0]]
        return [add_call(own, other) for own, other in zip(kept, got)]

    def join(chunks, stride, lower_side):
        out = []
        for own, got in zip(chunks, exchange(chunks, stride)):
            lower = jnp.where(lower_side, own, got)
            upper = jnp.where(lower_side, got, own)
            out.append((lower, upper))
        return out

    (block,) = split([values], splits[0], sides[0])
    half = block.shape[0] // 2
    chunks = [block[:half], block[half:]]
    for stride, lower_side in zip(splits[1:], sides[1:]):
        chunks = split(chunks, stride, lower_side)
    for stride in sums:
        chunks = [add_call(own, got) for own, got in zip(chunks, exchange(chunks, stride))]
    for stride, lower_side in reversed(list(zip(splits[1:], sides[1:]))):
        chunks = [jnp.concatenate(both, axis=0) for both in join(chunks, stride, lower_side)]
    lowers, uppers = zip(*join(chunks, splits[0], sides[0]))
    results.extend(task(f) for task in waiting)
    return jnp.concatenate(lowers + uppers, axis=0), results


def on_device(velocities, density, flow, thermal, deviation):
    count = lax.axis_size("vel")
    place = lax.axis_index("vel")
    sides = [place & stride == 0 for stride in plan(count)[0]]
    velocities, sides = lax.optimization_barrier((velocities, sides))
    f, moments, *tables, table, stream = start_call(
        velocities, density, flow, thermal, deviation, velocities.shape[1] * count
    )
    for iteration in range(ITERS):
        tasks = [
            functools.partial(lambda held, part: transport_call(stream, held, part), part=part)
            for part in range(PARTS)
        ]
        summed, g = staged_sum(moments, count, sides, f, tasks)
        last = iteration == ITERS - 1
        coefficients, *macro = fluid_call(summed, last)
        if not last:
            f, moments = update_call(g, coefficients, tables, table)
    return finish_call(g, coefficients, macro[0], tables)


def solution(mesh):
    return jax.shard_map(
        on_device,
        mesh=mesh,
        in_specs=(P(None, "vel"), P("grp"), P(None, "grp"), P("grp"), P("vel", "grp")),
        out_specs=(P("vel", "grp"), P(None, "grp")),
        check_vma=False,
    )
```

```python
import functools

import jax
import jax.numpy as jnp
from jax import lax
from jax.experimental import pallas as pl
from jax.experimental.pallas import tpu as pltpu
from jax.sharding import PartitionSpec as P

ITERS = 2

ADIABATIC_INDEX = 5.0 / 3.0
CONDUCTIVE_SHARE = 2.0 / 3.0
SHEAR_EXPONENT = 0.81
SHEAR_REFERENCE = 0.05
KINETIC_STEP = 0.05
COURANT = 0.4
SPREAD_SCALE = 1.5

LOG2E = 1.4426950408889634
LANES = 128
TILE = 1024
BASIS = 16
SENT = 13
COEF = 24
DAMP = 13
ROWS = 32
CHUNKS = 8
DEPARTURES = 8
PARTS = 8
BESIDE = (1, 2, 1, 1, 2, 1)
MIB = 1024 * 1024

WHOLE = pl.BlockSpec(memory_space=pltpu.VMEM)
OUTSIDE = pl.BlockSpec(memory_space=pltpu.HBM)


def params(mebibytes):
    return pltpu.CompilerParams(vmem_limit_bytes=mebibytes * MIB)


def near(values):
    return pltpu.with_memory_space_constraint(values, pltpu.VMEM)


def far(values):
    return pltpu.with_memory_space_constraint(values, pltpu.HBM)


def dot(left, right):
    return jnp.dot(left, right, preferred_element_type=jnp.float32)


def rounded(values):
    return values.astype(jnp.bfloat16).astype(jnp.float32)


def phi_rows(velocities):
    vx, vy, vz = velocities[0:1], velocities[1:2], velocities[2:3]
    sq = vx * vx + vy * vy + vz * vz
    zero = jnp.zeros_like(vx)
    rows = [
        jnp.ones_like(vx), vx, vy, vz, sq, vx * vx, vx * vy, vx * vz, vy * vy, vy * vz,
        vx * sq, vy * sq, vz * sq, zero, zero, zero,
    ]
    return jnp.concatenate(rows, axis=0), sq


def parts_of(values):
    high = rounded(values)
    middle = rounded(values - high)
    return high, middle, values - high - middle


def make_tables(velocities, total_count):
    phi, sq = phi_rows(velocities)
    high, middle, low = parts_of(phi)
    three = [high[:8], high[:8], high[:8], middle[:8], middle[:8], low[:8]]
    wide = jnp.zeros((128 - 6 * 8, phi.shape[1]), jnp.float32)
    exponent = jnp.concatenate(three + [wide], axis=0).T[:, : 6 * 8].astype(jnp.bfloat16)
    two = [high, high, middle]
    polynomial = jnp.concatenate(two + [wide], axis=0).T[:, : 3 * BASIS].astype(jnp.bfloat16)
    weighted = phi * (SPREAD_SCALE**3 * jnp.exp(sq / (2.0 * SPREAD_SCALE**2)) / total_count)
    top = rounded(weighted)
    rest = weighted - top
    moments = jnp.concatenate(
        [
            jnp.concatenate([top, top], axis=1),
            jnp.concatenate([rest, jnp.zeros_like(rest)], axis=1),
        ],
        axis=0,
    ).astype(jnp.bfloat16)
    return exponent, polynomial, moments


def expand_exponent(rows):
    high, middle, low = parts_of(rows)
    return jnp.concatenate([high, middle, low, high, middle, high], axis=0).astype(jnp.bfloat16)


def expand_polynomial(rows):
    high = rows.astype(jnp.bfloat16)
    middle = (rows - high.astype(jnp.float32)).astype(jnp.bfloat16)
    return jnp.concatenate([high, middle, high], axis=0)


def store_moments(moments_ref, table, split, tile, blocks):
    both = dot(table, split)
    sums = both[:BASIS] + both[BASIS:]
    per_tile = TILE // LANES
    for part in range(per_tile):
        block = tile * per_tile + part
        moments_ref[pl.ds(block, SENT, stride=blocks), :] = sums[
            :SENT, part * LANES : (part + 1) * LANES
        ]


def store_tile(f_ref, here, rows, values_of):
    high, low = [], []
    for first in range(0, rows, ROWS):
        some = pl.ds(first, ROWS)
        values = values_of(some)
        f_ref[some, here] = values
        high.append(values.astype(jnp.bfloat16))
        low.append((values - high[-1].astype(jnp.float32)).astype(jnp.bfloat16))
    return jnp.concatenate(high + low, axis=0)


def in_turn(front, back, tiles):
    made = front(0)
    for tile in range(1, tiles):
        upcoming = front(tile)
        back(tile - 1, made)
        made = upcoming
    back(tiles - 1, made)


def start_kernel(
    total_count,
    vel_hbm, density_hbm, flow_hbm, thermal_hbm, deviation_hbm,
    f_ref, moments_ref, exponent_ref, polynomial_ref, table_ref, stream_ref,
    vel_ref, density_ref, flow_ref, thermal_ref, deviation_ref, small_sems, sems,
):
    cells = f_ref.shape[1]
    width = cells // CHUNKS
    small = [
        pltpu.make_async_copy(source, target, small_sems.at[number])
        for number, (source, target) in enumerate(
            [
                (vel_hbm, vel_ref),
                (density_hbm, density_ref),
                (flow_hbm, flow_ref),
                (thermal_hbm, thermal_ref),
            ]
        )
    ]
    for copy in small:
        copy.start()
    copies = [
        pltpu.make_async_copy(
            deviation_hbm.at[:, pl.ds(chunk * width, width)],
            deviation_ref.at[:, pl.ds(chunk * width, width)],
            sems.at[chunk],
        )
        for chunk in range(CHUNKS)
    ]
    for copy in copies:
        copy.start()
    small[0].wait()
    exponent_table, polynomial_table, table = make_tables(vel_ref[...], total_count)
    exponent_ref[...] = exponent_table
    polynomial_ref[...] = polynomial_table
    table_ref[...] = table
    stream_ref[...] = jnp.broadcast_to(vel_ref[0:1, :], (LANES, vel_ref.shape[1])).T
    for copy in small[1:]:
        copy.wait()
    def front(tile):
        here = pl.ds(tile * TILE, TILE)
        density, flow, thermal = density_ref[:, here], flow_ref[:, here], thermal_ref[:, here]
        rate = (0.5 * LOG2E) / thermal
        speed_sq = flow[0:1] * flow[0:1] + flow[1:2] * flow[1:2] + flow[2:3] * flow[2:3]
        rows = [-rate * speed_sq, 2.0 * rate * flow, -rate, jnp.zeros((3, TILE), jnp.float32)]
        spread = expand_exponent(jnp.concatenate(rows, axis=0))
        scale = density / (thermal * jnp.sqrt(thermal))

        def values_of(some):
            exponent = dot(exponent_ref[some, :], spread)
            return jnp.exp2(exponent) * (scale * (1.0 + deviation_ref[some, here]))

        return store_tile(f_ref, here, f_ref.shape[0], values_of)

    def back(tile, split):
        store_moments(moments_ref, table, split, tile, cells // LANES)

    def front_when_here(tile):
        if tile * TILE % width == 0:
            copies[tile * TILE // width].wait()
        return front(tile)

    in_turn(front_when_here, back, cells // TILE)


def start_call(velocities, density, flow, thermal, deviation, total_count):
    local, cells = deviation.shape
    return pl.pallas_call(
        functools.partial(start_kernel, total_count),
        out_shape=(
            pltpu.VMEM((local, cells), jnp.float32),
            pltpu.VMEM((SENT * cells // LANES, LANES), jnp.float32),
            pltpu.VMEM((local, 6 * 8), jnp.bfloat16),
            pltpu.VMEM((local, 3 * BASIS), jnp.bfloat16),
            pltpu.VMEM((2 * BASIS, 2 * local), jnp.bfloat16),
            pltpu.VMEM((local, LANES), jnp.float32),
        ),
        in_specs=[OUTSIDE] * 5,
        out_specs=(WHOLE,) * 6,
        scratch_shapes=[
            pltpu.VMEM((3, local), jnp.float32),
            pltpu.VMEM((1, cells), jnp.float32),
            pltpu.VMEM((3, cells), jnp.float32),
            pltpu.VMEM((1, cells), jnp.float32),
            pltpu.VMEM((local, cells), jnp.float32),
            pltpu.SemaphoreType.DMA((4,)),
            pltpu.SemaphoreType.DMA((CHUNKS,)),
        ],
        compiler_params=params(16),
        name="start",
    )(
        far(velocities),
        far(density.reshape(1, cells)),
        far(flow),
        far(thermal.reshape(1, cells)),
        far(deviation),
    )


def transport_kernel(first_row, stream_ref, f_ref, g_ref):
    rows, cells = g_ref.shape
    blocks = cells // LANES
    lane = lax.broadcasted_iota(jnp.int32, (8, LANES), 1)
    at_first, at_last = lane == 0, lane == LANES - 1
    lag = 4

    def row_step(row_tile, carry):
        source = pl.ds(pl.multiple_of(first_row + row_tile * 8, 8), 8)
        target = pl.ds(pl.multiple_of(row_tile * 8, 8), 8)
        stream = stream_ref[source, :]
        upward = stream > 0
        rate = KINETIC_STEP * jnp.abs(stream)
        half = jnp.where(upward, 0.5, -0.5)
        x, up, rise, down, face, face_up, face_down = {}, {}, {}, {}, {}, {}, {}

        def load(b):
            at = (b % blocks) * LANES
            x[b] = f_ref[source, at : at + LANES]
            up[b] = pltpu.roll(x[b], 1, 1)

        def slope_in(b):
            rise[b] = x[b] - jnp.where(at_first, up[b - 1], up[b])
            down[b] = pltpu.roll(rise[b], LANES - 1, 1)

        def reconstruct(b):
            ahead = jnp.where(at_last, down[b + 1], down[b])
            slope = jnp.maximum(jnp.minimum(rise[b], ahead), 0.0) + jnp.minimum(
                jnp.maximum(rise[b], ahead), 0.0
            )
            face[b] = x[b] + half * slope
            face_up[b] = pltpu.roll(face[b], 1, 1)
            face_down[b] = pltpu.roll(face[b], LANES - 1, 1)

        def store(b):
            other = jnp.where(
                upward,
                jnp.where(at_first, face_up[b - 1], face_up[b]),
                jnp.where(at_last, face_down[b + 1], face_down[b]),
            )
            g_ref[target, b * LANES : (b + 1) * LANES] = x[b] - rate * (face[b] - other)

        for k in range(-2, blocks + 3 * lag + 4):
            for act, behind, low, high in (
                (load, 0, -2, blocks + 1),
                (slope_in, lag, -1, blocks + 1),
                (reconstruct, 2 * lag + 1, -1, blocks),
                (store, 3 * lag + 2, 0, blocks - 1),
            ):
                if low <= k - behind <= high:
                    act(k - behind)
        return carry

    lax.fori_loop(0, rows // 8, row_step, 0)


def transport_call(stream, f, part):
    local, cells = f.shape
    rows = local // PARTS
    return pl.pallas_call(
        functools.partial(transport_kernel, part * rows),
        out_shape=pltpu.VMEM((rows, cells), jnp.float32),
        in_specs=[WHOLE, WHOLE],
        out_specs=WHOLE,
        compiler_params=params(4),
        name="transport",
    )(near(stream), near(f))


def fluid_kernel(moments_ref, coef_ref, macro_ref=None):
    blocks = moments_ref.shape[0] // SENT
    m = [moments_ref[row * blocks : (row + 1) * blocks, :] for row in range(13)]
    lane = lax.broadcasted_iota(jnp.int32, (blocks, LANES), 1)

    def following(x):
        turned = pltpu.roll(x, LANES - 1, 1)
        return jnp.where(lane == LANES - 1, pltpu.roll(turned, blocks - 1, 0), turned)

    def preceding(x):
        turned = pltpu.roll(x, 1, 1)
        return jnp.where(lane == 0, pltpu.roll(turned, 1, 0), turned)

    def power(x, exponent):
        return jnp.exp2(exponent * jnp.log2(x))

    def primitives(w):
        inverse = 1.0 / w[0]
        u = [w[1] * inverse, w[2] * inverse, w[3] * inverse]
        uu = u[0] * u[0] + u[1] * u[1] + u[2] * u[2]
        t = (2.0 * w[4] * inverse - uu) * (1.0 / 3.0)
        return u, uu, t

    n = m[0]
    w = [n, m[1], m[2], m[3], 0.5 * m[4]]
    u, uu, t = primitives(w)
    p = n * t
    second = [[m[5], m[6], m[7]], [m[6], m[8], m[9]], [m[7], m[9], m[4] - m[5] - m[8]]]
    stress = [m[5] - m[1] * u[0] - p, m[6] - m[1] * u[1], m[7] - m[1] * u[2]]
    q = []
    for i in range(3):
        along = second[i][0] * u[0] + second[i][1] * u[1] + second[i][2] * u[2]
        q.append(0.5 * (m[10 + i] - u[i] * m[4] - 2.0 * along + 2.0 * n * u[i] * uu))

    shear = SHEAR_REFERENCE * power(t, SHEAR_EXPONENT)
    high_order = [
        stress[i] + ((4.0 / 3.0 if i == 0 else 1.0) * 0.5) * shear * (following(u[i]) - preceding(u[i]))
        for i in range(3)
    ]
    high_order.append(q[0] + (3.75 * 0.5) * shear * (following(t) - preceding(t)))
    half_order = [0.5 * h for h in high_order]
    face_order = [h + following(h) for h in half_order]

    def sweep(w, u, t, shear):
        rates = jnp.abs(u[0]) + jnp.sqrt(ADIABATIC_INDEX * t)
        signal = jnp.max(jnp.max(rates, axis=0, keepdims=True), axis=1, keepdims=True)
        step = COURANT / signal
        p = w[0] * t
        euler = [w[1], w[1] * u[0] + p, w[1] * u[1], w[1] * u[2], (w[4] + p) * u[0]]
        next_u = [following(x) for x in u]
        half_shear = 0.5 * shear
        face_shear = half_shear + following(half_shear)
        sxx = face_order[0] - (4.0 / 3.0) * face_shear * (next_u[0] - u[0])
        sxy = face_order[1] - face_shear * (next_u[1] - u[1])
        sxz = face_order[2] - face_shear * (next_u[2] - u[2])
        heat = face_order[3] - 3.75 * face_shear * (following(t) - t)
        work = 0.5 * (
            sxx * (u[0] + next_u[0]) + sxy * (u[1] + next_u[1]) + sxz * (u[2] + next_u[2])
        )
        viscous = [None, sxx, sxy, sxz, work + heat]
        out = []
        for i in range(5):
            spread = signal * w[i]
            total = 0.5 * ((euler[i] + spread) + following(euler[i] - spread))
            if viscous[i] is not None:
                total = total + viscous[i]
            out.append(w[i] - step * (total - preceding(total)))
        return out

    w = sweep(w, u, t, shear)
    u, uu, t = primitives(w)
    w = sweep(w, u, t, SHEAR_REFERENCE * power(t, SHEAR_EXPONENT))
    u, uu, t = primitives(w)
    n = w[0]

    if macro_ref is not None:
        for row, field in enumerate([n, u[0], u[1], u[2], t, q[0], q[1], q[2]]):
            macro_ref[pl.ds(row, blocks, stride=8), :] = field

    inverse = 1.0 / t
    relax = n * power(t, 1.0 - SHEAR_EXPONENT)
    damp = 1.0 / (1.0 + relax)
    scale = n * inverse * lax.rsqrt(t) * relax * damp
    beta = scale * ((1.0 - CONDUCTIVE_SHARE) / 5.0) * inverse * inverse / n
    cubic = beta * inverse
    qu = q[0] * u[0] + q[1] * u[1] + q[2] * u[2]
    offset = beta * (uu * inverse - 5.0)
    twice = 2.0 * cubic
    zz = q[2] * u[2]
    polynomial = [
        scale - qu * offset,
        offset * q[0] + twice * qu * u[0],
        offset * q[1] + twice * qu * u[1],
        offset * q[2] + twice * qu * u[2],
        -cubic * (qu + 2.0 * zz),
        -twice * (q[0] * u[0] - zz),
        -twice * (q[0] * u[1] + q[1] * u[0]),
        -twice * (q[0] * u[2] + q[2] * u[0]),
        -twice * (q[1] * u[1] - zz),
        -twice * (q[1] * u[2] + q[2] * u[1]),
        cubic * q[0],
        cubic * q[1],
        cubic * q[2],
    ]
    zero = jnp.zeros_like(n)
    rate = (0.5 * LOG2E) * inverse
    exponent = [-rate * uu, 2.0 * rate * u[0], 2.0 * rate * u[1], 2.0 * rate * u[2], -rate]
    rows = polynomial + [damp, zero, zero] + exponent + [zero, zero, zero]
    for row, field in enumerate(rows):
        coef_ref[pl.ds(row, blocks, stride=COEF), :] = field


def fluid_call(moments, last):
    blocks = moments.shape[0] // SENT
    shapes = [pltpu.VMEM((blocks * COEF, LANES), jnp.float32)]
    if last:
        shapes.append(pltpu.VMEM((blocks * 8, LANES), jnp.float32))
    return pl.pallas_call(
        fluid_kernel,
        out_shape=shapes,
        in_specs=[WHOLE],
        out_specs=[WHOLE] * len(shapes),
        compiler_params=params(8),
        name="fluid",
    )(near(moments))


def relaxed(g_refs, here, coef_ref, exponent_ref, polynomial_ref, tile):
    per_tile = TILE // LANES
    parts = [
        coef_ref[pl.ds((tile * per_tile + part) * COEF, COEF), :]
        for part in range(per_tile)
    ]
    coefficients = jnp.concatenate(parts, axis=1)
    cubic = expand_polynomial(coefficients[:BASIS])
    spread = expand_exponent(coefficients[BASIS:])
    rows = g_refs[0].shape[0]

    def values_of(some):
        polynomial = dot(polynomial_ref[some, :], cubic)
        exponent = dot(exponent_ref[some, :], spread)
        refs = g_refs[some.start // rows : (some.start + some.size) // rows]
        g = jnp.concatenate([ref[:, here] for ref in refs], axis=0)
        return g * coefficients[DAMP : DAMP + 1] + jnp.exp2(exponent) * polynomial

    return values_of


def update_kernel(*refs):
    g_refs = refs[:PARTS]
    coef_ref, exponent_ref, polynomial_ref, table_ref, f_ref, moments_ref = refs[PARTS:]
    cells = f_ref.shape[1]

    def front(tile):
        here = pl.ds(tile * TILE, TILE)
        values_of = relaxed(g_refs, here, coef_ref, exponent_ref, polynomial_ref, tile)
        return store_tile(f_ref, here, f_ref.shape[0], values_of)

    def back(tile, split):
        store_moments(moments_ref, table_ref[...], split, tile, cells // LANES)

    in_turn(front, back, cells // TILE)


def update_call(g, coefficients, tables, table):
    rows, cells = g[0].shape
    return pl.pallas_call(
        update_kernel,
        out_shape=(
            pltpu.VMEM((rows * PARTS, cells), jnp.float32),
            pltpu.VMEM((SENT * cells // LANES, LANES), jnp.float32),
        ),
        in_specs=[WHOLE] * (PARTS + 4),
        out_specs=(WHOLE, WHOLE),
        compiler_params=params(8),
        name="update",
    )(*map(near, g), near(coefficients), *map(near, tables), near(table))


def finish_kernel(*refs):
    g_refs = refs[:PARTS]
    coef_ref, macro_ref, exponent_ref, polynomial_ref, f_hbm, fields_hbm = refs[PARTS : PARTS + 6]
    held, fields, sems = refs[PARTS + 6 :]
    cells = held.shape[1]
    width = cells // DEPARTURES
    for block in range(cells // LANES):
        fields[:, block * LANES : (block + 1) * LANES] = macro_ref[block * 8 : (block + 1) * 8, :]
    copies = [pltpu.make_async_copy(fields, fields_hbm, sems.at[DEPARTURES])]
    copies[0].start()
    for chunk in range(DEPARTURES):
        for local in range(width // TILE):
            tile = chunk * (width // TILE) + local
            here = pl.ds(tile * TILE, TILE)
            values_of = relaxed(g_refs, here, coef_ref, exponent_ref, polynomial_ref, tile)
            for first in range(0, held.shape[0], ROWS):
                held[pl.ds(first, ROWS), here] = values_of(pl.ds(first, ROWS))
        there = pl.ds(chunk * width, width)
        copy = pltpu.make_async_copy(held.at[:, there], f_hbm.at[:, there], sems.at[chunk])
        copy.start()
        copies.append(copy)
    for copy in copies:
        copy.wait()


def finish_call(g, coefficients, macro, tables):
    rows, cells = g[0].shape
    return pl.pallas_call(
        finish_kernel,
        out_shape=(
            jax.ShapeDtypeStruct((rows * PARTS, cells), jnp.float32),
            jax.ShapeDtypeStruct((8, cells), jnp.float32),
        ),
        in_specs=[WHOLE] * (PARTS + 4),
        out_specs=(OUTSIDE, OUTSIDE),
        scratch_shapes=[
            pltpu.VMEM((rows * PARTS, cells), jnp.float32),
            pltpu.VMEM((8, cells), jnp.float32),
            pltpu.SemaphoreType.DMA((DEPARTURES + 1,)),
        ],
        compiler_params=params(16),
        name="finish",
    )(*map(near, g), near(coefficients), near(macro), *map(near, tables))


def add_kernel(left_ref, right_ref, out_ref):
    out_ref[...] = left_ref[...] + right_ref[...]


def add_call(left, right):
    return pl.pallas_call(
        add_kernel,
        out_shape=pltpu.VMEM(left.shape, left.dtype),
        in_specs=[WHOLE, WHOLE],
        out_specs=WHOLE,
        compiler_params=params(1),
        name="add",
    )(near(left), near(right))


def plan(count):
    strides = [1 << bit for bit in range(count.bit_length() - 1)]
    return strides[:2], strides[2:]


def swap(values, count, stride):
    return lax.ppermute(values, "vel", [(device, device ^ stride) for device in range(count)])


def staged_sum(values, count, sides, f, tasks):
    splits, sums = plan(count)
    results, waiting, portions = [], list(tasks), list(BESIDE)

    def exchange(chunks, stride):
        got = [swap(chunk, count, stride) for chunk in chunks]
        portion = portions.pop(0) if portions else 0
        if portion:
            _, held = lax.optimization_barrier((chunks[-1], f))
            made = [task(held) for task in waiting[:portion]]
            del waiting[:portion]
            got[0], made = lax.optimization_barrier((got[0], made))
            results.extend(made)
        return got

    def split(chunks, stride, lower_side):
        kept, sent = [], []
        for chunk in chunks:
            half = chunk.shape[0] // 2
            first, second = chunk[:half], chunk[half:]
            kept.append(jnp.where(lower_side, first, second))
            sent.append(jnp.where(lower_side, second, first))
        sent = lax.optimization_barrier(sent)
        got = exchange(sent, stride)
        if len(chunks) == 1:
            return [kept[0] + got[0]]
        return [add_call(own, other) for own, other in zip(kept, got)]

    def join(chunks, stride, lower_side):
        out = []
        for own, got in zip(chunks, exchange(chunks, stride)):
            lower = jnp.where(lower_side, own, got)
            upper = jnp.where(lower_side, got, own)
            out.append((lower, upper))
        return out

    (block,) = split([values], splits[0], sides[0])
    half = block.shape[0] // 2
    chunks = [block[:half], block[half:]]
    for stride, lower_side in zip(splits[1:], sides[1:]):
        chunks = split(chunks, stride, lower_side)
    for stride in sums:
        chunks = [add_call(own, got) for own, got in zip(chunks, exchange(chunks, stride))]
    for stride, lower_side in reversed(list(zip(splits[1:], sides[1:]))):
        chunks = [jnp.concatenate(both, axis=0) for both in join(chunks, stride, lower_side)]
    lowers, uppers = zip(*join(chunks, splits[0], sides[0]))
    results.extend(task(f) for task in waiting)
    return jnp.concatenate(lowers + uppers, axis=0), results


def on_device(velocities, density, flow, thermal, deviation):
    count = lax.axis_size("vel")
    place = lax.axis_index("vel")
    sides = [place & stride == 0 for stride in plan(count)[0]]
    velocities, sides = lax.optimization_barrier((velocities, sides))
    f, moments, *tables, table, stream = start_call(
        velocities, density, flow, thermal, deviation, velocities.shape[1] * count
    )
    for iteration in range(ITERS):
        tasks = [
            functools.partial(lambda held, part: transport_call(stream, held, part), part=part)
            for part in range(PARTS)
        ]
        summed, g = staged_sum(moments, count, sides, f, tasks)
        last = iteration == ITERS - 1
        coefficients, *macro = fluid_call(summed, last)
        if not last:
            f, moments = update_call(g, coefficients, tables, table)
    return finish_call(g, coefficients, macro[0], tables)


def solution(mesh):
    return jax.shard_map(
        on_device,
        mesh=mesh,
        in_specs=(P(None, "vel"), P("grp"), P(None, "grp"), P("grp"), P("vel", "grp")),
        out_specs=(P("vel", "grp"), P(None, "grp")),
        check_vma=False,
    )
```
